32 devices in a mesh: seq: 16 (over z, y, core), batch: 2 (over x).
Axes of the slice: x: 2, y: 2, z: 4, core: 2. Of those that a mesh axis runs over, the one named last changes fastest.
Arguments:
- tokens: bfloat16 [2, 2, 4096, 768], P(None, 'batch', 'seq'), may hold values from -6 to 6
- cotangent: bfloat16 [2, 2, 4096, 768], P(None, 'batch', 'seq'), may hold values from -6 to 6
- masked: int32 [2, 2, 4096], P(None, 'batch', 'seq'), may hold values from 0 to 1, as said below
- query_weight: bfloat16 [2, 768, 768], P(None, ('seq', 'batch')), may hold values from -0.21875 to 0.21875
- key_weight: bfloat16 [2, 768, 768], P(None, ('seq', 'batch')), may hold values from -0.21875 to 0.21875
- value_weight: bfloat16 [2, 768, 768], P(None, ('seq', 'batch')), may hold values from -0.21875 to 0.21875
- output_weight: bfloat16 [2, 768, 768], P(None, ('seq', 'batch')), may hold values from -0.875 to 0.875
- up_weight: bfloat16 [2, 768, 3072], P(None, ('seq', 'batch')), may hold values from -0.21875 to 0.21875
- down_weight: bfloat16 [2, 3072, 768], P(None, ('seq', 'batch')), may hold values from -0.109375 to 0.109375
- query_bias: bfloat16 [2, 768], P(None, ('seq', 'batch')), may hold values from -3 to 3
- value_bias: bfloat16 [2, 768], P(None, ('seq', 'batch')), may hold values from -3 to 3
- output_bias: bfloat16 [2, 768], P(None, ('seq', 'batch')), may hold values from -3 to 3
- up_bias: bfloat16 [2, 3072], P(None, ('seq', 'batch')), may hold values from -3 to 3
- down_bias: bfloat16 [2, 768], P(None, ('seq', 'batch')), may hold values from -3 to 3
- mixer_gain: bfloat16 [2, 768], P(None, ('seq', 'batch')), may hold values from 0.099609375 to 1.8984375
- mixer_shift: bfloat16 [2, 768], P(None, ('seq', 'batch')), may hold values from -3 to 3
- feed_gain: bfloat16 [2, 768], P(None, ('seq', 'batch')), may hold values from 0.099609375 to 1.8984375
- feed_shift: bfloat16 [2, 768], P(None, ('seq', 'batch')), may hold values from -3 to 3
- pool_key: bfloat16 [2, 5, 768], P(None, None, ('seq', 'batch')), may hold values from -3 to 3
- pool_value: bfloat16 [2, 5, 768], P(None, None, ('seq', 'batch')), may hold values from -3 to 3
Outputs:
- layer_output: bfloat16 [2, 2, 4096, 768], P(None, 'batch', 'seq')
- input_grad: bfloat16 [2, 2, 4096, 768], P(None, 'batch', 'seq')
- grad_query_weight: float32 [2, 768, 768], P(None, ('seq', 'batch'))
- grad_key_weight: float32 [2, 768, 768], P(None, ('seq', 'batch'))
- grad_value_weight: float32 [2, 768, 768], P(None, ('seq', 'batch'))
- grad_output_weight: float32 [2, 768, 768], P(None, ('seq', 'batch'))
- grad_up_weight: float32 [2, 768, 3072], P(None, ('seq', 'batch'))
- grad_down_weight: float32 [2, 3072, 768], P(None, ('seq', 'batch'))
- grad_query_bias: float32 [2, 768], P(None, ('seq', 'batch'))
- grad_value_bias: float32 [2, 768], P(None, ('seq', 'batch'))
- grad_output_bias: float32 [2, 768], P(None, ('seq', 'batch'))
- grad_up_bias: float32 [2, 3072], P(None, ('seq', 'batch'))
- grad_down_bias: float32 [2, 768], P(None, ('seq', 'batch'))
- grad_mixer_gain: float32 [2, 768], P(None, ('seq', 'batch'))
- grad_mixer_shift: float32 [2, 768], P(None, ('seq', 'batch'))
- grad_feed_gain: float32 [2, 768], P(None, ('seq', 'batch'))
- grad_feed_shift: float32 [2, 768], P(None, ('seq', 'batch'))
- grad_pool_key: float32 [2, 5, 768], P(None, None, ('seq', 'batch'))
- grad_pool_value: float32 [2, 5, 768], P(None, None, ('seq', 'batch'))
The draws below stay inside these ranges and needn't reach their ends.
Inputs may be any that keep to these rules, and one draw needn't show every extreme that they name: `masked`: 1 marks a token whose output gradient is taken, 0 one whose is not; in each aligned block of 64 tokens of a sequence the chance of a 1 is drawn between 5 and 40 percent.
All inputs are finite; a program needn't handle non-finite values.
Results may differ from the reference program's by a relative error of at most 0.033.
Values may be sent and summed in bfloat16 or wider, within the bound.
No kernel may reach another device: no remote copies, remote signals or barrier semaphores. Data moves between devices by JAX's collectives and lax.ppermute only.
A program may use at most 256 MiB of HBM per device.

```python
import jax
import jax.numpy as jnp
from jax import lax

D = 768
HEADS = 12
FF = 3072
LAYERS = 2
MICRO = 2
LEN = 4096
WIN = 64
PWIN = 256
SEQS = 2


def draw_masked(key, part):
    folded = jax.random.fold_in(key, 17)
    rate_key, roll_key = jax.random.split(folded)
    block_count = LEN // 64
    block_rates = jax.random.randint(rate_key, (MICRO, SEQS, block_count, 1), 5, 41)
    token_rolls = jax.random.randint(roll_key, (MICRO, SEQS, block_count, 64), 0, 100)
    return jnp.where(token_rolls < block_rates, 1, 0).astype(jnp.int32).reshape(MICRO, SEQS, LEN)


def shard_levels(own_key, shape, cuts, smallest, largest):
    level, own = 1.0, jax.random.fold_in(own_key, 6)
    for position, blocks in cuts:
        draws = jnp.exp(jax.random.uniform(jax.random.fold_in(own, position), (blocks,), jnp.float32, smallest / len(cuts), largest / len(cuts)))
        level = level * jnp.repeat(draws, shape[position] // blocks).reshape([-1 if axis == position else 1 for axis in range(len(shape))])
    return level


def bell_draw(key, shape, scale, limit, shards=(), kind=jnp.bfloat16):
    entries = scale * jax.random.normal(key, shape, jnp.float32)
    if shards:
        entries = entries * shard_levels(key, shape, shards, -0.22, 0.18)
    return jnp.clip(entries, -limit, limit).astype(kind)


def setup_inputs(seed: int = 0) -> dict:
    arg_keys = jax.random.split(jax.random.key(seed), 21)
    tokens = bell_draw(arg_keys[0], (MICRO, SEQS, LEN, D), 1.0, 6.0, ((1, 2), (2, 16)))
    cotangent = bell_draw(arg_keys[1], (MICRO, SEQS, LEN, D), 1.0, 6.0, ((1, 2), (2, 16)))
    masked = draw_masked(jax.random.fold_in(arg_keys[20], 71), 0)
    query_weight = bell_draw(arg_keys[3], (LAYERS, D, D), D ** -0.5, 0.21875, ((1, 32),))
    key_weight = bell_draw(arg_keys[4], (LAYERS, D, D), D ** -0.5, 0.21875, ((1, 32),))
    value_weight = bell_draw(arg_keys[5], (LAYERS, D, D), D ** -0.5, 0.21875, ((1, 32),))
    output_weight = bell_draw(arg_keys[6], (LAYERS, D, D), (D // 16) ** -0.5, 0.875, ((1, 32),))
    up_weight = bell_draw(arg_keys[7], (LAYERS, D, FF), D ** -0.5, 0.21875, ((1, 32),))
    down_weight = bell_draw(arg_keys[8], (LAYERS, FF, D), FF ** -0.5, 0.109375, ((1, 32),))
    query_bias = bell_draw(arg_keys[9], (LAYERS, D), 0.5, 3.0, ((1, 32),))
    value_bias = bell_draw(arg_keys[10], (LAYERS, D), 0.5, 3.0, ((1, 32),))
    output_bias = bell_draw(arg_keys[11], (LAYERS, D), 0.5, 3.0, ((1, 32),))
    up_bias = bell_draw(arg_keys[12], (LAYERS, FF), 0.5, 3.0, ((1, 32),))
    down_bias = bell_draw(arg_keys[13], (LAYERS, D), 0.5, 3.0, ((1, 32),))
    mixer_gain = jnp.clip(1.0 + 0.18 * jax.random.normal(arg_keys[14], (LAYERS, D), jnp.float32), 0.099609375, 1.8984375).astype(jnp.bfloat16)
    mixer_shift = bell_draw(arg_keys[15], (LAYERS, D), 0.5, 3.0, ((1, 32),))
    feed_gain = jnp.clip(1.0 + 0.18 * jax.random.normal(arg_keys[16], (LAYERS, D), jnp.float32), 0.099609375, 1.8984375).astype(jnp.bfloat16)
    feed_shift = bell_draw(arg_keys[17], (LAYERS, D), 0.5, 3.0, ((1, 32),))
    pool_key = bell_draw(arg_keys[18], (LAYERS, 5, D), 0.45, 3.0, ((2, 32),))
    pool_value = bell_draw(arg_keys[19], (LAYERS, 5, D), 0.45, 3.0, ((2, 32),))
    return {"tokens": tokens, "cotangent": cotangent, "masked": masked, "query_weight": query_weight, "key_weight": key_weight, "value_weight": value_weight, "output_weight": output_weight, "up_weight": up_weight, "down_weight": down_weight, "query_bias": query_bias, "value_bias": value_bias, "output_bias": output_bias, "up_bias": up_bias, "down_bias": down_bias, "mixer_gain": mixer_gain, "mixer_shift": mixer_shift, "feed_gain": feed_gain, "feed_shift": feed_shift, "pool_key": pool_key, "pool_value": pool_value}


highest = lax.Precision.HIGHEST
norm_eps = 1e-05
gelu_coef = 0.7978845608028654
masked_score = -1e+30

@jax.custom_vjp
def low(v):
    return lax.optimization_barrier(v.astype(jnp.bfloat16)).astype(jnp.float32)

@jax.custom_vjp
def low_back(v):
    return v

def low_keep(v):
    return (low(v), None)

def low_pass(kept, grad):
    return (grad,)

def back_keep(v):
    return (v, None)

def back_low(kept, grad):
    return (low(grad),)
low.defvjp(low_keep, low_pass)
low_back.defvjp(back_keep, back_low)

def layer_norm(inputs, gain_vec, shift_vec):
    centre = inputs - lax.optimization_barrier(jnp.mean(inputs, axis=-1, keepdims=True))
    spread = lax.optimization_barrier(jnp.mean(centre * centre, axis=-1, keepdims=True))
    return centre * lax.rsqrt(spread + norm_eps) * gain_vec + shift_vec

def gelu_tanh(inputs):
    return 0.5 * inputs * (1.0 + jnp.tanh(gelu_coef * (inputs + 0.044715 * inputs * inputs * inputs)))

def project(left_side, right_side):
    return jnp.dot(left_side, right_side, precision=highest, preferred_element_type=jnp.float32)

def pooling(inputs, kernel):
    seq_len = inputs.shape[0]
    padded = jnp.pad(inputs, ((2, 2), (0, 0)))
    total = jnp.zeros((seq_len // 4, inputs.shape[1]), jnp.float32)
    for offset in range(5):
        total = total + kernel[offset] * padded[offset:offset + seq_len:4]
    return total

def softmax_branch(query_block, key_block, value_block, allowed_mask, score_scale):
    scores = jnp.einsum('qhd,khd->hqk', query_block, key_block, precision=highest) * score_scale
    scores = jnp.where(allowed_mask[None], low_back(scores), masked_score)
    row_max = lax.optimization_barrier(jnp.max(scores, axis=-1, keepdims=True))
    weights = jnp.exp(scores - row_max)
    probability = weights / lax.optimization_barrier(jnp.sum(weights, axis=-1, keepdims=True))
    return jnp.einsum('hqk,khd->qhd', low(probability), value_block, precision=highest)

def attend(query, key_rows, value_rows, pooled_key, pooled_value):
    seq_len, width = query.shape
    head_dim = width // HEADS
    score_scale = head_dim ** (-0.5)
    block_len = min(512, seq_len)
    pooled_len = block_len // 4
    reach = PWIN // 4
    key_pad = jnp.pad(key_rows, ((WIN, WIN), (0, 0)))
    value_pad = jnp.pad(value_rows, ((WIN, WIN), (0, 0)))
    pkey_pad = jnp.pad(pooled_key, ((reach, reach), (0, 0)))
    pvalue_pad = jnp.pad(pooled_value, ((reach, reach), (0, 0)))

    def one_block(block_index):
        first_row = block_index * block_len
        first_pool = block_index * pooled_len
        query_block = lax.dynamic_slice_in_dim(query, first_row, block_len, 0).reshape(block_len, HEADS, head_dim)
        near_keys = lax.dynamic_slice_in_dim(key_pad, first_row, block_len + 2 * WIN, 0).reshape(-1, HEADS, head_dim)
        near_values = lax.dynamic_slice_in_dim(value_pad, first_row, block_len + 2 * WIN, 0).reshape(-1, HEADS, head_dim)
        far_keys = lax.dynamic_slice_in_dim(pkey_pad, first_pool, pooled_len + 2 * reach, 0).reshape(-1, HEADS, head_dim)
        far_values = lax.dynamic_slice_in_dim(pvalue_pad, first_pool, pooled_len + 2 * reach, 0).reshape(-1, HEADS, head_dim)
        positions = first_row + jnp.arange(block_len, dtype=jnp.int32)
        near_pos = first_row - WIN + jnp.arange(block_len + 2 * WIN, dtype=jnp.int32)
        far_pos = first_pool - reach + jnp.arange(pooled_len + 2 * reach, dtype=jnp.int32)
        near_mask = (jnp.abs(positions[:, None] - near_pos[None, :]) <= WIN) & (near_pos[None, :] >= 0) & (near_pos[None, :] < seq_len)
        far_mask = (jnp.abs(positions[:, None] - 4 * far_pos[None, :]) <= PWIN) & (far_pos[None, :] >= 0) & (far_pos[None, :] < seq_len // 4)
        mixed = softmax_branch(query_block, near_keys, near_values, near_mask, score_scale)
        mixed = mixed + softmax_branch(query_block, far_keys, far_values, far_mask, score_scale)
        return mixed.reshape(block_len, width)
    blocks = lax.map(jax.checkpoint(one_block), jnp.arange(seq_len // block_len, dtype=jnp.int32))
    return blocks.reshape(seq_len, width)

def one_layer(inputs, params):
    query_weight, key_weight, value_weight, output_weight, up_weight, down_weight, query_bias, value_bias, output_bias, up_bias, down_bias, mixer_gain, mixer_shift, feed_gain, feed_shift, pool_key, pool_value = params
    inputs_low = low(inputs)
    query = low(low_back(project(inputs_low, query_weight) + query_bias))
    key_rows = low(low_back(project(inputs_low, key_weight)))
    value_rows = low(low_back(project(inputs_low, value_weight) + value_bias))
    pooled_key = low(low_back(pooling(key_rows, pool_key)))
    pooled_value = low(low_back(pooling(value_rows, pool_value)))
    mixed = low(low_back(attend(query, key_rows, value_rows, pooled_key, pooled_value)))
    attention = low_back(project(mixed, output_weight) + output_bias)
    hidden = layer_norm(inputs + attention, mixer_gain, mixer_shift)
    pre_act = low_back(project(low(hidden), up_weight) + up_bias)
    act_low = low(gelu_tanh(pre_act))
    feed_out = low_back(project(act_low, down_weight) + down_bias)
    return layer_norm(hidden + feed_out, feed_gain, feed_shift)

def reference(tokens, cotangent, masked, query_weight, key_weight, value_weight, output_weight, up_weight, down_weight, query_bias, value_bias, output_bias, up_bias, down_bias, mixer_gain, mixer_shift, feed_gain, feed_shift, pool_key, pool_value):
    params = tuple((weight.astype(jnp.float32) for weight in (query_weight, key_weight, value_weight, output_weight, up_weight, down_weight, query_bias, value_bias, output_bias, up_bias, down_bias, mixer_gain, mixer_shift, feed_gain, feed_shift, pool_key, pool_value)))
    seq_count = tokens.shape[0] * tokens.shape[1]
    inputs = tokens.astype(jnp.float32).reshape(seq_count, LEN, D)
    grad_out = (cotangent.astype(jnp.float32) * masked.astype(jnp.float32)[..., None]).reshape(seq_count, LEN, D)

    def forward(weights, batch_rows):

        def one_sequence(seq_rows):
            for layer_index in range(LAYERS):
                seq_rows = one_layer(seq_rows, tuple((weight[layer_index] for weight in weights)))
            return seq_rows
        return lax.map(jax.checkpoint(one_sequence), batch_rows)
    outputs, pullback = jax.vjp(forward, params, inputs)
    grads, grad_inputs = pullback(grad_out)
    return (outputs.reshape(tokens.shape).astype(jnp.bfloat16), grad_inputs.reshape(tokens.shape).astype(jnp.bfloat16), grads[0], grads[1], grads[2], grads[3], grads[4], grads[5], grads[6], grads[7], grads[8], grads[9], grads[10], grads[11], grads[12], grads[13], grads[14], grads[15], grads[16])
```

```python
import functools

import jax
import jax.numpy as jnp
from jax import lax
from jax.experimental import pallas as pl
from jax.experimental.pallas import tpu as pltpu
from jax.sharding import PartitionSpec as P

HEADS = 12
WIN = 64
PWIN = 256
TAPS = 5
REACH = PWIN // 4
QROWS = 128
norm_eps = 1e-05
gelu_coef = 0.7978845608028654
masked_score = -1e30
f32 = jnp.float32
bf16 = jnp.bfloat16
VMEM_LIMIT = 48 * 1024 * 1024


def axis_bits():
    bits = []
    for axis in ("seq", "batch"):
        step = lax.axis_size(axis) // 2
        while step:
            bits.append((axis, step))
            step //= 2
    return bits


def path(name):
    bits = axis_bits()
    core, row = ("seq", 1), ("seq", 2)
    column = [bit for bit in bits if bit[0] == "seq" and bit[1] > 2]
    across = [bit for bit in bits if bit[0] == "batch"]
    order = {
        "y": column + across + [row],
        "x": column + [row] + across,
        "z": across + [row] + column,
        "w": [row] + column + across,
    }[name]
    return order + [core]


def exchange(value, axis, step):
    pairs = [(i, i ^ step) for i in range(lax.axis_size(axis))]
    return lax.ppermute(value, axis, pairs)


def block_order():
    bits = axis_bits()
    return [("seq", 1), ("seq", 2)] + [b for b in bits if b[0] == "batch"] + [
        b for b in bits if b[0] == "seq" and b[1] > 2
    ]


def flat_index():
    return lax.axis_index("seq") * lax.axis_size("batch") + lax.axis_index("batch")


def relative_blocks():
    spread = []
    for axis, step in block_order():
        spread.append(step * lax.axis_size("batch") if axis == "seq" else step)
    count = len(spread)
    return [
        sum(spread[k] for k in range(count) if place >> (count - 1 - k) & 1)
        for place in range(2**count)
    ]


def tied(values):
    return list(lax.optimization_barrier(tuple(values)))


class Gather:
    def __init__(self, shard, order):
        self.current, self.order = shard, order
        self.have, self.halves, self.flying = [], None, None
        self.parts, self.rows, self.cols = shard.shape

    def ready(self):
        return self.current

    def hold(self, value):
        self.current = value

    def launch(self):
        self.flying = exchange(self.current, *self.order[len(self.have)])

    def land(self):
        stage = self.order[len(self.have)]
        if stage == self.order[-1]:
            self.halves = (self.current, self.flying)
            return
        significance = block_order()
        place = significance.index(stage)
        before = sum(1 for p in self.have if p < place)
        split = (self.parts * 2**before, 1, 2 ** (len(self.have) - before) * self.rows, self.cols)
        self.have.append(place)
        joined = jnp.concatenate([self.current.reshape(split), self.flying.reshape(split)], axis=1)
        self.current = joined.reshape(self.parts, 2 ** len(self.have) * self.rows, self.cols)

    @property
    def left(self):
        return 0 if self.halves is not None else len(self.order) - len(self.have)

    @property
    def done(self):
        return self.halves is not None


class Scatter:
    def __init__(self, halves, order):
        self.keep, self.give = halves
        self.order, self.stage, self.total, self.flying = order, 0, None, None
        self.have = list(range(1, len(order)))
        self.parts, half_rows, self.cols = self.keep.shape
        self.rows = half_rows // 2 ** len(self.have)

    def ready(self):
        return self.give

    def hold(self, value):
        self.give = value

    def launch(self):
        self.flying = exchange(self.give, *self.order[self.stage])

    def land(self):
        total = self.keep.astype(f32) + self.flying.astype(f32)
        self.stage += 1
        if self.stage == len(self.order):
            self.total = total.reshape(self.parts, self.rows, self.cols)
            return
        place = self.have.index(block_order().index(self.order[self.stage]))
        self.have.pop(place)
        left = 2 ** len(self.have) * self.rows
        split = total.astype(bf16).reshape(self.parts * 2**place, 2, left >> place, self.cols)
        self.keep, self.give = [split[:, i].reshape(self.parts, left, self.cols) for i in range(2)]

    @property
    def done(self):
        return self.total is not None


def checkpoint(value, flows, begin=()):
    value, *flying = tied([value] + [flow.flying for flow in flows])
    for flow, arrived in zip(flows, flying):
        flow.flying = arrived
        flow.land()
    going = [flow for flow in flows if not flow.done] + list(begin)
    value, *ready = tied([value] + [flow.ready() for flow in going])
    for flow, part in zip(going, ready):
        flow.hold(part)
        flow.launch()
    return value


def passed_along(value, steps):
    count = lax.axis_size("seq")
    pairs = [(i, i + steps) for i in range(count) if 0 <= i + steps < count]
    return lax.ppermute(value, "seq", pairs)


def pooled_hops(size):
    return -(-REACH // size)


def pooled_rims(pooled):
    size = pooled.shape[1]
    hops = range(1, pooled_hops(size) + 1)
    low = [passed_along(pooled, hop) for hop in reversed(hops)]
    up = [passed_along(pooled, -hop) for hop in hops]
    low = low[0] if len(low) == 1 else jnp.concatenate(low, axis=1)
    up = up[0] if len(up) == 1 else jnp.concatenate(up, axis=1)
    return low[:, low.shape[1] - REACH :], up[:, :REACH]


def rims_return(rim_low, rim_up, pooled_own):
    size = pooled_own.shape[2]
    hops = pooled_hops(size)
    far_low, far_up = rim_low[:, :, WIN:], rim_up[:, :, WIN:]
    for hop in range(2, hops + 1):
        start = REACH - hop * size
        pooled_own = pooled_own + passed_along(far_low[:, :, start : start + size], -hop).astype(f32)
        start = (hop - 1) * size
        pooled_own = pooled_own + passed_along(far_up[:, :, start : start + size], hop).astype(f32)
    if hops > 1:
        near_low, near_up = rim_low[:, :, :WIN], rim_up[:, :, :WIN]
        rim_low = jnp.concatenate([near_low, far_low[:, :, REACH - size :]], axis=2)
        rim_up = jnp.concatenate([near_up, far_up[:, :, :size]], axis=2)
    return passed_along(rim_up, 1), passed_along(rim_low, -1), pooled_own


def dot_nt(a, b):
    return lax.dot_general(a, b, (((1,), (1,)), ((), ())), preferred_element_type=f32)


def dot_nn(a, b):
    return lax.dot_general(a, b, (((1,), (0,)), ((), ())), preferred_element_type=f32)


def flipped(block):
    return jnp.transpose(block.astype(f32)).astype(bf16)


def two_heads(rows):
    lane = lax.broadcasted_iota(jnp.int32, rows.shape, 1)
    none = jnp.zeros_like(rows)
    half = rows.shape[1] // 2
    return jnp.concatenate(
        [jnp.where(lane < half, rows, none), jnp.where(lane < half, none, rows)], axis=0
    )


def heads_apart(block):
    half, queries = block.shape[0] // 2, block.shape[1] // 2
    return jnp.transpose(
        jnp.concatenate([block[:half, :queries], block[half:, queries:]], axis=0)
    )


def attend_kernel(near_ref, far_ref, q_ref, k_ref, v_ref, kl_ref, vl_ref, ku_ref, vu_ref,
                  pk_ref, pv_ref, pkl_ref, pvl_ref, pku_ref, pvu_ref, mixed_ref, stat_ref):
    blocks = q_ref.shape[1] // QROWS
    pairs = q_ref.shape[2] // 128
    for pair in range(pairs):
        at = slice(128 * pair, 128 * pair + 128)
        keys = jnp.concatenate([kl_ref[0, :, at], k_ref[0, :, at], ku_ref[0, :, at]], axis=0)
        values = jnp.concatenate([vl_ref[0, :, at], v_ref[0, :, at], vu_ref[0, :, at]], axis=0)
        far_keys = jnp.concatenate([pkl_ref[0, :, at], pk_ref[0, :, at], pku_ref[0, :, at]], axis=0)
        far_values = jnp.concatenate(
            [pvl_ref[0, :, at], pv_ref[0, :, at], pvu_ref[0, :, at]], axis=0
        )
        values_t, far_values_t = flipped(values), flipped(far_values)
        for block in range(blocks):
            first = QROWS * block
            query = two_heads(q_ref[0, first : first + QROWS, at] * 0.125)
            stop = first + QROWS + 2 * WIN
            score = dot_nt(keys[first:stop], query) + near_ref[block]
            top = jnp.max(score, axis=0, keepdims=True)
            prob = jnp.exp(score - top)
            total = jnp.sum(prob, axis=0, keepdims=True)
            near_low = (prob * (1.0 / total)).astype(bf16)
            row = (pair * blocks + block) * 2
            stat_ref[0, 0, row : row + 1, :] = top + jnp.log(total)
            score = dot_nt(far_keys, query) + far_ref[block]
            top = jnp.max(score, axis=0, keepdims=True)
            prob = jnp.exp(score - top)
            total = jnp.sum(prob, axis=0, keepdims=True)
            far_low = (prob * (1.0 / total)).astype(bf16)
            stat_ref[0, 0, row + 1 : row + 2, :] = top + jnp.log(total)
            mixed = dot_nn(values_t[:, first:stop], near_low) + dot_nn(far_values_t, far_low)
            mixed_ref[0, first : first + QROWS, at] = heads_apart(mixed).astype(bf16)


def attend_back_kernel(near_ref, far_ref, stat_ref, g_ref, q_ref, k_ref, v_ref, kl_ref, vl_ref,
                       ku_ref, vu_ref, pk_ref, pv_ref, pkl_ref, pvl_ref, pku_ref, pvu_ref,
                       dq_ref, own_ref, pool_ref, low_ref, up_ref):
    blocks = q_ref.shape[1] // QROWS
    pairs = q_ref.shape[2] // 128
    length = q_ref.shape[1]
    for pair in range(pairs):
        at = slice(128 * pair, 128 * pair + 128)
        keys = jnp.concatenate([kl_ref[0, :, at], k_ref[0, :, at], ku_ref[0, :, at]], axis=0)
        values = jnp.concatenate([vl_ref[0, :, at], v_ref[0, :, at], vu_ref[0, :, at]], axis=0)
        far_keys = jnp.concatenate([pkl_ref[0, :, at], pk_ref[0, :, at], pku_ref[0, :, at]], axis=0)
        far_values = jnp.concatenate(
            [pvl_ref[0, :, at], pv_ref[0, :, at], pvu_ref[0, :, at]], axis=0
        )
        keys_t, far_keys_t = flipped(keys), flipped(far_keys)
        near_parts = ([], [])
        far_totals = [None, None]
        for block in range(blocks):
            first = QROWS * block
            query = two_heads(q_ref[0, first : first + QROWS, at] * 0.125)
            grads = two_heads(g_ref[0, first : first + QROWS, at])
            stop = first + QROWS + 2 * WIN
            row = (pair * blocks + block) * 2
            prob = jnp.exp(
                dot_nt(keys[first:stop], query) + near_ref[block] - stat_ref[0, 0, row : row + 1, :]
            )
            grad_prob = dot_nt(values[first:stop], grads)
            inner = jnp.sum(prob * grad_prob, axis=0, keepdims=True)
            grad_score = (prob * (grad_prob - inner)).astype(bf16)
            near_parts[0].append(dot_nn(grad_score, query))
            near_parts[1].append(dot_nn(prob.astype(bf16), grads))
            grad_query = dot_nn(keys_t[:, first:stop], grad_score)
            prob = jnp.exp(
                dot_nt(far_keys, query) + far_ref[block] - stat_ref[0, 0, row + 1 : row + 2, :]
            )
            grad_prob = dot_nt(far_values, grads)
            inner = jnp.sum(prob * grad_prob, axis=0, keepdims=True)
            grad_score = (prob * (grad_prob - inner)).astype(bf16)
            parts = (dot_nn(grad_score, query), dot_nn(prob.astype(bf16), grads))
            grad_query = grad_query + dot_nn(far_keys_t, grad_score)
            dq_ref[0, first : first + QROWS, at] = (heads_apart(grad_query) * 0.125).astype(bf16)
            for kind in range(2):
                far_totals[kind] = parts[kind] if block == 0 else far_totals[kind] + parts[kind]
        for kind in range(2):
            rows = []
            for chunk in range(blocks + 1):
                terms = []
                if chunk < blocks:
                    terms.append(near_parts[kind][chunk][:QROWS])
                if chunk > 0:
                    terms.append(near_parts[kind][chunk - 1][QROWS:])
                rows.append(functools.reduce(jnp.add, terms))
            rows = jnp.concatenate(rows, axis=0)
            own_ref[kind, 0, :, at] = rows[WIN : WIN + length]
            low_ref[kind, 0, :WIN, at] = rows[:WIN].astype(bf16)
            up_ref[kind, 0, :WIN, at] = rows[WIN + length :].astype(bf16)
            far = far_totals[kind]
            pool_ref[kind, 0, :, at] = far[REACH : far.shape[0] - REACH]
            low_ref[kind, 0, WIN:, at] = far[:REACH].astype(bf16)
            up_ref[kind, 0, WIN:, at] = far[far.shape[0] - REACH :].astype(bf16)


LANES = 256


def attend_specs(length, width):
    groups = width // LANES
    pooled = length // 4

    def spec(rows, shift):
        return pl.BlockSpec((1, rows, LANES), lambda g, j: (g, 0, j + shift))

    def whole(count, rows):
        return pl.BlockSpec((count, rows, 2 * QROWS), lambda g, j: (0, 0, 0))

    blocks = length // QROWS
    masks = [whole(blocks, QROWS + 2 * WIN), whole(blocks, pooled + 2 * REACH)]
    stat_rows = LANES // 128 * blocks * 2
    stat = pl.BlockSpec((1, 1, stat_rows, 2 * QROWS), lambda g, j: (g, j, 0, 0))
    operands = [spec(length, 0), spec(length, groups), spec(length, 2 * groups)]
    operands += [spec(WIN, 0), spec(WIN, groups)] * 2
    operands += [spec(pooled, 0), spec(pooled, groups)]
    operands += [spec(REACH, 0), spec(REACH, groups)] * 2
    return groups, masks, stat, stat_rows, operands, spec


def attend_operands(qkv, rows_low, rows_up, pooled, pooled_low, pooled_up):
    return (
        qkv, qkv, qkv, rows_low, rows_low, rows_up, rows_up,
        pooled, pooled, pooled_low, pooled_low, pooled_up, pooled_up,
    )


def attend(masks, operands, width):
    qkv = operands[0]
    count, length = qkv.shape[:2]
    groups, mask_specs, stat, stat_rows, specs, spec = attend_specs(length, width)
    return pl.pallas_call(
        attend_kernel,
        grid=(count, groups),
        in_specs=mask_specs + specs,
        out_specs=[spec(length, 0), stat],
        out_shape=[
            jax.ShapeDtypeStruct((count, length, width), bf16),
            jax.ShapeDtypeStruct((count, groups, stat_rows, 2 * QROWS), f32),
        ],
        compiler_params=pltpu.CompilerParams(vmem_limit_bytes=VMEM_LIMIT),
        cost_estimate=pl.CostEstimate(
            flops=count * length * width * 2000, bytes_accessed=8000000, transcendentals=3000000
        ),
        name="attend",
    )(*masks, *operands)


def attend_back(masks, stats, grad_mixed, operands):
    count, length, width = grad_mixed.shape
    groups, mask_specs, stat, stat_rows, specs, spec = attend_specs(length, width)
    pooled = length // 4

    def pair_spec(rows):
        return pl.BlockSpec((2, 1, rows, LANES), lambda g, j: (0, g, 0, j))

    return pl.pallas_call(
        attend_back_kernel,
        grid=(count, groups),
        in_specs=mask_specs + [stat, spec(length, 0)] + specs,
        out_specs=[
            spec(length, 0), pair_spec(length), pair_spec(pooled),
            pair_spec(WIN + REACH), pair_spec(WIN + REACH),
        ],
        out_shape=[
            jax.ShapeDtypeStruct((count, length, width), bf16),
            jax.ShapeDtypeStruct((2, count, length, width), f32),
            jax.ShapeDtypeStruct((2, count, pooled, width), f32),
            jax.ShapeDtypeStruct((2, count, WIN + REACH, width), bf16),
            jax.ShapeDtypeStruct((2, count, WIN + REACH, width), bf16),
        ],
        compiler_params=pltpu.CompilerParams(vmem_limit_bytes=VMEM_LIMIT),
        cost_estimate=pl.CostEstimate(
            flops=count * length * width * 5000, bytes_accessed=12000000, transcendentals=3000000
        ),
        name="attend_back",
    )(*masks, stats, grad_mixed, *operands)


def window_masks(length):
    blocks = length // QROWS
    index, devices = lax.axis_index("seq"), lax.axis_size("seq")

    def bias(width, offset, scale, reach):
        key = lax.broadcasted_iota(jnp.int32, (blocks, width, QROWS), 1)
        query = lax.broadcasted_iota(jnp.int32, (blocks, width, QROWS), 2)
        block = lax.broadcasted_iota(jnp.int32, (blocks, width, QROWS), 0)
        key = key - offset + (block * QROWS if scale == 1 else 0)
        query = query + block * QROWS
        size = length // scale
        allowed = jnp.abs(query - scale * key) <= reach
        place = key + index * size
        allowed &= (place >= 0) & (place < size * devices)
        one = jnp.where(allowed, 0.0, masked_score).astype(f32)
        return jnp.concatenate([one, one], axis=2)

    return bias(QROWS + 2 * WIN, WIN, 1, WIN), bias(length // 4 + 2 * REACH, REACH, 4, PWIN)


def tap_select(length):
    pooled = length // 4
    row = jnp.arange(TAPS * pooled, dtype=jnp.int32)
    column = jnp.arange(length, dtype=jnp.int32)
    source = 4 * (row % pooled) + row // pooled - 2
    return (source[:, None] == column[None, :]).astype(bf16)


def pool_kernel(select_ref, kernel_ref, rows_ref, low_ref, pooled_ref):
    pooled = pooled_ref.shape[1]
    for group in range(rows_ref.shape[0]):
        taps = dot_nn(select_ref[...], rows_ref[group])
        total = kernel_ref[0, 0:1, :] * taps[:pooled]
        for tap in range(1, TAPS):
            total = total + kernel_ref[0, tap : tap + 1, :] * taps[tap * pooled : (tap + 1) * pooled]
        low = low_ref[group].astype(f32)
        edge = kernel_ref[0, 0:1, :] * low[14:15] + kernel_ref[0, 1:2, :] * low[15:16]
        row = lax.broadcasted_iota(jnp.int32, total.shape, 0)
        pooled_ref[group] = (total + jnp.where(row == 0, edge, 0.0)).astype(bf16)


def pool(select, kernel, qkv, rows_low, width):
    count, length = qkv.shape[:2]
    groups = width // LANES
    return pl.pallas_call(
        pool_kernel,
        grid=(2 * groups,),
        in_specs=[
            pl.BlockSpec(select.shape, lambda j: (0, 0)),
            pl.BlockSpec((1, 8, LANES), lambda j: (j // groups, 0, j % groups)),
            pl.BlockSpec((count, length, LANES), lambda j: (0, 0, j + groups)),
            pl.BlockSpec((count, 16, LANES), lambda j: (0, WIN // 16 - 1, j)),
        ],
        out_specs=pl.BlockSpec((count, length // 4, LANES), lambda j: (0, 0, j)),
        out_shape=jax.ShapeDtypeStruct((count, length // 4, 2 * width), bf16),
        compiler_params=pltpu.CompilerParams(vmem_limit_bytes=VMEM_LIMIT),
        cost_estimate=pl.CostEstimate(
            flops=count * length * width * 1300, bytes_accessed=2500000, transcendentals=0
        ),
        name="pool",
    )(select, kernel, qkv, rows_low)


def pool_back_kernel(select_ref, spread_ref, kernel_ref, rows_ref, low_rows_ref, own_ref, pool_ref,
                     low_ref, up_ref, grad_ref, tail_ref, taps_ref):
    pooled = pool_ref.shape[2]
    length = rows_ref.shape[1]
    tap_row = lax.broadcasted_iota(jnp.int32, (8, LANES), 0)
    tail_row = lax.broadcasted_iota(jnp.int32, (16, LANES), 0)
    taps_total = jnp.zeros((8, LANES), f32)
    for group in range(rows_ref.shape[0]):
        grads = pool_ref[0, group] + low_ref[0, group, WIN:].astype(f32)
        grads = (grads + up_ref[0, group, WIN:].astype(f32)).astype(bf16).astype(f32)
        taps = dot_nn(select_ref[...], rows_ref[group])
        low_rows = low_rows_ref[group].astype(f32)
        edge = grads[0:1]
        spread = []
        for tap in range(TAPS):
            line = jnp.sum(grads * taps[tap * pooled : (tap + 1) * pooled], axis=0, keepdims=True)
            if tap < 2:
                line = line + edge * low_rows[14 + tap : 15 + tap]
            taps_total = taps_total + jnp.where(tap_row == tap, line, 0.0)
            spread.append(grads * kernel_ref[0, tap : tap + 1, :])
        spread = jnp.concatenate(spread, axis=0)
        high = spread.astype(bf16)
        rest = (spread - high.astype(f32)).astype(bf16)
        total = own_ref[0, group] + dot_nn(spread_ref[...], high) + dot_nn(spread_ref[...], rest)
        grad_ref[0, group] = total
        grad_ref[0, group, :WIN] = total[:WIN] + low_ref[0, group, :WIN].astype(f32)
        grad_ref[0, group, length - WIN :] = total[length - WIN :] + up_ref[0, group, :WIN].astype(f32)
        tail = jnp.where(tail_row == 14, edge * kernel_ref[0, 0:1, :], 0.0)
        tail = tail + jnp.where(tail_row == 15, edge * kernel_ref[0, 1:2, :], 0.0)
        tail_ref[0, group] = tail.astype(bf16)
    taps_ref[0] = taps_total


def pool_back(select, kernel, qkv, rows_low, own, pooled_own, from_low, from_up):
    count, length, width = own.shape[1:]
    groups = width // LANES
    pooled = length // 4

    def pair_spec(rows):
        return pl.BlockSpec((1, count, rows, LANES), lambda j: (j // groups, 0, 0, j % groups))

    return pl.pallas_call(
        pool_back_kernel,
        grid=(2 * groups,),
        in_specs=[
            pl.BlockSpec(select.shape, lambda j: (0, 0)),
            pl.BlockSpec(select.shape[::-1], lambda j: (0, 0)),
            pl.BlockSpec((1, 8, LANES), lambda j: (j // groups, 0, j % groups)),
            pl.BlockSpec((count, length, LANES), lambda j: (0, 0, j + groups)),
            pl.BlockSpec((count, 16, LANES), lambda j: (0, WIN // 16 - 1, j)),
            pair_spec(length), pair_spec(pooled),
            pair_spec(from_low.shape[2]), pair_spec(from_up.shape[2]),
        ],
        out_specs=[
            pair_spec(length), pair_spec(16),
            pl.BlockSpec((1, 8, LANES), lambda j: (j // groups, 0, j % groups)),
        ],
        out_shape=[
            jax.ShapeDtypeStruct((2, count, length, width), f32),
            jax.ShapeDtypeStruct((2, count, 16, width), bf16),
            jax.ShapeDtypeStruct((2, 8, width), f32),
        ],
        compiler_params=pltpu.CompilerParams(vmem_limit_bytes=VMEM_LIMIT),
        cost_estimate=pl.CostEstimate(
            flops=count * length * width * 4000, bytes_accessed=9000000, transcendentals=0
        ),
        name="pool_back",
    )(select, select.T, kernel, qkv, rows_low, own, pooled_own, from_low, from_up)


def matmul(a, b):
    return jnp.dot(a, b, preferred_element_type=f32)


def matmul_t(a, b):
    return lax.dot_general(a, b, (((1,), (1,)), ((), ())), preferred_element_type=f32)


def weight_grad(a, b):
    return lax.dot_general(a, b, (((0,), (0,)), ((), ())), preferred_element_type=f32)


def normalised(rows):
    centre = rows - jnp.mean(rows, axis=-1, keepdims=True)
    inverse = lax.rsqrt(jnp.mean(centre * centre, axis=-1, keepdims=True) + norm_eps)
    return centre * inverse, inverse


def normalised_back(grads, gain, norm, inverse):
    scaled = grads * gain
    mean = jnp.mean(scaled, axis=-1, keepdims=True)
    inner = jnp.mean(scaled * norm, axis=-1, keepdims=True)
    return (scaled - mean - norm * inner) * inverse


def gelu_both(value):
    inside = jnp.tanh(gelu_coef * (value + 0.044715 * value * value * value))
    act = 0.5 * value * (1.0 + inside)
    slope = 0.5 * (1.0 + inside) + 0.5 * value * (1.0 - inside * inside) * gelu_coef * (
        1.0 + 3 * 0.044715 * value * value
    )
    return act, slope


def small_index():
    return flat_index().reshape(1).astype(jnp.int32)


def place_kernel(blocks, index_ref, mine_ref, other_ref, out_ref):
    half = len(blocks) // 2
    for place, bits in enumerate(blocks):
        source = mine_ref if place < half else other_ref
        out_ref[0, index_ref[0] ^ bits] = source[0, place % half]


def in_place(halves, block_cols, skip=0, take=None):
    blocks = relative_blocks()
    half = len(blocks) // 2
    all_parts, half_rows, cols = halves[0].shape
    parts = take or all_parts
    rows = half_rows // half
    spec = pl.BlockSpec((1, half, rows, block_cols), lambda p, j, index: (p + skip, 0, 0, j))
    whole = pl.pallas_call(
        functools.partial(place_kernel, blocks),
        grid_spec=pltpu.PrefetchScalarGridSpec(
            num_scalar_prefetch=1,
            grid=(parts, cols // block_cols),
            in_specs=[spec, spec],
            out_specs=pl.BlockSpec(
                (1, 2 * half, rows, block_cols), lambda p, j, index: (p, 0, 0, j)
            ),
        ),
        out_shape=jax.ShapeDtypeStruct((parts, 2 * half, rows, cols), halves[0].dtype),
        compiler_params=pltpu.CompilerParams(vmem_limit_bytes=VMEM_LIMIT),
        cost_estimate=pl.CostEstimate(
            flops=0, bytes_accessed=8 * parts * half_rows * cols, transcendentals=0
        ),
        name="in_place",
    )(small_index(), *[h.reshape(all_parts, half, rows, cols) for h in halves])
    return whole.reshape(parts * 2 * half_rows, cols)


def store_blocks(blocks, index, total_ref, keep_ref, give_ref):
    half = len(blocks) // 2
    rows = total_ref.shape[0] // len(blocks)
    for place, bits in enumerate(blocks):
        target = keep_ref if place < half else give_ref
        start = pl.multiple_of((index ^ bits) * rows, 8)
        target[0, place % half] = total_ref[pl.ds(start, rows), :].astype(bf16)


def weight_grads_kernel(blocks, plan, index_ref, *refs):
    operands, (keep_ref, give_ref, total_ref) = refs[:-3], refs[-3:]
    width = total_ref.shape[0]
    for step, (left, left_at, right, right_at) in enumerate(plan):

        @pl.when(pl.program_id(0) == step)
        def _():
            rows = operands[left][:, left_at * width : (left_at + 1) * width]
            grads = operands[right][:, right_at * width : (right_at + 1) * width]
            total_ref[...] = weight_grad(rows, grads)

    store_blocks(blocks, index_ref[0], total_ref, keep_ref, give_ref)


def turned(whole):
    bits = axis_bits()
    cols = whole.shape[1]
    split = whole.reshape((2,) * len(bits) + (-1, cols))
    for place, (axis, step) in enumerate(bits):
        mine = (lax.axis_index(axis) // step) % 2
        split = jnp.where(mine == 1, jnp.flip(split, place), split)
    order = [bits.index(bit) for bit in block_order()]
    split = split.transpose(*order, len(bits), len(bits) + 1)
    return split.reshape(1, 2, -1, cols)


def weight_grads(operands, plan, width, stacked=False):
    blocks = relative_blocks()
    half = len(blocks) // 2
    rows = width // len(blocks)
    count = len(plan)
    if rows % 8:
        pieces = []
        for left, left_at, right, right_at in plan:
            left_rows = operands[left][:, left_at * width : (left_at + 1) * width]
            grads = operands[right][:, right_at * width : (right_at + 1) * width]
            pieces.append(turned(weight_grad(left_rows, grads).astype(bf16)))
        joined = jnp.concatenate(pieces, axis=0 if stacked else 3)
        return joined[:, 0], joined[:, 1]
    if stacked:
        shape, spec = (count, half, rows, width), lambda j, index: (j, 0, 0, 0)
    else:
        shape, spec = (1, half, rows, count * width), lambda j, index: (0, 0, 0, j)
    out = jax.ShapeDtypeStruct(shape, bf16)
    spec = pl.BlockSpec((1, half, rows, width), spec)
    tokens = operands[0].shape[0]
    pair = pl.pallas_call(
        functools.partial(weight_grads_kernel, blocks, plan),
        grid_spec=pltpu.PrefetchScalarGridSpec(
            num_scalar_prefetch=1,
            grid=(count,),
            in_specs=[pl.BlockSpec(a.shape, lambda j, index: (0, 0)) for a in operands],
            out_specs=[spec, spec],
            scratch_shapes=[pltpu.VMEM((width, width), f32)],
        ),
        out_shape=[out, out],
        compiler_params=pltpu.CompilerParams(vmem_limit_bytes=VMEM_LIMIT),
        cost_estimate=pl.CostEstimate(
            flops=2 * tokens * width * width * count,
            bytes_accessed=2 * sum(a.size for a in operands) + 2 * count * width * width,
            transcendentals=0,
        ),
        name="weight_grads",
    )(small_index(), *operands)
    return [side.reshape(shape[0], half * rows, shape[3]) for side in pair]


def units_back_kernel(spread_ref, *refs):
    parts, out_ref = refs[:-1], refs[-1]
    total = None
    for part, rows_ref in enumerate(parts):
        left = rows_ref[...]
        for _ in range(3):
            piece = left.astype(bf16)
            left = left - piece.astype(f32)
            term = dot_nn(piece, spread_ref[part])
            total = term if total is None else total + term
    out_ref[...] = total


def units_back(rows, ratio, shard_rows):
    count, cols = rows.shape
    block = cols // ratio // 2
    source = jnp.arange(block, dtype=jnp.int32)
    target = jnp.arange(ratio * block, dtype=jnp.int32)
    device, rest = target // (ratio * shard_rows), target % (ratio * shard_rows)
    wanted = device * shard_rows + rest % shard_rows
    spread = jnp.stack([
        (source[:, None] == wanted[None, :]) & (rest[None, :] // shard_rows == part)
        for part in range(ratio)
    ]).astype(bf16)
    return pl.pallas_call(
        units_back_kernel,
        grid=(2,),
        in_specs=[pl.BlockSpec(spread.shape, lambda j: (0, 0, 0))] + [
            pl.BlockSpec((count, block), functools.partial(lambda part, j: (0, 2 * part + j), part))
            for part in range(ratio)
        ],
        out_specs=pl.BlockSpec((count, ratio * block), lambda j: (0, j)),
        out_shape=jax.ShapeDtypeStruct((count, cols), f32),
        compiler_params=pltpu.CompilerParams(vmem_limit_bytes=VMEM_LIMIT),
        name="units_back",
    )(spread, *[rows] * ratio)


SMALL_COLUMNS = 128


def small_grads_kernel(blocks, layers, index_ref, *refs):
    sources, (keep_ref, give_ref, lines_ref, columns_ref) = refs[:-4], refs[-4:]
    lines_ref[...] = jnp.zeros_like(lines_ref)
    width = lines_ref.shape[1]
    each = len(sources) // layers
    at = 0
    for layer in range(layers):
        *vectors, up_ref, taps_ref = sources[layer * each : (layer + 1) * each]
        for vector in vectors:
            lines_ref[at : at + 1, :] = vector[...]
            at += 1
        for kind in range(2):
            lines_ref[at : at + TAPS, :] = taps_ref[kind, :TAPS]
            at += TAPS
        for part in range(up_ref.shape[1] // width):
            lines_ref[at : at + 1, :] = up_ref[:, part * width : (part + 1) * width]
            at += 1
    columns_ref[...] = jnp.transpose(lines_ref[...])
    store_blocks(blocks, index_ref[0], columns_ref, keep_ref, give_ref)


def small_grads(per_layer, width):
    blocks = relative_blocks()
    half = len(blocks) // 2
    rows = width // len(blocks)
    if rows % 8:
        lines = []
        for *vectors, up, taps in per_layer:
            lines += vectors + [taps[0, :TAPS], taps[1, :TAPS], up.reshape(-1, width)]
        lines = jnp.concatenate(lines, axis=0)
        lines = jnp.pad(lines, ((0, SMALL_COLUMNS - lines.shape[0]), (0, 0))).T.astype(bf16)
        lines = turned(lines)
        return lines[:, 0], lines[:, 1]
    flat = [a for arrays in per_layer for a in arrays]
    out = jax.ShapeDtypeStruct((1, half, rows, SMALL_COLUMNS), bf16)
    pair = pl.pallas_call(
        functools.partial(small_grads_kernel, blocks, len(per_layer)),
        in_specs=[pl.BlockSpec(memory_space=pltpu.SMEM)]
        + [pl.BlockSpec(memory_space=pltpu.VMEM)] * len(flat),
        out_specs=[pl.BlockSpec(memory_space=pltpu.VMEM)] * 2,
        out_shape=[out, out],
        scratch_shapes=[pltpu.VMEM((SMALL_COLUMNS, width), f32), pltpu.VMEM((width, SMALL_COLUMNS), f32)],
        compiler_params=pltpu.CompilerParams(vmem_limit_bytes=VMEM_LIMIT),
        name="small_grads",
    )(small_index(), *flat)
    return [side.reshape(1, half * rows, SMALL_COLUMNS) for side in pair]


def layer_forward(x, weights, masks, select, count, at):
    qkv_weight, late_weights, small = weights
    width = x.shape[1]
    length = x.shape[0] // count
    x_low = x.astype(bf16)
    bias = jnp.concatenate([small["query_bias"], jnp.zeros((width,), f32), small["value_bias"]])
    qkv = matmul(x_low, qkv_weight)
    qkv = at("projected", (qkv + bias).astype(bf16).reshape(count, length, -1))
    rows_low = passed_along(qkv[:, length - WIN :, width:], 1)
    rows_up = passed_along(qkv[:, :WIN, width:], -1)
    pooled = at("pooled", pool(select, small["taps"], qkv, rows_low, width))
    pooled_low, pooled_up = pooled_rims(pooled)
    pooled_up = at("attending", pooled_up)
    operands = attend_operands(qkv, rows_low, rows_up, pooled, pooled_low, pooled_up)
    mixed, stats = attend(masks, operands, width)
    mixed = at("attended", mixed.reshape(count * length, width))
    out_weight, up_weight, down_weight = late_weights()
    norm, inverse = normalised(x + matmul(mixed, out_weight) + small["output_bias"])
    hidden = norm * small["mixer_gain"] + small["mixer_shift"]
    hidden = at("mixed", hidden)
    hidden_low = hidden.astype(bf16)
    act, slope = gelu_both(matmul(hidden_low, up_weight) + small["up_bias"])
    act_low, slope = act.astype(bf16), slope.astype(bf16)
    norm_two, inverse_two = normalised(hidden + matmul(act_low, down_weight) + small["down_bias"])
    y = at("fed", norm_two * small["feed_gain"] + small["feed_shift"])
    kept = (x_low, operands, stats, mixed, norm, inverse, hidden_low, act_low, slope,
            norm_two, inverse_two)
    return y, kept, (qkv_weight, out_weight, up_weight, down_weight, small)


def layer_backward(grads, kept, weights, masks, select, count, at):
    qkv_weight, out_weight, up_weight, down_weight, small = weights
    (x_low, operands, stats, mixed, norm, inverse, hidden_low, act_low, slope,
     norm_two, inverse_two) = kept
    rows, width = grads.shape
    length = rows // count
    ratio = act_low.shape[1] // width

    def total(value):
        return jnp.sum(value.astype(f32), axis=0, keepdims=True)

    feed_gain, feed_shift = total(grads * norm_two), total(grads)
    grad_two = normalised_back(grads, small["feed_gain"], norm_two, inverse_two)
    feed_low = grad_two.astype(bf16)
    feed_low = at("down", feed_low, (act_low, feed_low))
    grad_pre = (slope.astype(f32) * matmul_t(feed_low, down_weight)).astype(bf16)
    grad_pre = at("up", grad_pre, (hidden_low, grad_pre))
    grad_hidden = grad_two + matmul_t(grad_pre, up_weight)
    mixer_gain, mixer_shift = total(grad_hidden * norm), total(grad_hidden)
    grad_one = normalised_back(grad_hidden, small["mixer_gain"], norm, inverse)
    attention_low = grad_one.astype(bf16)
    grad_mixed = matmul_t(attention_low, out_weight).astype(bf16).reshape(count, length, width)
    grad_mixed = at("attending", grad_mixed)
    grad_query, own, pooled_own, rim_low, rim_up = attend_back(masks, stats, grad_mixed, operands)
    grad_query = grad_query.reshape(rows, width)
    from_low, from_up, pooled_own = rims_return(rim_low, rim_up, pooled_own)
    pooled_own = at("attended", pooled_own, (x_low, grad_query, mixed, attention_low))
    own, tail, taps = pool_back(
        select, small["taps"], operands[0], operands[3], own, pooled_own, from_low, from_up
    )
    tail = passed_along(tail, -1).astype(f32)
    own = at("pooled", own)
    own = own + jnp.pad(tail, ((0, 0), (0, 0), (length - 16, 0), (0, 0)))
    own = own.astype(bf16).reshape(2, rows, width)
    grad_qkv = (grad_query, own[0], own[1])
    grad_x = grad_one + matmul_t(jnp.concatenate(grad_qkv, axis=1), qkv_weight)
    small_sums = [
        total(grad_query), total(own[1]), total(attention_low), total(feed_low),
        mixer_gain, mixer_shift, feed_gain, feed_shift, total(grad_pre), taps,
    ]
    return grad_x, (x_low, *grad_qkv, mixed, attention_low), small_sums


def pack_small(vectors, up_biases, taps):
    columns = []
    for layer in range(vectors[0].shape[0]):
        rows = vectors[0].shape[1]
        columns.append(jnp.stack([v[layer] for v in vectors]))
        columns.append(taps[0][layer])
        columns.append(taps[1][layer])
        columns.append(up_biases[layer].reshape(-1, rows))
    packed = jnp.concatenate(columns, axis=0)
    return jnp.pad(packed, ((0, SMALL_COLUMNS - packed.shape[0]), (0, 0))).T


def unpack_small(columns, layers, ratio):
    width = columns.shape[0]
    lines = columns.astype(f32).T
    per_layer = 8 + 2 * TAPS + ratio
    pad = ((0, 8 - TAPS), (0, 0))
    result = []
    for layer in range(layers):
        piece = lines[layer * per_layer : (layer + 1) * per_layer]
        result.append({
            "query_bias": piece[0],
            "value_bias": piece[1],
            "output_bias": piece[2],
            "down_bias": piece[3],
            "mixer_gain": piece[4],
            "mixer_shift": piece[5],
            "feed_gain": piece[6],
            "feed_shift": piece[7],
            "taps": jnp.stack([
                jnp.pad(piece[8 : 8 + TAPS], pad), jnp.pad(piece[8 + TAPS : 8 + 2 * TAPS], pad),
            ]),
            "up_bias": piece[8 + 2 * TAPS :].reshape(ratio * width),
        })
    return result


def on_device(
    tokens, cotangent, masked, query_weight, key_weight, value_weight, output_weight, up_weight,
    down_weight, query_bias, value_bias, output_bias, up_bias, down_bias, mixer_gain, mixer_shift,
    feed_gain, feed_shift, pool_key, pool_value,
):
    micro, seqs, length, width = tokens.shape
    count = micro * seqs
    layers = query_weight.shape[0]
    devices = lax.axis_size("seq") * lax.axis_size("batch")
    shard_rows = width // devices
    small_shard = pack_small(
        (query_bias, value_bias, output_bias, down_bias, mixer_gain, mixer_shift, feed_gain,
         feed_shift), up_bias, (pool_key, pool_value),
    )
    masks = window_masks(length)
    select = tap_select(length)
    ratio = up_weight.shape[2] // width

    def units_apart(rows):
        split = rows.reshape(rows.shape[0], devices, ratio, shard_rows)
        return split.transpose(0, 2, 1, 3).reshape(rows.shape)

    up_shards = [units_apart(up_weight[layer]) for layer in range(layers)]
    down_shards = [down_weight[layer].reshape(ratio, shard_rows, width) for layer in range(layers)]
    shard = jnp.concatenate(
        [query_weight[0], key_weight[0], value_weight[0], small_shard], axis=1
    )
    first = Gather(shard[None], path("y"))

    later = [
        Gather(jnp.concatenate(
            [query_weight[layer], key_weight[layer], value_weight[layer]], axis=1
        )[None], path("z"))
        for layer in range(1, layers)
    ]
    x = tokens.reshape(count * length, width).astype(f32)
    feeds = []
    for layer in range(layers):
        shard = jnp.concatenate(
            [output_weight[layer], up_shards[layer], *down_shards[layer]], axis=1
        )
        feeds.append(lax.all_gather(shard, ("seq", "batch"), axis=0, tiled=True))
    x = checkpoint(x, [], [first])
    while first.left > 1:
        x = checkpoint(x, [first])
    x = checkpoint(x, [first], later)
    first_whole = in_place(first.halves, first.cols)
    smalls = unpack_small(first_whole[:, 3 * width :], layers, ratio)

    def late_weights(layer):
        whole = feeds[layer]
        down_whole = whole[:, (1 + ratio) * width :].reshape(width, ratio, width)
        return (
            whole[:, :width], whole[:, width : (1 + ratio) * width],
            down_whole.transpose(1, 0, 2).reshape(-1, width),
        )

    def landed(value, flows, left):
        while True:
            behind = [flow for flow in flows if flow.left > left]
            if not behind:
                return value
            value = checkpoint(value, behind)

    def forward_at(layer):
        following = later[layer : layer + 1]

        def at(name, value):
            if name in ("projected", "pooled", "attended"):
                return checkpoint(value, following)
            if name == "fed":
                return landed(value, following, 0)
            return value

        return at

    states, weights = [], []
    for layer in range(layers):
        if layer == 0:
            qkv_weight = first_whole[:, : 3 * width]
        else:
            qkv_weight = in_place(later[layer - 1].halves, width)
        late = functools.partial(late_weights, layer)
        x, kept, whole = layer_forward(
            x, (qkv_weight, late, smalls[layer]), masks, select, count, forward_at(layer)
        )
        states.append(kept)
        weights.append(whole)
    layer_output = x.astype(bf16).reshape(tokens.shape)
    grads = cotangent.astype(f32) * masked.astype(f32)[..., None]
    grads = grads.reshape(count * length, width)
    flows = {}
    plans = {
        "down": ["up", "attended", "pooled", "end", "next down", "never"],
        "up": ["attending", "pooled", "end", "next up", "next attending", "never"],
        "in": ["next down", "next attended", "next pooled", "never"],
        "query": ["pooled", "never"],
    }

    def due(layer, name):
        result = []
        for (kind, owner), flow in flows.items():
            when = plans[kind][min(flow.stage, len(plans[kind]) - 1)]
            if not flow.done and when == ("next " if owner > layer else "") + name:
                result.append(flow)
            elif not flow.done and owner > layer + 1:
                result.append(flow)
        return result

    def backward_at(layer):
        def at(name, value, given=None):
            landing, begin = due(layer, name), []
            if name == "down":
                plan = [(0, part, 1, 0) for part in range(ratio)]
                flow = Scatter(weight_grads(given, plan, width, stacked=True), path("y")[::-1])
                flows[name, layer] = flow
                begin.append(flow)
            if name == "up":
                plan = [(0, 0, 1, part) for part in range(ratio)]
                flow = Scatter(weight_grads(given, plan, width), path("x")[::-1])
                flows[name, layer] = flow
                begin.append(flow)
            if name == "attended" and layer == 0:
                plan = [(0, 0, 1, 0), (2, 0, 3, 0)]
                flow = Scatter(weight_grads(given, plan, width), path("z")[::-1])
                flows["query", layer] = flow
                begin.append(flow)
            return checkpoint(value, landing, begin)

        return at

    small_sums = [None] * layers
    for layer in reversed(range(layers)):
        grads, given, small_sums[layer] = layer_backward(
            grads, states[layer], weights[layer], masks, select, count, backward_at(layer)
        )
        if layer > 0:
            plan = [(0, 0, 1 + i, 0) for i in range(3)] + [(4, 0, 5, 0)]
            flow = Scatter(weight_grads(given, plan, width), path("z")[::-1])
            flows["in", layer] = flow
            grads = checkpoint(grads, due(layer, "end"), [flow])
    halves = weight_grads((given[0], *given[2:4]), [(0, 0, 1, 0), (0, 0, 2, 0)], width)
    sides = small_grads(small_sums, width)
    joined = [jnp.concatenate(parts, axis=2) for parts in zip(halves, sides)]
    last = Scatter(joined, path("y")[::-1])
    flows["last", 0] = last
    marker = checkpoint(last.keep[:1, :1, :1], [], [last])
    while True:
        flying = [flow for flow in flows.values() if not flow.done]
        if not flying:
            break
        marker = checkpoint(marker, flying)
    totals = []
    for layer in range(layers):
        if layer > 0:
            whole = flows["in", layer].total[0]
            parts = [whole[:, i * width : (i + 1) * width] for i in range(4)]
        else:
            whole = flows["query", 0].total[0]
            end = last.total[0]
            parts = [whole[:, :width], end[:, :width], end[:, width : 2 * width], whole[:, width:]]
        parts.append(flows["up", layer].total[0])
        parts.append(flows["down", layer].total.reshape(ratio * shard_rows, width))
        totals.append(parts)
    up_totals = units_back(
        jnp.concatenate([parts[4] for parts in totals]), ratio, shard_rows
    ).reshape(layers, shard_rows, ratio * width)
    input_grad = grads.astype(bf16).reshape(tokens.shape)
    lines = last.total[0, :, 2 * width :].T
    per_layer = 8 + 2 * TAPS + ratio
    lines = lines[: layers * per_layer].reshape(layers, per_layer, shard_rows)
    vectors = [lines[:, i] for i in range(8)]
    after = 8 + 2 * TAPS
    grad_up_bias = lines[:, after:].reshape(layers, -1)
    return (
        layer_output, input_grad,
        *[jnp.stack([t[i] for t in totals]) if i != 4 else up_totals for i in range(6)],
        vectors[0], vectors[1], vectors[2], grad_up_bias, *vectors[3:],
        lines[:, 8 : 8 + TAPS], lines[:, 8 + TAPS : after],
    )


def solution(mesh):
    rows = P(None, "batch", "seq", None)
    matrix = P(None, ("seq", "batch"), None)
    vector = P(None, ("seq", "batch"))
    taps = P(None, None, ("seq", "batch"))
    params = (matrix,) * 6 + (vector,) * 9 + (taps,) * 2
    return jax.shard_map(
        on_device,
        mesh=mesh,
        in_specs=(rows, rows, P(None, "batch", "seq")) + params,
        out_specs=(rows, rows) + params,
        check_vma=False,
    )
```

```python
import functools

import jax
import jax.numpy as jnp
from jax import lax
from jax.experimental import pallas as pl
from jax.experimental.pallas import tpu as pltpu
from jax.sharding import PartitionSpec as P

HEADS = 12
WIN = 64
PWIN = 256
TAPS = 5
REACH = PWIN // 4
QROWS = 128
norm_eps = 1e-05
gelu_coef = 0.7978845608028654
masked_score = -1e30
f32 = jnp.float32
bf16 = jnp.bfloat16
VMEM_LIMIT = 48 * 1024 * 1024


def axis_bits():
    bits = []
    for axis in ("seq", "batch"):
        step = lax.axis_size(axis) // 2
        while step:
            bits.append((axis, step))
            step //= 2
    return bits


def path(name):
    bits = axis_bits()
    core, row = ("seq", 1), ("seq", 2)
    column = [bit for bit in bits if bit[0] == "seq" and bit[1] > 2]
    across = [bit for bit in bits if bit[0] == "batch"]
    order = {
        "y": column + across + [row],
        "x": column + [row] + across,
        "z": column[:-1] + across + [row] + column[-1:],
        "w": [row] + column + across,
    }[name]
    return order + [core]


def exchange(value, axis, step):
    pairs = [(i, i ^ step) for i in range(lax.axis_size(axis))]
    return lax.ppermute(value, axis, pairs)


def block_order():
    bits = axis_bits()
    return [("seq", 1), ("seq", 2)] + [b for b in bits if b[0] == "batch"] + [
        b for b in bits if b[0] == "seq" and b[1] > 2
    ]


def flat_index():
    return lax.axis_index("seq") * lax.axis_size("batch") + lax.axis_index("batch")


def relative_blocks():
    spread = []
    for axis, step in block_order():
        spread.append(step * lax.axis_size("batch") if axis == "seq" else step)
    count = len(spread)
    return [
        sum(spread[k] for k in range(count) if place >> (count - 1 - k) & 1)
        for place in range(2**count)
    ]


def tied(values):
    return list(lax.optimization_barrier(tuple(values)))


class Gather:
    def __init__(self, shard, order):
        self.current, self.order = shard, order
        self.have, self.halves, self.flying = [], None, None
        self.parts, self.rows, self.cols = shard.shape

    def ready(self):
        return self.current

    def hold(self, value):
        self.current = value

    def launch(self):
        self.flying = exchange(self.current, *self.order[len(self.have)])

    def land(self):
        stage = self.order[len(self.have)]
        if stage == self.order[-1]:
            self.halves = (self.current, self.flying)
            return
        significance = block_order()
        place = significance.index(stage)
        before = sum(1 for p in self.have if p < place)
        split = (self.parts * 2**before, 1, 2 ** (len(self.have) - before) * self.rows, self.cols)
        self.have.append(place)
        joined = jnp.concatenate([self.current.reshape(split), self.flying.reshape(split)], axis=1)
        self.current = joined.reshape(self.parts, 2 ** len(self.have) * self.rows, self.cols)

    @property
    def left(self):
        return 0 if self.halves is not None else len(self.order) - len(self.have)

    @property
    def done(self):
        return self.halves is not None


class Scatter:
    def __init__(self, halves, order):
        self.keep, self.give = halves
        self.order, self.stage, self.total, self.flying = order, 0, None, None
        self.have = list(range(1, len(order)))
        self.parts, half_rows, self.cols = self.keep.shape
        self.rows = half_rows // 2 ** len(self.have)

    def ready(self):
        return self.give

    def hold(self, value):
        self.give = value

    def launch(self):
        self.flying = exchange(self.give, *self.order[self.stage])

    def land(self):
        self.stage += 1
        if self.stage == len(self.order):
            total = self.keep.astype(f32) + self.flying.astype(f32)
            self.total = total.reshape(self.parts, self.rows, self.cols)
            return
        place = self.have.index(block_order().index(self.order[self.stage]))
        self.have.pop(place)
        left = 2 ** len(self.have) * self.rows
        split = (self.parts * 2**place, 2, left >> place, self.cols)
        keep, got = self.keep.reshape(split), self.flying.reshape(split)
        self.keep, self.give = [
            (keep[:, side].astype(f32) + got[:, side].astype(f32)).astype(bf16).reshape(
                self.parts, left, self.cols
            ) for side in range(2)
        ]

    @property
    def done(self):
        return self.total is not None


def checkpoint(value, flows, begin=(), waiting=()):
    value, *flying = tied([value] + [flow.flying for flow in flows])
    for flow, arrived in zip(flows, flying):
        flow.flying = arrived
        flow.land()
    going = [flow for flow in flows if not flow.done and flow not in waiting] + list(begin)
    value, *ready = tied([value] + [flow.ready() for flow in going])
    for flow, part in zip(going, ready):
        flow.hold(part)
        flow.launch()
    return value


def passed_along(value, steps):
    count = lax.axis_size("seq")
    pairs = [(i, i + steps) for i in range(count) if 0 <= i + steps < count]
    return lax.ppermute(value, "seq", pairs)


def pooled_hops(size):
    return -(-REACH // size)


def pooled_rims(pooled):
    size = pooled.shape[1]
    hops = range(1, pooled_hops(size) + 1)
    low = [passed_along(pooled, hop) for hop in reversed(hops)]
    up = [passed_along(pooled, -hop) for hop in hops]
    low = low[0] if len(low) == 1 else jnp.concatenate(low, axis=1)
    up = up[0] if len(up) == 1 else jnp.concatenate(up, axis=1)
    return low[:, low.shape[1] - REACH :], up[:, :REACH]


def rims_return(rim_low, rim_up, pooled_own):
    size = pooled_own.shape[2]
    hops = pooled_hops(size)
    far_low, far_up = rim_low[:, :, WIN:], rim_up[:, :, WIN:]
    for hop in range(2, hops + 1):
        start = REACH - hop * size
        pooled_own = pooled_own + passed_along(far_low[:, :, start : start + size], -hop).astype(f32)
        start = (hop - 1) * size
        pooled_own = pooled_own + passed_along(far_up[:, :, start : start + size], hop).astype(f32)
    if hops > 1:
        near_low, near_up = rim_low[:, :, :WIN], rim_up[:, :, :WIN]
        rim_low = jnp.concatenate([near_low, far_low[:, :, REACH - size :]], axis=2)
        rim_up = jnp.concatenate([near_up, far_up[:, :, :size]], axis=2)
    return passed_along(rim_up, 1), passed_along(rim_low, -1), pooled_own


def dot_nt(a, b):
    return lax.dot_general(a, b, (((1,), (1,)), ((), ())), preferred_element_type=f32)


def dot_nn(a, b):
    return lax.dot_general(a, b, (((1,), (0,)), ((), ())), preferred_element_type=f32)


def flipped(block):
    return jnp.transpose(block.astype(f32)).astype(bf16)


def two_heads(rows):
    lane = lax.broadcasted_iota(jnp.int32, rows.shape, 1)
    none = jnp.zeros_like(rows)
    half = rows.shape[1] // 2
    return jnp.concatenate(
        [jnp.where(lane < half, rows, none), jnp.where(lane < half, none, rows)], axis=0
    )


def heads_apart(block):
    half, queries = block.shape[0] // 2, block.shape[1] // 2
    return jnp.transpose(
        jnp.concatenate([block[:half, :queries], block[half:, queries:]], axis=0)
    )


def attend_kernel(near_ref, far_ref, q_ref, k_ref, v_ref, kl_ref, vl_ref, ku_ref, vu_ref,
                  pk_ref, pv_ref, pkl_ref, pvl_ref, pku_ref, pvu_ref, mixed_ref, stat_ref):
    blocks = q_ref.shape[1] // QROWS
    pairs = q_ref.shape[2] // 128
    for pair in range(pairs):
        at = slice(128 * pair, 128 * pair + 128)
        keys = jnp.concatenate([kl_ref[0, :, at], k_ref[0, :, at], ku_ref[0, :, at]], axis=0)
        values = jnp.concatenate([vl_ref[0, :, at], v_ref[0, :, at], vu_ref[0, :, at]], axis=0)
        far_keys = jnp.concatenate([pkl_ref[0, :, at], pk_ref[0, :, at], pku_ref[0, :, at]], axis=0)
        far_values = jnp.concatenate(
            [pvl_ref[0, :, at], pv_ref[0, :, at], pvu_ref[0, :, at]], axis=0
        )
        values_t, far_values_t = flipped(values), flipped(far_values)
        for block in range(blocks):
            first = QROWS * block
            query = two_heads(q_ref[0, first : first + QROWS, at] * 0.125)
            stop = first + QROWS + 2 * WIN
            score = dot_nt(keys[first:stop], query) + near_ref[block]
            top = jnp.max(score, axis=0, keepdims=True)
            prob = jnp.exp(score - top)
            total = jnp.sum(prob, axis=0, keepdims=True)
            near_low = (prob * (1.0 / total)).astype(bf16)
            row = (pair * blocks + block) * 2
            stat_ref[0, 0, row : row + 1, :] = top + jnp.log(total)
            score = dot_nt(far_keys, query) + far_ref[block]
            top = jnp.max(score, axis=0, keepdims=True)
            prob = jnp.exp(score - top)
            total = jnp.sum(prob, axis=0, keepdims=True)
            far_low = (prob * (1.0 / total)).astype(bf16)
            stat_ref[0, 0, row + 1 : row + 2, :] = top + jnp.log(total)
            mixed = dot_nn(values_t[:, first:stop], near_low) + dot_nn(far_values_t, far_low)
            mixed_ref[0, first : first + QROWS, at] = heads_apart(mixed).astype(bf16)


def attend_back_kernel(near_ref, far_ref, stat_ref, g_ref, q_ref, k_ref, v_ref, kl_ref, vl_ref,
                       ku_ref, vu_ref, pk_ref, pv_ref, pkl_ref, pvl_ref, pku_ref, pvu_ref,
                       dq_ref, own_ref, pool_ref, low_ref, up_ref):
    blocks = q_ref.shape[1] // QROWS
    pairs = q_ref.shape[2] // 128
    length = q_ref.shape[1]
    for pair in range(pairs):
        at = slice(128 * pair, 128 * pair + 128)
        keys = jnp.concatenate([kl_ref[0, :, at], k_ref[0, :, at], ku_ref[0, :, at]], axis=0)
        values = jnp.concatenate([vl_ref[0, :, at], v_ref[0, :, at], vu_ref[0, :, at]], axis=0)
        far_keys = jnp.concatenate([pkl_ref[0, :, at], pk_ref[0, :, at], pku_ref[0, :, at]], axis=0)
        far_values = jnp.concatenate(
            [pvl_ref[0, :, at], pv_ref[0, :, at], pvu_ref[0, :, at]], axis=0
        )
        keys_t, far_keys_t = flipped(keys), flipped(far_keys)
        near_parts = ([], [])
        far_totals = [None, None]
        for block in range(blocks):
            first = QROWS * block
            query = two_heads(q_ref[0, first : first + QROWS, at] * 0.125)
            grads = two_heads(g_ref[0, first : first + QROWS, at])
            stop = first + QROWS + 2 * WIN
            row = (pair * blocks + block) * 2
            prob = jnp.exp(
                dot_nt(keys[first:stop], query) + near_ref[block] - stat_ref[0, 0, row : row + 1, :]
            )
            grad_prob = dot_nt(values[first:stop], grads)
            inner = jnp.sum(prob * grad_prob, axis=0, keepdims=True)
            grad_score = (prob * (grad_prob - inner)).astype(bf16)
            near_parts[0].append(dot_nn(grad_score, query))
            near_parts[1].append(dot_nn(prob.astype(bf16), grads))
            grad_query = dot_nn(keys_t[:, first:stop], grad_score)
            prob = jnp.exp(
                dot_nt(far_keys, query) + far_ref[block] - stat_ref[0, 0, row + 1 : row + 2, :]
            )
            grad_prob = dot_nt(far_values, grads)
            inner = jnp.sum(prob * grad_prob, axis=0, keepdims=True)
            grad_score = (prob * (grad_prob - inner)).astype(bf16)
            parts = (dot_nn(grad_score, query), dot_nn(prob.astype(bf16), grads))
            grad_query = grad_query + dot_nn(far_keys_t, grad_score)
            dq_ref[0, first : first + QROWS, at] = (heads_apart(grad_query) * 0.125).astype(bf16)
            for kind in range(2):
                far_totals[kind] = parts[kind] if block == 0 else far_totals[kind] + parts[kind]
        for kind in range(2):
            rows = []
            for chunk in range(blocks + 1):
                terms = []
                if chunk < blocks:
                    terms.append(near_parts[kind][chunk][:QROWS])
                if chunk > 0:
                    terms.append(near_parts[kind][chunk - 1][QROWS:])
                rows.append(functools.reduce(jnp.add, terms))
            rows = jnp.concatenate(rows, axis=0)
            own_ref[kind, 0, :, at] = rows[WIN : WIN + length]
            low_ref[kind, 0, :WIN, at] = rows[:WIN].astype(bf16)
            up_ref[kind, 0, :WIN, at] = rows[WIN + length :].astype(bf16)
            far = far_totals[kind]
            pool_ref[kind, 0, :, at] = far[REACH : far.shape[0] - REACH]
            low_ref[kind, 0, WIN:, at] = far[:REACH].astype(bf16)
            up_ref[kind, 0, WIN:, at] = far[far.shape[0] - REACH :].astype(bf16)


LANES = 256


def attend_specs(length, width):
    groups = width // LANES
    pooled = length // 4

    def spec(rows, shift):
        return pl.BlockSpec((1, rows, LANES), lambda g, j: (g, 0, j + shift))

    def whole(count, rows):
        return pl.BlockSpec((count, rows, 2 * QROWS), lambda g, j: (0, 0, 0))

    blocks = length // QROWS
    masks = [whole(blocks, QROWS + 2 * WIN), whole(blocks, pooled + 2 * REACH)]
    stat_rows = LANES // 128 * blocks * 2
    stat = pl.BlockSpec((1, 1, stat_rows, 2 * QROWS), lambda g, j: (g, j, 0, 0))
    operands = [spec(length, 0), spec(length, groups), spec(length, 2 * groups)]
    operands += [spec(WIN, 0), spec(WIN, groups)] * 2
    operands += [spec(pooled, 0), spec(pooled, groups)]
    operands += [spec(REACH, 0), spec(REACH, groups)] * 2
    return groups, masks, stat, stat_rows, operands, spec


def attend_operands(qkv, rows_low, rows_up, pooled, pooled_low, pooled_up):
    return (
        qkv, qkv, qkv, rows_low, rows_low, rows_up, rows_up,
        pooled, pooled, pooled_low, pooled_low, pooled_up, pooled_up,
    )


def attend(masks, operands, width):
    qkv = operands[0]
    count, length = qkv.shape[:2]
    groups, mask_specs, stat, stat_rows, specs, spec = attend_specs(length, width)
    return pl.pallas_call(
        attend_kernel,
        grid=(count, groups),
        in_specs=mask_specs + specs,
        out_specs=[spec(length, 0), stat],
        out_shape=[
            jax.ShapeDtypeStruct((count, length, width), bf16),
            jax.ShapeDtypeStruct((count, groups, stat_rows, 2 * QROWS), f32),
        ],
        compiler_params=pltpu.CompilerParams(vmem_limit_bytes=VMEM_LIMIT),
        cost_estimate=pl.CostEstimate(
            flops=count * length * width * 2000, bytes_accessed=8000000, transcendentals=3000000
        ),
        name="attend",
    )(*masks, *operands)


def attend_back(masks, stats, grad_mixed, operands, first, count, before=None):
    every, length, width = grad_mixed.shape
    groups, mask_specs, stat, stat_rows, specs, spec = attend_specs(length, width)
    pooled = length // 4

    def pair_spec(rows):
        return pl.BlockSpec((2, 1, rows, LANES), lambda g, j: (0, g, 0, j))

    def moved(block):
        index_map = block.index_map
        return pl.BlockSpec(block.block_shape, lambda g, j: index_map(g + first, j))

    in_specs = [stat, spec(length, 0)] + specs
    out_specs = [
        spec(length, 0), pair_spec(length), pair_spec(pooled),
        pair_spec(WIN + REACH), pair_spec(WIN + REACH),
    ]
    out_specs = [moved(block) for block in out_specs[:1]] + [
        pl.BlockSpec(
            block.block_shape, functools.partial(lambda g, j: (0, g + first, 0, j))
        ) for block in out_specs[1:]
    ]
    before = before or []
    kernel_inputs = len(mask_specs) + len(in_specs)

    def kernel(*refs):
        attend_back_kernel(*refs[:kernel_inputs], *refs[kernel_inputs + len(before) :])

    return pl.pallas_call(
        kernel,
        grid=(count, groups),
        in_specs=mask_specs + [moved(block) for block in in_specs]
        + [pl.BlockSpec(memory_space=pl.ANY)] * len(before),
        out_specs=out_specs,
        out_shape=[
            jax.ShapeDtypeStruct((every, length, width), bf16),
            jax.ShapeDtypeStruct((2, every, length, width), f32),
            jax.ShapeDtypeStruct((2, every, pooled, width), f32),
            jax.ShapeDtypeStruct((2, every, WIN + REACH, width), bf16),
            jax.ShapeDtypeStruct((2, every, WIN + REACH, width), bf16),
        ],
        input_output_aliases={kernel_inputs + i: i for i in range(len(before))},
        compiler_params=pltpu.CompilerParams(vmem_limit_bytes=VMEM_LIMIT),
        cost_estimate=pl.CostEstimate(
            flops=count * length * width * 5000, bytes_accessed=6000000 * count,
            transcendentals=1500000 * count,
        ),
        name="attend_back",
    )(*masks, stats, grad_mixed, *operands, *before)


def window_masks(length):
    blocks = length // QROWS
    index, devices = lax.axis_index("seq"), lax.axis_size("seq")

    def bias(width, offset, scale, reach):
        key = lax.broadcasted_iota(jnp.int32, (blocks, width, QROWS), 1)
        query = lax.broadcasted_iota(jnp.int32, (blocks, width, QROWS), 2)
        block = lax.broadcasted_iota(jnp.int32, (blocks, width, QROWS), 0)
        key = key - offset + (block * QROWS if scale == 1 else 0)
        query = query + block * QROWS
        size = length // scale
        allowed = jnp.abs(query - scale * key) <= reach
        place = key + index * size
        allowed &= (place >= 0) & (place < size * devices)
        one = jnp.where(allowed, 0.0, masked_score).astype(f32)
        return jnp.concatenate([one, one], axis=2)

    return bias(QROWS + 2 * WIN, WIN, 1, WIN), bias(length // 4 + 2 * REACH, REACH, 4, PWIN)


def tap_select(length):
    pooled = length // 4
    row = jnp.arange(TAPS * pooled, dtype=jnp.int32)
    column = jnp.arange(length, dtype=jnp.int32)
    source = 4 * (row % pooled) + row // pooled - 2
    return (source[:, None] == column[None, :]).astype(bf16)


def pool_kernel(select_ref, kernel_ref, rows_ref, low_ref, pooled_ref):
    pooled = pooled_ref.shape[1]
    for group in range(rows_ref.shape[0]):
        taps = dot_nn(select_ref[...], rows_ref[group])
        total = kernel_ref[0, 0:1, :] * taps[:pooled]
        for tap in range(1, TAPS):
            total = total + kernel_ref[0, tap : tap + 1, :] * taps[tap * pooled : (tap + 1) * pooled]
        low = low_ref[group].astype(f32)
        edge = kernel_ref[0, 0:1, :] * low[14:15] + kernel_ref[0, 1:2, :] * low[15:16]
        row = lax.broadcasted_iota(jnp.int32, total.shape, 0)
        pooled_ref[group] = (total + jnp.where(row == 0, edge, 0.0)).astype(bf16)


def pool(select, kernel, qkv, rows_low, width):
    count, length = qkv.shape[:2]
    groups = width // LANES
    return pl.pallas_call(
        pool_kernel,
        grid=(2 * groups,),
        in_specs=[
            pl.BlockSpec(select.shape, lambda j: (0, 0)),
            pl.BlockSpec((1, 8, LANES), lambda j: (j // groups, 0, j % groups)),
            pl.BlockSpec((count, length, LANES), lambda j: (0, 0, j + groups)),
            pl.BlockSpec((count, 16, LANES), lambda j: (0, WIN // 16 - 1, j)),
        ],
        out_specs=pl.BlockSpec((count, length // 4, LANES), lambda j: (0, 0, j)),
        out_shape=jax.ShapeDtypeStruct((count, length // 4, 2 * width), bf16),
        compiler_params=pltpu.CompilerParams(vmem_limit_bytes=VMEM_LIMIT),
        cost_estimate=pl.CostEstimate(
            flops=count * length * width * 1300, bytes_accessed=2500000, transcendentals=0
        ),
        name="pool",
    )(select, kernel, qkv, rows_low)


def pool_back_kernel(select_ref, spread_ref, kernel_ref, rows_ref, low_rows_ref, own_ref, pool_ref,
                     low_ref, up_ref, grad_ref, tail_ref, taps_ref):
    pooled = pool_ref.shape[2]
    length = rows_ref.shape[1]
    tap_row = lax.broadcasted_iota(jnp.int32, (8, LANES), 0)
    tail_row = lax.broadcasted_iota(jnp.int32, (16, LANES), 0)
    taps_total = jnp.zeros((8, LANES), f32)
    for group in range(rows_ref.shape[0]):
        grads = pool_ref[0, group] + low_ref[0, group, WIN:].astype(f32)
        grads = (grads + up_ref[0, group, WIN:].astype(f32)).astype(bf16).astype(f32)
        taps = dot_nn(select_ref[...], rows_ref[group])
        low_rows = low_rows_ref[group].astype(f32)
        edge = grads[0:1]
        spread = []
        for tap in range(TAPS):
            line = jnp.sum(grads * taps[tap * pooled : (tap + 1) * pooled], axis=0, keepdims=True)
            if tap < 2:
                line = line + edge * low_rows[14 + tap : 15 + tap]
            taps_total = taps_total + jnp.where(tap_row == tap, line, 0.0)
            spread.append(grads * kernel_ref[0, tap : tap + 1, :])
        spread = jnp.concatenate(spread, axis=0)
        high = spread.astype(bf16)
        rest = (spread - high.astype(f32)).astype(bf16)
        total = own_ref[0, group] + dot_nn(spread_ref[...], high) + dot_nn(spread_ref[...], rest)
        grad_ref[0, group] = total
        grad_ref[0, group, :WIN] = total[:WIN] + low_ref[0, group, :WIN].astype(f32)
        grad_ref[0, group, length - WIN :] = total[length - WIN :] + up_ref[0, group, :WIN].astype(f32)
        tail = jnp.where(tail_row == 14, edge * kernel_ref[0, 0:1, :], 0.0)
        tail = tail + jnp.where(tail_row == 15, edge * kernel_ref[0, 1:2, :], 0.0)
        tail_ref[0, group] = tail.astype(bf16)
    taps_ref[0] = taps_total


def pool_back(select, kernel, qkv, rows_low, own, pooled_own, from_low, from_up):
    count, length, width = own.shape[1:]
    groups = width // LANES
    pooled = length // 4

    def pair_spec(rows):
        return pl.BlockSpec((1, count, rows, LANES), lambda j: (j // groups, 0, 0, j % groups))

    return pl.pallas_call(
        pool_back_kernel,
        grid=(2 * groups,),
        in_specs=[
            pl.BlockSpec(select.shape, lambda j: (0, 0)),
            pl.BlockSpec(select.shape[::-1], lambda j: (0, 0)),
            pl.BlockSpec((1, 8, LANES), lambda j: (j // groups, 0, j % groups)),
            pl.BlockSpec((count, length, LANES), lambda j: (0, 0, j + groups)),
            pl.BlockSpec((count, 16, LANES), lambda j: (0, WIN // 16 - 1, j)),
            pair_spec(length), pair_spec(pooled),
            pair_spec(from_low.shape[2]), pair_spec(from_up.shape[2]),
        ],
        out_specs=[
            pair_spec(length), pair_spec(16),
            pl.BlockSpec((1, 8, LANES), lambda j: (j // groups, 0, j % groups)),
        ],
        out_shape=[
            jax.ShapeDtypeStruct((2, count, length, width), f32),
            jax.ShapeDtypeStruct((2, count, 16, width), bf16),
            jax.ShapeDtypeStruct((2, 8, width), f32),
        ],
        compiler_params=pltpu.CompilerParams(vmem_limit_bytes=VMEM_LIMIT),
        cost_estimate=pl.CostEstimate(
            flops=count * length * width * 4000, bytes_accessed=9000000, transcendentals=0
        ),
        name="pool_back",
    )(select, select.T, kernel, qkv, rows_low, own, pooled_own, from_low, from_up)


def matmul(a, b):
    return jnp.dot(a, b, preferred_element_type=f32)


def matmul_t(a, b):
    return lax.dot_general(a, b, (((1,), (1,)), ((), ())), preferred_element_type=f32)


def weight_grad(a, b):
    return lax.dot_general(a, b, (((0,), (0,)), ((), ())), preferred_element_type=f32)


def normalised(rows):
    centre = rows - jnp.mean(rows, axis=-1, keepdims=True)
    inverse = lax.rsqrt(jnp.mean(centre * centre, axis=-1, keepdims=True) + norm_eps)
    return centre * inverse, inverse


def normalised_back(grads, gain, norm, inverse):
    scaled = grads * gain
    mean = jnp.mean(scaled, axis=-1, keepdims=True)
    inner = jnp.mean(scaled * norm, axis=-1, keepdims=True)
    return (scaled - mean - norm * inner) * inverse


def gelu_both(value):
    square = value * value
    inside = jnp.tanh(value * (gelu_coef + (gelu_coef * 0.044715) * square))
    half = 0.5 * value
    bend = gelu_coef + (3 * 0.044715 * gelu_coef) * square
    return half + half * inside, 0.5 + 0.5 * inside + half * (1.0 - inside * inside) * bend


def small_index():
    return flat_index().reshape(1).astype(jnp.int32)


def place_kernel(blocks, index_ref, mine_ref, other_ref, out_ref):
    half = len(blocks) // 2
    for place, bits in enumerate(blocks):
        source = mine_ref if place < half else other_ref
        out_ref[0, index_ref[0] ^ bits] = source[0, place % half]


def in_place(halves, block_cols, skip=0, take=None):
    blocks = relative_blocks()
    half = len(blocks) // 2
    all_parts, half_rows, cols = halves[0].shape
    parts = take or all_parts
    rows = half_rows // half
    spec = pl.BlockSpec((1, half, rows, block_cols), lambda p, j, index: (p + skip, 0, 0, j))
    whole = pl.pallas_call(
        functools.partial(place_kernel, blocks),
        grid_spec=pltpu.PrefetchScalarGridSpec(
            num_scalar_prefetch=1,
            grid=(parts, cols // block_cols),
            in_specs=[spec, spec],
            out_specs=pl.BlockSpec(
                (1, 2 * half, rows, block_cols), lambda p, j, index: (p, 0, 0, j)
            ),
        ),
        out_shape=jax.ShapeDtypeStruct((parts, 2 * half, rows, cols), halves[0].dtype),
        compiler_params=pltpu.CompilerParams(vmem_limit_bytes=VMEM_LIMIT),
        cost_estimate=pl.CostEstimate(
            flops=0, bytes_accessed=8 * parts * half_rows * cols, transcendentals=0
        ),
        name="in_place",
    )(small_index(), *[h.reshape(all_parts, half, rows, cols) for h in halves])
    return whole.reshape(parts * 2 * half_rows, cols)


def store_blocks(blocks, index, total_ref, keep_ref, give_ref):
    half = len(blocks) // 2
    rows = total_ref.shape[0] // len(blocks)
    for place, bits in enumerate(blocks):
        target = keep_ref if place < half else give_ref
        start = pl.multiple_of((index ^ bits) * rows, 8)
        target[0, place % half] = total_ref[pl.ds(start, rows), :].astype(bf16)


def weight_grads_kernel(blocks, plan, index_ref, *refs):
    operands, (keep_ref, give_ref, total_ref) = refs[:-3], refs[-3:]
    width = total_ref.shape[0]
    for step, (left, left_at, right, right_at) in enumerate(plan):

        @pl.when(pl.program_id(0) == step)
        def _():
            rows = operands[left][:, left_at * width : (left_at + 1) * width]
            grads = operands[right][:, right_at * width : (right_at + 1) * width]
            total_ref[...] = weight_grad(rows, grads)

    store_blocks(blocks, index_ref[0], total_ref, keep_ref, give_ref)


def turned(whole):
    bits = axis_bits()
    cols = whole.shape[1]
    split = whole.reshape((2,) * len(bits) + (-1, cols))
    for place, (axis, step) in enumerate(bits):
        mine = (lax.axis_index(axis) // step) % 2
        split = jnp.where(mine == 1, jnp.flip(split, place), split)
    order = [bits.index(bit) for bit in block_order()]
    split = split.transpose(*order, len(bits), len(bits) + 1)
    return split.reshape(1, 2, -1, cols)


def weight_grads(operands, plan, width, stacked=False):
    blocks = relative_blocks()
    half = len(blocks) // 2
    rows = width // len(blocks)
    count = len(plan)
    if rows % 8:
        pieces = []
        for left, left_at, right, right_at in plan:
            left_rows = operands[left][:, left_at * width : (left_at + 1) * width]
            grads = operands[right][:, right_at * width : (right_at + 1) * width]
            pieces.append(turned(weight_grad(left_rows, grads).astype(bf16)))
        joined = jnp.concatenate(pieces, axis=0 if stacked else 3)
        return joined[:, 0], joined[:, 1]
    if stacked:
        shape, spec = (count, half, rows, width), lambda j, index: (j, 0, 0, 0)
    else:
        shape, spec = (1, half, rows, count * width), lambda j, index: (0, 0, 0, j)
    out = jax.ShapeDtypeStruct(shape, bf16)
    spec = pl.BlockSpec((1, half, rows, width), spec)
    tokens = operands[0].shape[0]
    pair = pl.pallas_call(
        functools.partial(weight_grads_kernel, blocks, plan),
        grid_spec=pltpu.PrefetchScalarGridSpec(
            num_scalar_prefetch=1,
            grid=(count,),
            in_specs=[pl.BlockSpec(a.shape, lambda j, index: (0, 0)) for a in operands],
            out_specs=[spec, spec],
            scratch_shapes=[pltpu.VMEM((width, width), f32)],
        ),
        out_shape=[out, out],
        compiler_params=pltpu.CompilerParams(vmem_limit_bytes=VMEM_LIMIT),
        cost_estimate=pl.CostEstimate(
            flops=2 * tokens * width * width * count,
            bytes_accessed=2 * sum(a.size for a in operands) + 2 * count * width * width,
            transcendentals=0,
        ),
        name="weight_grads",
    )(small_index(), *operands)
    return [side.reshape(shape[0], half * rows, shape[3]) for side in pair]


ROWS = 128
EDGES = ("output_bias", "down_bias", "mixer_gain", "mixer_shift", "feed_gain", "feed_shift")


def by_rows(count, body, rows=ROWS):
    for first in range(0, count, rows):
        body(slice(first, first + rows))


def feed_kernel(x_ref, mixed_ref, vectors_ref, bias_ref, out_ref, up_ref, down_ref,
                norm_ref, inverse_ref, low_ref, act_ref, slope_ref, norm_two_ref, inverse_two_ref,
                y_ref, hidden_ref, total_ref):
    step, last = pl.program_id(0), pl.num_programs(0) - 1
    count = x_ref.shape[0]

    def vector(name):
        at = EDGES.index(name)
        return vectors_ref[at : at + 1, :]

    @pl.when(step == 0)
    def _():
        total_ref[...] = dot_nn(mixed_ref[...], out_ref[...])

        def body(at):
            norm, inverse = normalised(x_ref[at, :] + total_ref[at, :] + vector("output_bias"))
            hidden = norm * vector("mixer_gain") + vector("mixer_shift")
            norm_ref[at, :], inverse_ref[at, :] = norm, inverse
            hidden_ref[at, :] = hidden
            low_ref[at, :] = hidden.astype(bf16)
            total_ref[at, :] = jnp.zeros_like(hidden)

        by_rows(count, body)

    def units(at):
        act, slope = gelu_both(dot_nn(low_ref[at, :], up_ref[...]) + bias_ref[...])
        act = act.astype(bf16)
        act_ref[at, :], slope_ref[at, :] = act, slope.astype(bf16)
        total_ref[at, :] += dot_nn(act, down_ref[...])

    by_rows(count, units, 256)

    @pl.when(step == last)
    def _():
        def body(at):
            rows = hidden_ref[at, :] + total_ref[at, :] + vector("down_bias")
            norm, inverse = normalised(rows)
            norm_two_ref[at, :], inverse_two_ref[at, :] = norm, inverse
            y_ref[at, :] = norm * vector("feed_gain") + vector("feed_shift")

        by_rows(count, body)


def feed_forward(x, mixed, small, whole, ratio):
    count, width = x.shape
    rows = pl.BlockSpec((count, width), lambda j: (0, 0))
    line = pl.BlockSpec((count, 1), lambda j: (0, 0))
    part = pl.BlockSpec((count, width), lambda j: (0, j))

    def weight(shift, moves):
        return pl.BlockSpec((width, width), lambda j: (0, shift + moves * j))

    def shape(cols, kind):
        return jax.ShapeDtypeStruct((count, cols), kind)

    return pl.pallas_call(
        feed_kernel,
        grid=(ratio,),
        in_specs=[
            rows, rows, pl.BlockSpec((8, width), lambda j: (0, 0)),
            pl.BlockSpec((1, width), lambda j: (0, j)),
            weight(0, 0), weight(1, 1), weight(1 + ratio, 1),
        ],
        out_specs=[rows, line, rows, part, part, rows, line, rows],
        out_shape=[
            shape(width, f32), shape(1, f32), shape(width, bf16), shape(ratio * width, bf16),
            shape(ratio * width, bf16), shape(width, f32), shape(1, f32), shape(width, f32),
        ],
        scratch_shapes=[pltpu.VMEM((count, width), f32)] * 2,
        compiler_params=pltpu.CompilerParams(vmem_limit_bytes=VMEM_LIMIT),
        cost_estimate=pl.CostEstimate(
            flops=2 * count * width * width * (1 + 2 * ratio), transcendentals=count * width * ratio,
            bytes_accessed=2 * whole.size + 4 * count * width * ratio + 20 * count * width,
        ),
        name="feed_forward",
    )(x, mixed, small["vectors"], small["up_bias"], whole, whole, whole)


def feed_back_kernel(blocks, index_ref, grads_ref, norm_ref, inverse_ref, norm_two_ref,
                     inverse_two_ref, vectors_ref, low_ref, act_ref, slope_ref, out_ref, up_ref,
                     down_ref, one_ref, attention_ref, mixed_ref, sums_ref, bias_ref, *rest):
    outs, (feed_ref, hidden_ref, total_ref, pre_ref, turn_ref) = rest[:-5], rest[-5:]
    step, last = pl.program_id(0), pl.num_programs(0) - 1
    count, width = grads_ref.shape

    def vector(name):
        at = EDGES.index(name)
        return vectors_ref[at : at + 1, :]

    def add(name, rows):
        at = EDGES.index(name)
        sums_ref[at : at + 1, :] += jnp.sum(rows, axis=0, keepdims=True)

    def store(pair):
        if blocks is None:
            pair[0][0] = total_ref[...].astype(bf16)
        else:
            store_blocks(blocks, index_ref[0], total_ref, *pair)

    @pl.when(step == 0)
    def _():
        sums_ref[...] = jnp.zeros_like(sums_ref)
        turn_ref[...] = jnp.transpose(low_ref[...])

        def body(at):
            grads, norm = grads_ref[at, :], norm_two_ref[at, :]
            add("feed_gain", grads * norm)
            add("feed_shift", grads)
            back = normalised_back(grads, vector("feed_gain"), norm, inverse_two_ref[at, :])
            hidden_ref[at, :] = back
            back = back.astype(bf16)
            feed_ref[at, :] = back
            add("down_bias", back.astype(f32))

        by_rows(count, body)

    pre_ref[...] = (
        slope_ref[...].astype(f32) * dot_nt(feed_ref[...], down_ref[...])
    ).astype(bf16)
    bias_ref[...] = jnp.sum(pre_ref[...].astype(f32), axis=0, keepdims=True)
    hidden_ref[...] += dot_nt(pre_ref[...], up_ref[...])
    total_ref[...] = weight_grad(act_ref[...], feed_ref[...])
    store(outs[: len(outs) // 2])
    total_ref[...] = dot_nn(turn_ref[...], pre_ref[...])
    store(outs[len(outs) // 2 :])

    @pl.when(step == last)
    def _():
        def body(at):
            grads, norm = hidden_ref[at, :], norm_ref[at, :]
            add("mixer_gain", grads * norm)
            add("mixer_shift", grads)
            back = normalised_back(grads, vector("mixer_gain"), norm, inverse_ref[at, :])
            one_ref[at, :] = back
            back = back.astype(bf16)
            attention_ref[at, :] = back
            add("output_bias", back.astype(f32))

        by_rows(count, body)
        mixed_ref[...] = dot_nt(attention_ref[...], out_ref[...]).astype(bf16)


def feed_back(grads, kept, small, whole, ratio):
    norm, inverse, low, act, slope, norm_two, inverse_two = kept
    count, width = grads.shape
    blocks = relative_blocks()
    half = len(blocks) // 2
    shard = width // len(blocks)
    rows = pl.BlockSpec((count, width), lambda j, index: (0, 0))
    line = pl.BlockSpec((count, 1), lambda j, index: (0, 0))
    part = pl.BlockSpec((count, width), lambda j, index: (0, j))
    edge = pl.BlockSpec((8, width), lambda j, index: (0, 0))

    def weight(shift, moves):
        return pl.BlockSpec((width, width), lambda j, index: (0, shift + moves * j))

    if shard % 8:
        blocks = None
        out = [jax.ShapeDtypeStruct((ratio, width, width), bf16)] * 2
        specs = [pl.BlockSpec((1, width, width), lambda j, index: (j, 0, 0))] * 2
    else:
        block = (1, half, shard, width)
        out = [jax.ShapeDtypeStruct((ratio, half, shard, width), bf16)] * 2
        out += [jax.ShapeDtypeStruct((1, half, shard, ratio * width), bf16)] * 2
        specs = [pl.BlockSpec(block, lambda j, index: (j, 0, 0, 0))] * 2
        specs += [pl.BlockSpec(block, lambda j, index: (0, 0, 0, j))] * 2
    results = pl.pallas_call(
        functools.partial(feed_back_kernel, blocks),
        grid_spec=pltpu.PrefetchScalarGridSpec(
            num_scalar_prefetch=1,
            grid=(ratio,),
            in_specs=[
                rows, rows, line, rows, line, edge, rows, part, part,
                weight(0, 0), weight(1, 1), weight(1 + ratio, 1),
            ],
            out_specs=[
                rows, rows, rows, edge, pl.BlockSpec((1, width), lambda j, index: (0, j)), *specs
            ],
            scratch_shapes=[
                pltpu.VMEM((count, width), bf16), pltpu.VMEM((count, width), f32),
                pltpu.VMEM((width, width), f32), pltpu.VMEM((count, width), bf16),
                pltpu.VMEM((width, count), bf16),
            ],
        ),
        out_shape=[
            jax.ShapeDtypeStruct((count, width), f32), jax.ShapeDtypeStruct((count, width), bf16),
            jax.ShapeDtypeStruct((count, width), bf16), jax.ShapeDtypeStruct((8, width), f32),
            jax.ShapeDtypeStruct((1, ratio * width), f32), *out,
        ],
        compiler_params=pltpu.CompilerParams(vmem_limit_bytes=VMEM_LIMIT),
        cost_estimate=pl.CostEstimate(
            flops=2 * count * width * width * (1 + 4 * ratio), transcendentals=0,
            bytes_accessed=4 * whole.size + 4 * count * width * ratio + 20 * count * width,
        ),
        name="feed_back",
    )(small_index(), grads, norm, inverse, norm_two, inverse_two, small["vectors"], low, act, slope,
      whole, whole, whole)
    one, attention_low, grad_mixed, sums, up_sums, *out = results
    if blocks is None:
        down = [turned(out[0][i]) for i in range(ratio)]
        down = [jnp.concatenate([d[:, side] for d in down]) for side in range(2)]
        up = [turned(out[1][i]) for i in range(ratio)]
        up = [jnp.concatenate([u[:, side] for u in up], axis=2) for side in range(2)]
    else:
        down = [side.reshape(ratio, half * shard, width) for side in out[:2]]
        up = [side.reshape(1, half * shard, ratio * width) for side in out[2:]]
    return one, attention_low, grad_mixed, sums, up_sums, down, up


def units_back_kernel(spread_ref, *refs):
    parts, out_ref = refs[:-1], refs[-1]
    total = None
    for part, rows_ref in enumerate(parts):
        left = rows_ref[...]
        for _ in range(3):
            piece = left.astype(bf16)
            left = left - piece.astype(f32)
            term = dot_nn(piece, spread_ref[part])
            total = term if total is None else total + term
    out_ref[...] = total


def units_back(rows, ratio, shard_rows):
    count, cols = rows.shape
    block = cols // ratio // 2
    source = jnp.arange(block, dtype=jnp.int32)
    target = jnp.arange(ratio * block, dtype=jnp.int32)
    device, rest = target // (ratio * shard_rows), target % (ratio * shard_rows)
    wanted = device * shard_rows + rest % shard_rows
    spread = jnp.stack([
        (source[:, None] == wanted[None, :]) & (rest[None, :] // shard_rows == part)
        for part in range(ratio)
    ]).astype(bf16)
    return pl.pallas_call(
        units_back_kernel,
        grid=(2,),
        in_specs=[pl.BlockSpec(spread.shape, lambda j: (0, 0, 0))] + [
            pl.BlockSpec((count, block), functools.partial(lambda part, j: (0, 2 * part + j), part))
            for part in range(ratio)
        ],
        out_specs=pl.BlockSpec((count, ratio * block), lambda j: (0, j)),
        out_shape=jax.ShapeDtypeStruct((count, cols), f32),
        compiler_params=pltpu.CompilerParams(vmem_limit_bytes=VMEM_LIMIT),
        name="units_back",
    )(spread, *[rows] * ratio)


SMALL_COLUMNS = 128


def small_grads_kernel(blocks, layers, index_ref, *refs):
    sources, (keep_ref, give_ref, lines_ref, columns_ref) = refs[:-4], refs[-4:]
    lines_ref[...] = jnp.zeros_like(lines_ref)
    width = lines_ref.shape[1]
    each = len(sources) // layers
    at = 0
    for layer in range(layers):
        query_ref, value_ref, sums_ref, up_ref, taps_ref = sources[layer * each : (layer + 1) * each]
        lines_ref[at : at + 1, :] = query_ref[...]
        lines_ref[at + 1 : at + 2, :] = value_ref[...]
        lines_ref[at + 2 : at + 2 + len(EDGES), :] = sums_ref[: len(EDGES), :]
        at += 2 + len(EDGES)
        for kind in range(2):
            lines_ref[at : at + TAPS, :] = taps_ref[kind, :TAPS]
            at += TAPS
        for part in range(up_ref.shape[1] // width):
            lines_ref[at : at + 1, :] = up_ref[:, part * width : (part + 1) * width]
            at += 1
    columns_ref[...] = jnp.transpose(lines_ref[...])
    store_blocks(blocks, index_ref[0], columns_ref, keep_ref, give_ref)


def small_grads(per_layer, width):
    blocks = relative_blocks()
    half = len(blocks) // 2
    rows = width // len(blocks)
    if rows % 8:
        lines = []
        for query, value, sums, up, taps in per_layer:
            lines += [query, value, sums[: len(EDGES)], taps[0, :TAPS], taps[1, :TAPS]]
            lines.append(up.reshape(-1, width))
        lines = jnp.concatenate(lines, axis=0)
        lines = jnp.pad(lines, ((0, SMALL_COLUMNS - lines.shape[0]), (0, 0))).T.astype(bf16)
        lines = turned(lines)
        return lines[:, 0], lines[:, 1]
    flat = [a for arrays in per_layer for a in arrays]
    out = jax.ShapeDtypeStruct((1, half, rows, SMALL_COLUMNS), bf16)
    pair = pl.pallas_call(
        functools.partial(small_grads_kernel, blocks, len(per_layer)),
        in_specs=[pl.BlockSpec(memory_space=pltpu.SMEM)]
        + [pl.BlockSpec(memory_space=pltpu.VMEM)] * len(flat),
        out_specs=[pl.BlockSpec(memory_space=pltpu.VMEM)] * 2,
        out_shape=[out, out],
        scratch_shapes=[pltpu.VMEM((SMALL_COLUMNS, width), f32), pltpu.VMEM((width, SMALL_COLUMNS), f32)],
        compiler_params=pltpu.CompilerParams(vmem_limit_bytes=VMEM_LIMIT),
        name="small_grads",
    )(small_index(), *flat)
    return [side.reshape(1, half * rows, SMALL_COLUMNS) for side in pair]


def layer_forward(x, weights, masks, select, count, at):
    qkv_weight, feed_weights, small = weights
    width = x.shape[1]
    length = x.shape[0] // count
    x_low = x.astype(bf16)
    bias = jnp.concatenate([small["query_bias"], jnp.zeros((width,), f32), small["value_bias"]])
    qkv = matmul(x_low, qkv_weight)
    qkv = at("projected", (qkv + bias).astype(bf16).reshape(count, length, -1))
    rows_low = passed_along(qkv[:, length - WIN :, width:], 1)
    rows_up = passed_along(qkv[:, :WIN, width:], -1)
    rows_low, rows_up = tied([rows_low, rows_up])
    pooled = at("pooled", pool(select, small["taps"], qkv, rows_low, width))
    pooled_low, pooled_up = pooled_rims(pooled)
    pooled_up = at("attending", pooled_up)
    operands = attend_operands(qkv, rows_low, rows_up, pooled, pooled_low, pooled_up)
    mixed, stats = attend(masks, operands, width)
    mixed = at("attended", mixed.reshape(count * length, width))
    ratio = small["up_bias"].shape[1] // width
    norm, inverse, hidden_low, act_low, slope, norm_two, inverse_two, y = feed_forward(
        x, mixed, small, feed_weights, ratio
    )
    y = at("fed", y)
    kept = (x_low, operands, stats, mixed, (norm, inverse, hidden_low, act_low, slope, norm_two, inverse_two))
    return y, kept


def layer_backward(grads, kept, weights, masks, select, count, at):
    qkv_weight, feed_weights, small = weights
    x_low, operands, stats, mixed, feed_kept = kept
    rows, width = grads.shape
    length = rows // count
    ratio = small["up_bias"].shape[1] // width

    def total(value):
        return jnp.sum(value.astype(f32), axis=0, keepdims=True)

    grad_one, attention_low, grad_mixed, sums, up_sums, down_halves, up_halves = feed_back(
        grads, feed_kept, small, feed_weights, ratio
    )
    grad_mixed = at("attending", grad_mixed, (down_halves, up_halves))
    grad_mixed = grad_mixed.reshape(count, length, width)
    part = max(count // 2, 1)
    pieces = list(attend_back(masks, stats, grad_mixed, operands, 0, part))
    if part < count:
        pieces[0] = at("halfway", pieces[0])
        pieces = attend_back(masks, stats, grad_mixed, operands, part, count - part, pieces)
    grad_query, own, pooled_own, rim_low, rim_up = pieces
    rim_up = at("rims", rim_up)
    grad_query = grad_query.reshape(rows, width)
    from_low, from_up, pooled_own = rims_return(rim_low, rim_up, pooled_own)
    own, tail, taps = pool_back(
        select, small["taps"], operands[0], operands[3], own, pooled_own, from_low, from_up
    )
    tail = passed_along(tail, -1).astype(f32)
    own = at("pooled", own, (x_low, grad_query, mixed, attention_low))
    own = own + jnp.pad(tail, ((0, 0), (0, 0), (length - 16, 0), (0, 0)))
    own = own.astype(bf16).reshape(2, rows, width)
    grad_qkv = (grad_query, own[0], own[1])
    grad_x = grad_one + matmul_t(jnp.concatenate(grad_qkv, axis=1), qkv_weight)
    small_sums = [total(grad_query), total(own[1]), sums, up_sums, taps]
    return grad_x, (x_low, *grad_qkv, mixed, attention_low), small_sums


def pack_small(vectors, up_biases, taps):
    columns = []
    for layer in range(vectors[0].shape[0]):
        rows = vectors[0].shape[1]
        columns.append(jnp.stack([v[layer] for v in vectors]))
        columns.append(taps[0][layer])
        columns.append(taps[1][layer])
        columns.append(up_biases[layer].reshape(-1, rows))
    packed = jnp.concatenate(columns, axis=0)
    return jnp.pad(packed, ((0, SMALL_COLUMNS - packed.shape[0]), (0, 0))).T


def unpack_small(columns, layers, ratio):
    width = columns.shape[0]
    lines = columns.astype(f32).T
    per_layer = 8 + 2 * TAPS + ratio
    pad = ((0, 8 - TAPS), (0, 0))
    result = []
    for layer in range(layers):
        piece = lines[layer * per_layer : (layer + 1) * per_layer]
        result.append({
            "query_bias": piece[0],
            "value_bias": piece[1],
            "vectors": piece[2:10],
            "taps": jnp.stack([
                jnp.pad(piece[8 : 8 + TAPS], pad), jnp.pad(piece[8 + TAPS : 8 + 2 * TAPS], pad),
            ]),
            "up_bias": piece[8 + 2 * TAPS :].reshape(1, ratio * width),
        })
    return result


def on_device(
    tokens, cotangent, masked, query_weight, key_weight, value_weight, output_weight, up_weight,
    down_weight, query_bias, value_bias, output_bias, up_bias, down_bias, mixer_gain, mixer_shift,
    feed_gain, feed_shift, pool_key, pool_value,
):
    micro, seqs, length, width = tokens.shape
    count = micro * seqs
    layers = query_weight.shape[0]
    devices = lax.axis_size("seq") * lax.axis_size("batch")
    shard_rows = width // devices
    small_shard = pack_small(
        (query_bias, value_bias, output_bias, down_bias, mixer_gain, mixer_shift, feed_gain,
         feed_shift), up_bias, (pool_key, pool_value),
    )
    masks = window_masks(length)
    select = tap_select(length)
    ratio = up_weight.shape[2] // width

    def units_apart(rows):
        split = rows.reshape(rows.shape[0], devices, ratio, shard_rows)
        return split.transpose(0, 2, 1, 3).reshape(rows.shape)

    shard = jnp.concatenate(
        [query_weight[0], key_weight[0], value_weight[0], small_shard], axis=1
    )
    first = Gather(shard[None], path("y"))

    later = [
        Gather(jnp.concatenate(
            [query_weight[layer], key_weight[layer], value_weight[layer]], axis=1
        )[None], path("x"))
        for layer in range(1, layers)
    ]
    x = tokens.reshape(count * length, width).astype(f32)
    feeds = []

    def gather_feed(layer, after):
        out, up, down, after = tied(
            [output_weight[layer], up_weight[layer], down_weight[layer], after]
        )
        parts = down.reshape(ratio, shard_rows, width)
        shard = jnp.concatenate([out, units_apart(up), *parts], axis=1)
        feeds.append(lax.all_gather(shard, ("seq", "batch"), axis=0, tiled=True))
        return after

    x = checkpoint(x, [], [first])
    x = gather_feed(0, checkpoint(x, [first]))
    while first.left > 2:
        x = checkpoint(x, [first])
    for layer in range(1, layers):
        x = gather_feed(layer, x)
    x = checkpoint(x, [first])
    x = checkpoint(x, [first], later)
    first_whole = in_place(first.halves, first.cols)
    smalls = unpack_small(first_whole[:, 3 * width :], layers, ratio)

    def landed(value, flows, left):
        while True:
            behind = [flow for flow in flows if flow.left > left]
            if not behind:
                return value
            value = checkpoint(value, behind)

    def forward_at(layer):
        following = later[layer : layer + 1]

        def at(name, value):
            if name in ("projected", "pooled", "attended"):
                return checkpoint(value, following)
            if name == "fed":
                return landed(value, following, 0)
            return value

        return at

    states, weights = [], []
    for layer in range(layers):
        if layer == 0:
            qkv_weight = first_whole[:, : 3 * width]
        else:
            qkv_weight = in_place(later[layer - 1].halves, width)
        whole = (qkv_weight, feeds[layer], smalls[layer])
        x, kept = layer_forward(x, whole, masks, select, count, forward_at(layer))
        states.append(kept)
        weights.append(whole)
    layer_output = x.astype(bf16).reshape(tokens.shape)
    grads = cotangent.astype(f32) * masked.astype(f32)[..., None]
    grads = grads.reshape(count * length, width)
    flows = {}
    plans = {
        "down": ["rims", "next attending", "next halfway", "next rims", "never"],
        "up": ["rims", "next attending", "next halfway", "next rims", "never"],
        "in": ["next attending", "next rims", "never"],
        "query": ["never"],
    }
    last_plans = {
        "down": ["halfway", "rims", "never"],
        "up": ["halfway", "rims", "never"],
    }
    waiting = []

    def due(layer, name):
        result = []
        for (kind, owner), flow in flows.items():
            plan = last_plans[kind] if owner == 0 and kind in last_plans else plans[kind]
            when = plan[min(flow.stage, len(plan) - 1)]
            if flow.done or flow in waiting:
                continue
            if when == ("next " if owner > layer else "") + name or owner > layer + 1:
                result.append(flow)
        return result

    def backward_at(layer):
        def at(name, value, given=None):
            landing, begin = due(layer, name), []
            if name == "attending":
                for kind, halves, last in zip(("down", "up"), given, "yx"):
                    flows[kind, layer] = Scatter(halves, path(last)[::-1])
                    begin.append(flows[kind, layer])
            if name == "pooled" and layer == 0:
                plan = [(0, 0, 1, 0), (2, 0, 3, 0)]
                flow = Scatter(weight_grads(given, plan, width), path("z")[::-1])
                flows["query", layer] = flow
            if name in ("rims", "pooled"):
                waiting.extend(flow for flow in landing if len(flow.order) - flow.stage > 2)
            return checkpoint(value, landing, [] if name == "pooled" else begin, waiting)

        return at

    small_sums = [None] * layers
    for layer in reversed(range(layers)):
        grads, given, small_sums[layer] = layer_backward(
            grads, states[layer], weights[layer], masks, select, count, backward_at(layer)
        )
        if layer > 0:
            plan = [(0, 0, 1 + i, 0) for i in range(3)] + [(4, 0, 5, 0)]
            flow = Scatter(weight_grads(given, plan, width), path("z")[::-1])
            flows["in", layer] = flow
            grads = checkpoint(grads, due(layer, "end"), [flow] + waiting)
            waiting.clear()
    halves = weight_grads((given[0], *given[2:4]), [(0, 0, 1, 0), (0, 0, 2, 0)], width)
    sides = small_grads(small_sums, width)
    joined = [jnp.concatenate(parts, axis=2) for parts in zip(halves, sides)]
    last = Scatter(joined, path("x")[::-1])
    flows["last", 0] = last
    ends = [last, flows["query", 0]]
    marker = checkpoint(last.keep[:1, :1, :1], [], ends)
    marker = checkpoint(marker, ends, waiting)
    while True:
        ends = [flow for flow in ends if not flow.done]
        others = [flow for flow in flows.values() if not flow.done and flow not in ends]
        if not ends + others:
            break
        if ends:
            marker = checkpoint(marker, ends)
        if others:
            marker = checkpoint(marker, others)
    totals = []
    for layer in range(layers):
        if layer > 0:
            whole = flows["in", layer].total[0]
            parts = [whole[:, i * width : (i + 1) * width] for i in range(4)]
        else:
            whole = flows["query", 0].total[0]
            end = last.total[0]
            parts = [whole[:, :width], end[:, :width], end[:, width : 2 * width], whole[:, width:]]
        parts.append(flows["up", layer].total[0])
        parts.append(flows["down", layer].total.reshape(ratio * shard_rows, width))
        totals.append(parts)
    up_totals = units_back(
        jnp.concatenate([parts[4] for parts in totals]), ratio, shard_rows
    ).reshape(layers, shard_rows, ratio * width)
    input_grad = grads.astype(bf16).reshape(tokens.shape)
    lines = last.total[0, :, 2 * width :].T
    per_layer = 8 + 2 * TAPS + ratio
    lines = lines[: layers * per_layer].reshape(layers, per_layer, shard_rows)
    vectors = [lines[:, i] for i in range(8)]
    after = 8 + 2 * TAPS
    grad_up_bias = lines[:, after:].reshape(layers, -1)
    return (
        layer_output, input_grad,
        *[jnp.stack([t[i] for t in totals]) if i != 4 else up_totals for i in range(6)],
        vectors[0], vectors[1], vectors[2], grad_up_bias, *vectors[3:],
        lines[:, 8 : 8 + TAPS], lines[:, 8 + TAPS : after],
    )


def solution(mesh):
    rows = P(None, "batch", "seq", None)
    matrix = P(None, ("seq", "batch"), None)
    vector = P(None, ("seq", "batch"))
    taps = P(None, None, ("seq", "batch"))
    params = (matrix,) * 6 + (vector,) * 9 + (taps,) * 2
    return jax.shard_map(
        on_device,
        mesh=mesh,
        in_specs=(rows, rows, P(None, "batch", "seq")) + params,
        out_specs=(rows, rows) + params,
        check_vma=False,
    )
```

```python
import functools

import jax
import jax.numpy as jnp
from jax import lax
from jax.experimental import pallas as pl
from jax.experimental.pallas import tpu as pltpu
from jax.sharding import PartitionSpec as P

HEADS = 12
WIN = 64
PWIN = 256
TAPS = 5
REACH = PWIN // 4
QROWS = 128
norm_eps = 1e-05
gelu_coef = 0.7978845608028654
masked_score = -1e30
f32 = jnp.float32
bf16 = jnp.bfloat16
VMEM_LIMIT = 48 * 1024 * 1024


def axis_bits():
    bits = []
    for axis in ("seq", "batch"):
        step = lax.axis_size(axis) // 2
        while step:
            bits.append((axis, step))
            step //= 2
    return bits


def path(name):
    bits = axis_bits()
    core, row = ("seq", 1), ("seq", 2)
    column = [bit for bit in bits if bit[0] == "seq" and bit[1] > 2]
    across = [bit for bit in bits if bit[0] == "batch"]
    order = {
        "y": column + across + [row],
        "x": column + [row] + across,
        "z": column[:-1] + across + [row] + column[-1:],
        "w": [row] + column + across,
    }[name]
    return order + [core]


def exchange(value, axis, step):
    pairs = [(i, i ^ step) for i in range(lax.axis_size(axis))]
    return lax.ppermute(value, axis, pairs)


def block_order():
    bits = axis_bits()
    return [("seq", 1), ("seq", 2)] + [b for b in bits if b[0] == "batch"] + [
        b for b in bits if b[0] == "seq" and b[1] > 2
    ]


def flat_index():
    return lax.axis_index("seq") * lax.axis_size("batch") + lax.axis_index("batch")


def relative_blocks():
    spread = []
    for axis, step in block_order():
        spread.append(step * lax.axis_size("batch") if axis == "seq" else step)
    count = len(spread)
    return [
        sum(spread[k] for k in range(count) if place >> (count - 1 - k) & 1)
        for place in range(2**count)
    ]


def tied(values):
    return list(lax.optimization_barrier(tuple(values)))


class Gather:
    def __init__(self, shard, order):
        self.current, self.order = shard, order
        self.have, self.halves, self.flying = [], None, None
        self.parts, self.rows, self.cols = shard.shape

    def ready(self):
        return self.current

    def hold(self, value):
        self.current = value

    def launch(self):
        self.flying = exchange(self.current, *self.order[len(self.have)])

    def land(self):
        stage = self.order[len(self.have)]
        if stage == self.order[-1]:
            self.halves = (self.current, self.flying)
            return
        significance = block_order()
        place = significance.index(stage)
        before = sum(1 for p in self.have if p < place)
        split = (self.parts * 2**before, 1, 2 ** (len(self.have) - before) * self.rows, self.cols)
        self.have.append(place)
        joined = jnp.concatenate([self.current.reshape(split), self.flying.reshape(split)], axis=1)
        self.current = joined.reshape(self.parts, 2 ** len(self.have) * self.rows, self.cols)

    @property
    def left(self):
        return 0 if self.halves is not None else len(self.order) - len(self.have)

    @property
    def done(self):
        return self.halves is not None


class Scatter:
    def __init__(self, halves, order):
        self.keep, self.give = halves
        self.order, self.stage, self.total, self.flying = order, 0, None, None
        self.have = list(range(1, len(order)))
        self.parts, half_rows, self.cols = self.keep.shape
        self.rows = half_rows // 2 ** len(self.have)

    def ready(self):
        return self.give

    def hold(self, value):
        self.give = value

    def launch(self):
        self.flying = exchange(self.give, *self.order[self.stage])

    def land(self):
        self.stage += 1
        if self.stage == len(self.order):
            total = self.keep.astype(f32) + self.flying.astype(f32)
            self.total = total.reshape(self.parts, self.rows, self.cols)
            return
        place = self.have.index(block_order().index(self.order[self.stage]))
        self.have.pop(place)
        left = 2 ** len(self.have) * self.rows
        split = (self.parts * 2**place, 2, left >> place, self.cols)
        keep, got = self.keep.reshape(split), self.flying.reshape(split)
        self.keep, self.give = [
            (keep[:, side].astype(f32) + got[:, side].astype(f32)).astype(bf16).reshape(
                self.parts, left, self.cols
            ) for side in range(2)
        ]

    @property
    def done(self):
        return self.total is not None


def checkpoint(value, flows, begin=(), waiting=()):
    value, *flying = tied([value] + [flow.flying for flow in flows])
    for flow, arrived in zip(flows, flying):
        flow.flying = arrived
        flow.land()
    going = [flow for flow in flows if not flow.done and flow not in waiting] + list(begin)
    value, *ready = tied([value] + [flow.ready() for flow in going])
    for flow, part in zip(going, ready):
        flow.hold(part)
        flow.launch()
    return value


def passed_along(value, steps):
    count = lax.axis_size("seq")
    pairs = [(i, i + steps) for i in range(count) if 0 <= i + steps < count]
    return lax.ppermute(value, "seq", pairs)


def pooled_hops(size):
    return -(-REACH // size)


def pooled_rims(pooled):
    size = pooled.shape[1]
    hops = range(1, pooled_hops(size) + 1)
    low = [passed_along(pooled, hop) for hop in reversed(hops)]
    up = [passed_along(pooled, -hop) for hop in hops]
    low = low[0] if len(low) == 1 else jnp.concatenate(low, axis=1)
    up = up[0] if len(up) == 1 else jnp.concatenate(up, axis=1)
    return low[:, low.shape[1] - REACH :], up[:, :REACH]


def rims_return(rim_low, rim_up, pooled_own):
    size = pooled_own.shape[2]
    hops = pooled_hops(size)
    if hops == 1:
        second = passed_along(rim_low[:, :, WIN : WIN + 16], -2)
        return tied([passed_along(rim_up, 1), passed_along(rim_low, -1), second]) + [pooled_own]
    far_low, far_up = rim_low[:, :, WIN : WIN + REACH], rim_up[:, :, WIN:]
    for hop in range(2, hops + 1):
        start = REACH - hop * size
        pooled_own = pooled_own + passed_along(far_low[:, :, start : start + size], -hop).astype(f32)
        start = (hop - 1) * size
        pooled_own = pooled_own + passed_along(far_up[:, :, start : start + size], hop).astype(f32)
    near_low, near_up = rim_low[:, :, :WIN], rim_up[:, :, :WIN]
    rim_low = jnp.concatenate([near_low, far_low[:, :, REACH - size :]], axis=2)
    rim_up = jnp.concatenate([near_up, far_up[:, :, :size]], axis=2)
    return passed_along(rim_up, 1), passed_along(rim_low, -1), None, pooled_own


def dot_nt(a, b):
    return lax.dot_general(a, b, (((1,), (1,)), ((), ())), preferred_element_type=f32)


def dot_nn(a, b):
    return lax.dot_general(a, b, (((1,), (0,)), ((), ())), preferred_element_type=f32)


def flipped(block):
    return jnp.transpose(block.astype(f32)).astype(bf16)


def two_heads(rows):
    lane = lax.broadcasted_iota(jnp.int32, rows.shape, 1)
    none = jnp.zeros_like(rows)
    half = rows.shape[1] // 2
    return jnp.concatenate(
        [jnp.where(lane < half, rows, none), jnp.where(lane < half, none, rows)], axis=0
    )


def heads_apart(block):
    half, queries = block.shape[0] // 2, block.shape[1] // 2
    return jnp.transpose(
        jnp.concatenate([block[:half, :queries], block[half:, queries:]], axis=0)
    )


def attend_kernel(near_ref, far_ref, q_ref, k_ref, v_ref, kl_ref, vl_ref, ku_ref, vu_ref,
                  pk_ref, pv_ref, pkl_ref, pvl_ref, pku_ref, pvu_ref, mixed_ref, stat_ref):
    blocks = q_ref.shape[1] // QROWS
    pairs = q_ref.shape[2] // 128
    for pair in range(pairs):
        at = slice(128 * pair, 128 * pair + 128)
        keys = jnp.concatenate([kl_ref[0, :, at], k_ref[0, :, at], ku_ref[0, :, at]], axis=0)
        values = jnp.concatenate([vl_ref[0, :, at], v_ref[0, :, at], vu_ref[0, :, at]], axis=0)
        far_keys = jnp.concatenate([pkl_ref[0, :, at], pk_ref[0, :, at], pku_ref[0, :, at]], axis=0)
        far_values = jnp.concatenate(
            [pvl_ref[0, :, at], pv_ref[0, :, at], pvu_ref[0, :, at]], axis=0
        )
        values_t, far_values_t = flipped(values), flipped(far_values)
        for block in range(blocks):
            first = QROWS * block
            query = two_heads(q_ref[0, first : first + QROWS, at] * 0.125)
            stop = first + QROWS + 2 * WIN
            score = dot_nt(keys[first:stop], query) + near_ref[block]
            top = jnp.max(score, axis=0, keepdims=True)
            prob = jnp.exp(score - top)
            total = jnp.sum(prob, axis=0, keepdims=True)
            near_low = (prob * (1.0 / total)).astype(bf16)
            row = (pair * blocks + block) * 2
            stat_ref[0, 0, row : row + 1, :] = top + jnp.log(total)
            score = dot_nt(far_keys, query) + far_ref[block]
            top = jnp.max(score, axis=0, keepdims=True)
            prob = jnp.exp(score - top)
            total = jnp.sum(prob, axis=0, keepdims=True)
            far_low = (prob * (1.0 / total)).astype(bf16)
            stat_ref[0, 0, row + 1 : row + 2, :] = top + jnp.log(total)
            mixed = dot_nn(values_t[:, first:stop], near_low) + dot_nn(far_values_t, far_low)
            mixed_ref[0, first : first + QROWS, at] = heads_apart(mixed).astype(bf16)


def attend_back_kernel(near_ref, far_ref, stat_ref, g_ref, q_ref, k_ref, v_ref, kl_ref, vl_ref,
                       ku_ref, vu_ref, pk_ref, pv_ref, pkl_ref, pvl_ref, pku_ref, pvu_ref,
                       dq_ref, own_ref, pool_ref, low_ref, up_ref):
    blocks = q_ref.shape[1] // QROWS
    pairs = q_ref.shape[2] // 128
    length = q_ref.shape[1]
    for pair in range(pairs):
        at = slice(128 * pair, 128 * pair + 128)
        keys = jnp.concatenate([kl_ref[0, :, at], k_ref[0, :, at], ku_ref[0, :, at]], axis=0)
        values = jnp.concatenate([vl_ref[0, :, at], v_ref[0, :, at], vu_ref[0, :, at]], axis=0)
        far_keys = jnp.concatenate([pkl_ref[0, :, at], pk_ref[0, :, at], pku_ref[0, :, at]], axis=0)
        far_values = jnp.concatenate(
            [pvl_ref[0, :, at], pv_ref[0, :, at], pvu_ref[0, :, at]], axis=0
        )
        keys_t, far_keys_t = flipped(keys), flipped(far_keys)
        near_parts = ([], [])
        far_totals = [None, None]
        for block in range(blocks):
            first = QROWS * block
            query = two_heads(q_ref[0, first : first + QROWS, at] * 0.125)
            grads = two_heads(g_ref[0, first : first + QROWS, at])
            stop = first + QROWS + 2 * WIN
            row = (pair * blocks + block) * 2
            prob = jnp.exp(
                dot_nt(keys[first:stop], query) + near_ref[block] - stat_ref[0, 0, row : row + 1, :]
            )
            grad_prob = dot_nt(values[first:stop], grads)
            inner = jnp.sum(prob * grad_prob, axis=0, keepdims=True)
            grad_score = (prob * (grad_prob - inner)).astype(bf16)
            near_parts[0].append(dot_nn(grad_score, query))
            near_parts[1].append(dot_nn(prob.astype(bf16), grads))
            grad_query = dot_nn(keys_t[:, first:stop], grad_score)
            prob = jnp.exp(
                dot_nt(far_keys, query) + far_ref[block] - stat_ref[0, 0, row + 1 : row + 2, :]
            )
            grad_prob = dot_nt(far_values, grads)
            inner = jnp.sum(prob * grad_prob, axis=0, keepdims=True)
            grad_score = (prob * (grad_prob - inner)).astype(bf16)
            parts = (dot_nn(grad_score, query), dot_nn(prob.astype(bf16), grads))
            grad_query = grad_query + dot_nn(far_keys_t, grad_score)
            dq_ref[0, first : first + QROWS, at] = (heads_apart(grad_query) * 0.125).astype(bf16)
            for kind in range(2):
                far_totals[kind] = parts[kind] if block == 0 else far_totals[kind] + parts[kind]
        for kind in range(2):
            rows = []
            for chunk in range(blocks + 1):
                terms = []
                if chunk < blocks:
                    terms.append(near_parts[kind][chunk][:QROWS])
                if chunk > 0:
                    terms.append(near_parts[kind][chunk - 1][QROWS:])
                rows.append(functools.reduce(jnp.add, terms))
            rows = jnp.concatenate(rows, axis=0)
            own_ref[kind, 0, :, at] = rows[WIN : WIN + length]
            low_ref[kind, 0, :WIN, at] = rows[:WIN].astype(bf16)
            up_ref[kind, 0, :WIN, at] = rows[WIN + length :].astype(bf16)
            far = far_totals[kind]
            pool_ref[kind, 0, :, at] = far[REACH : far.shape[0] - REACH]
            low_ref[kind, 0, WIN : WIN + REACH, at] = far[:REACH].astype(bf16)
            low_ref[kind, 0, WIN + REACH :, at] = far[REACH : REACH + 16].astype(bf16)
            up_ref[kind, 0, WIN:, at] = far[far.shape[0] - REACH :].astype(bf16)


LANES = 256


def attend_specs(length, width):
    groups = width // LANES
    pooled = length // 4

    def spec(rows, shift):
        return pl.BlockSpec((1, rows, LANES), lambda g, j: (g, 0, j + shift))

    def whole(count, rows):
        return pl.BlockSpec((count, rows, 2 * QROWS), lambda g, j: (0, 0, 0))

    blocks = length // QROWS
    masks = [whole(blocks, QROWS + 2 * WIN), whole(blocks, pooled + 2 * REACH)]
    stat_rows = LANES // 128 * blocks * 2
    stat = pl.BlockSpec((1, 1, stat_rows, 2 * QROWS), lambda g, j: (g, j, 0, 0))
    operands = [spec(length, 0), spec(length, groups), spec(length, 2 * groups)]
    operands += [spec(WIN, 0), spec(WIN, groups)] * 2
    operands += [spec(pooled, 0), spec(pooled, groups)]
    operands += [spec(REACH, 0), spec(REACH, groups)] * 2
    return groups, masks, stat, stat_rows, operands, spec


def attend_operands(qkv, rows_low, rows_up, pooled, pooled_low, pooled_up):
    return (
        qkv, qkv, qkv, rows_low, rows_low, rows_up, rows_up,
        pooled, pooled, pooled_low, pooled_low, pooled_up, pooled_up,
    )


def attend(masks, operands, width):
    qkv = operands[0]
    count, length = qkv.shape[:2]
    groups, mask_specs, stat, stat_rows, specs, spec = attend_specs(length, width)
    return pl.pallas_call(
        attend_kernel,
        grid=(count, groups),
        in_specs=mask_specs + specs,
        out_specs=[spec(length, 0), stat],
        out_shape=[
            jax.ShapeDtypeStruct((count, length, width), bf16),
            jax.ShapeDtypeStruct((count, groups, stat_rows, 2 * QROWS), f32),
        ],
        compiler_params=pltpu.CompilerParams(vmem_limit_bytes=VMEM_LIMIT),
        cost_estimate=pl.CostEstimate(
            flops=count * length * width * 2000, bytes_accessed=8000000, transcendentals=3000000
        ),
        name="attend",
    )(*masks, *operands)


def attend_back(masks, stats, grad_mixed, operands, first, count, before=None):
    every, length, width = grad_mixed.shape
    groups, mask_specs, stat, stat_rows, specs, spec = attend_specs(length, width)
    pooled = length // 4

    def pair_spec(rows):
        return pl.BlockSpec((2, 1, rows, LANES), lambda g, j: (0, g, 0, j))

    def moved(block):
        index_map = block.index_map
        return pl.BlockSpec(block.block_shape, lambda g, j: index_map(g + first, j))

    in_specs = [stat, spec(length, 0)] + specs
    out_specs = [
        spec(length, 0), pair_spec(length), pair_spec(pooled),
        pair_spec(WIN + REACH + 16), pair_spec(WIN + REACH),
    ]
    out_specs = [moved(block) for block in out_specs[:1]] + [
        pl.BlockSpec(
            block.block_shape, functools.partial(lambda g, j: (0, g + first, 0, j))
        ) for block in out_specs[1:]
    ]
    before = before or []
    kernel_inputs = len(mask_specs) + len(in_specs)

    def kernel(*refs):
        attend_back_kernel(*refs[:kernel_inputs], *refs[kernel_inputs + len(before) :])

    return pl.pallas_call(
        kernel,
        grid=(count, groups),
        in_specs=mask_specs + [moved(block) for block in in_specs]
        + [pl.BlockSpec(memory_space=pl.ANY)] * len(before),
        out_specs=out_specs,
        out_shape=[
            jax.ShapeDtypeStruct((every, length, width), bf16),
            jax.ShapeDtypeStruct((2, every, length, width), f32),
            jax.ShapeDtypeStruct((2, every, pooled, width), f32),
            jax.ShapeDtypeStruct((2, every, WIN + REACH + 16, width), bf16),
            jax.ShapeDtypeStruct((2, every, WIN + REACH, width), bf16),
        ],
        input_output_aliases={kernel_inputs + i: i for i in range(len(before))},
        compiler_params=pltpu.CompilerParams(vmem_limit_bytes=VMEM_LIMIT),
        cost_estimate=pl.CostEstimate(
            flops=count * length * width * 5000, bytes_accessed=6000000 * count,
            transcendentals=1500000 * count,
        ),
        name="attend_back",
    )(*masks, stats, grad_mixed, *operands, *before)


def window_masks(length):
    blocks = length // QROWS
    index, devices = lax.axis_index("seq"), lax.axis_size("seq")

    def bias(width, offset, scale, reach):
        key = lax.broadcasted_iota(jnp.int32, (blocks, width, QROWS), 1)
        query = lax.broadcasted_iota(jnp.int32, (blocks, width, QROWS), 2)
        block = lax.broadcasted_iota(jnp.int32, (blocks, width, QROWS), 0)
        key = key - offset + (block * QROWS if scale == 1 else 0)
        query = query + block * QROWS
        size = length // scale
        allowed = jnp.abs(query - scale * key) <= reach
        place = key + index * size
        allowed &= (place >= 0) & (place < size * devices)
        one = jnp.where(allowed, 0.0, masked_score).astype(f32)
        return jnp.concatenate([one, one], axis=2)

    return bias(QROWS + 2 * WIN, WIN, 1, WIN), bias(length // 4 + 2 * REACH, REACH, 4, PWIN)


def tap_select(length):
    pooled = length // 4
    row = jnp.arange(TAPS * pooled, dtype=jnp.int32)
    column = jnp.arange(length, dtype=jnp.int32)
    source = 4 * (row % pooled) + row // pooled - 2
    return (source[:, None] == column[None, :]).astype(bf16)


def pool_kernel(select_ref, kernel_ref, rows_ref, low_ref, pooled_ref):
    pooled = pooled_ref.shape[1]
    for group in range(rows_ref.shape[0]):
        taps = dot_nn(select_ref[...], rows_ref[group])
        total = kernel_ref[0, 0:1, :] * taps[:pooled]
        for tap in range(1, TAPS):
            total = total + kernel_ref[0, tap : tap + 1, :] * taps[tap * pooled : (tap + 1) * pooled]
        low = low_ref[group].astype(f32)
        edge = kernel_ref[0, 0:1, :] * low[14:15] + kernel_ref[0, 1:2, :] * low[15:16]
        row = lax.broadcasted_iota(jnp.int32, total.shape, 0)
        pooled_ref[group] = (total + jnp.where(row == 0, edge, 0.0)).astype(bf16)


def pool(select, kernel, qkv, rows_low, width):
    count, length = qkv.shape[:2]
    groups = width // LANES
    return pl.pallas_call(
        pool_kernel,
        grid=(2 * groups,),
        in_specs=[
            pl.BlockSpec(select.shape, lambda j: (0, 0)),
            pl.BlockSpec((1, 8, LANES), lambda j: (j // groups, 0, j % groups)),
            pl.BlockSpec((count, length, LANES), lambda j: (0, 0, j + groups)),
            pl.BlockSpec((count, 16, LANES), lambda j: (0, WIN // 16 - 1, j)),
        ],
        out_specs=pl.BlockSpec((count, length // 4, LANES), lambda j: (0, 0, j)),
        out_shape=jax.ShapeDtypeStruct((count, length // 4, 2 * width), bf16),
        compiler_params=pltpu.CompilerParams(vmem_limit_bytes=VMEM_LIMIT),
        cost_estimate=pl.CostEstimate(
            flops=count * length * width * 1300, bytes_accessed=2500000, transcendentals=0
        ),
        name="pool",
    )(select, kernel, qkv, rows_low)


def pool_back_kernel(select_ref, spread_ref, kernel_ref, rows_ref, low_rows_ref, own_ref, pool_ref,
                     low_ref, up_ref, *rest):
    *rims, grad_ref, tail_ref, taps_ref = rest if len(rest) == 3 else (*rest[:3], None, rest[3])
    pooled = pool_ref.shape[2]
    length = rows_ref.shape[1]
    tap_row = lax.broadcasted_iota(jnp.int32, (8, LANES), 0)
    tail_row = lax.broadcasted_iota(jnp.int32, (16, LANES), 0)
    taps_total = jnp.zeros((8, LANES), f32)
    for group in range(rows_ref.shape[0]):
        grads = pool_ref[0, group] + low_ref[0, group, WIN : WIN + pooled].astype(f32)
        grads = (grads + up_ref[0, group, WIN : WIN + pooled].astype(f32)).astype(bf16).astype(f32)
        taps = dot_nn(select_ref[...], rows_ref[group])
        low_rows = low_rows_ref[group].astype(f32)
        edge = grads[0:1]
        spread = []
        for tap in range(TAPS):
            line = jnp.sum(grads * taps[tap * pooled : (tap + 1) * pooled], axis=0, keepdims=True)
            if tap < 2:
                line = line + edge * low_rows[14 + tap : 15 + tap]
            taps_total = taps_total + jnp.where(tap_row == tap, line, 0.0)
            spread.append(grads * kernel_ref[0, tap : tap + 1, :])
        spread = jnp.concatenate(spread, axis=0)
        high = spread.astype(bf16)
        rest = (spread - high.astype(f32)).astype(bf16)
        total = own_ref[0, group] + dot_nn(spread_ref[...], high) + dot_nn(spread_ref[...], rest)
        first, last = kernel_ref[0, 0:1, :], kernel_ref[0, 1:2, :]
        if rims:
            mine_ref, second_ref = rims
            edge = up_ref[0, group, WIN + pooled : WIN + pooled + 1].astype(f32)
            edge = edge + mine_ref[0, group, 0:1].astype(f32) + second_ref[0, group, 0:1].astype(f32)
            edge = edge.astype(bf16).astype(f32)
        tail = jnp.where(tail_row == 14, edge * first, 0.0)
        tail = tail + jnp.where(tail_row == 15, edge * last, 0.0)
        kind = grad_ref.dtype
        upper = total[length - WIN :] + up_ref[0, group, :WIN].astype(f32)
        if length > 2 * WIN:
            grad_ref[0, group, WIN : length - WIN] = total[WIN : length - WIN].astype(kind)
        grad_ref[0, group, :WIN] = (total[:WIN] + low_ref[0, group, :WIN].astype(f32)).astype(kind)
        if rims:
            grad_ref[0, group, length - WIN : length - 16] = upper[: WIN - 16].astype(kind)
            grad_ref[0, group, length - 16 :] = (upper[WIN - 16 :] + tail).astype(kind)
        else:
            grad_ref[0, group, length - WIN :] = upper.astype(kind)
            tail_ref[0, group] = tail.astype(bf16)
    taps_ref[0] = taps_total


def pool_back(select, kernel, qkv, rows_low, own, pooled_own, from_low, from_up, rim_up, second):
    count, length, width = own.shape[1:]
    groups = width // LANES
    pooled = length // 4

    def pair_spec(rows):
        return pl.BlockSpec((1, count, rows, LANES), lambda j: (j // groups, 0, 0, j % groups))

    joined = second is not None
    tail_shape = jax.ShapeDtypeStruct((2, count, 16, width), bf16)
    tail_specs, tail_shapes = ([], []) if joined else ([pair_spec(16)], [tail_shape])
    rim_spec = pl.BlockSpec(
        (1, count, 16, LANES), lambda j: (j // groups, 0, WIN // 16, j % groups)
    )
    extra_specs, extra = ([rim_spec, pair_spec(16)], [rim_up, second]) if joined else ([], [])
    return pl.pallas_call(
        pool_back_kernel,
        grid=(2 * groups,),
        in_specs=[
            pl.BlockSpec(select.shape, lambda j: (0, 0)),
            pl.BlockSpec(select.shape[::-1], lambda j: (0, 0)),
            pl.BlockSpec((1, 8, LANES), lambda j: (j // groups, 0, j % groups)),
            pl.BlockSpec((count, length, LANES), lambda j: (0, 0, j + groups)),
            pl.BlockSpec((count, 16, LANES), lambda j: (0, WIN // 16 - 1, j)),
            pair_spec(length), pair_spec(pooled),
            pair_spec(from_low.shape[2]), pair_spec(from_up.shape[2]),
        ] + extra_specs,
        out_specs=[pair_spec(length)] + tail_specs + [
            pl.BlockSpec((1, 8, LANES), lambda j: (j // groups, 0, j % groups)),
        ],
        out_shape=[
            jax.ShapeDtypeStruct((2, count, length, width), bf16 if joined else f32),
            *tail_shapes,
            jax.ShapeDtypeStruct((2, 8, width), f32),
        ],
        compiler_params=pltpu.CompilerParams(vmem_limit_bytes=VMEM_LIMIT),
        cost_estimate=pl.CostEstimate(
            flops=count * length * width * 4000, bytes_accessed=9000000, transcendentals=0
        ),
        name="pool_back",
    )(select, select.T, kernel, qkv, rows_low, own, pooled_own, from_low, from_up, *extra)


def matmul(a, b):
    return jnp.dot(a, b, preferred_element_type=f32)


def matmul_t(a, b):
    return lax.dot_general(a, b, (((1,), (1,)), ((), ())), preferred_element_type=f32)


def weight_grad(a, b):
    return lax.dot_general(a, b, (((0,), (0,)), ((), ())), preferred_element_type=f32)


def normalised(rows):
    centre = rows - jnp.mean(rows, axis=-1, keepdims=True)
    inverse = lax.rsqrt(jnp.mean(centre * centre, axis=-1, keepdims=True) + norm_eps)
    return centre * inverse, inverse


def normalised_back(grads, gain, norm, inverse):
    scaled = grads * gain
    mean = jnp.mean(scaled, axis=-1, keepdims=True)
    inner = jnp.mean(scaled * norm, axis=-1, keepdims=True)
    return (scaled - mean - norm * inner) * inverse


def gelu_both(value):
    square = value * value
    inside = jnp.tanh(value * (gelu_coef + (gelu_coef * 0.044715) * square))
    half = 0.5 * value
    bend = gelu_coef + (3 * 0.044715 * gelu_coef) * square
    return half + half * inside, 0.5 + 0.5 * inside + half * (1.0 - inside * inside) * bend


def small_index():
    return flat_index().reshape(1).astype(jnp.int32)


def place_kernel(blocks, index_ref, mine_ref, other_ref, out_ref):
    half = len(blocks) // 2
    for place, bits in enumerate(blocks):
        source = mine_ref if place < half else other_ref
        out_ref[0, index_ref[0] ^ bits] = source[0, place % half]


def in_place(halves, block_cols, skip=0, take=None):
    blocks = relative_blocks()
    half = len(blocks) // 2
    all_parts, half_rows, cols = halves[0].shape
    parts = take or all_parts
    rows = half_rows // half
    spec = pl.BlockSpec((1, half, rows, block_cols), lambda p, j, index: (p + skip, 0, 0, j))
    whole = pl.pallas_call(
        functools.partial(place_kernel, blocks),
        grid_spec=pltpu.PrefetchScalarGridSpec(
            num_scalar_prefetch=1,
            grid=(parts, cols // block_cols),
            in_specs=[spec, spec],
            out_specs=pl.BlockSpec(
                (1, 2 * half, rows, block_cols), lambda p, j, index: (p, 0, 0, j)
            ),
        ),
        out_shape=jax.ShapeDtypeStruct((parts, 2 * half, rows, cols), halves[0].dtype),
        compiler_params=pltpu.CompilerParams(vmem_limit_bytes=VMEM_LIMIT),
        cost_estimate=pl.CostEstimate(
            flops=0, bytes_accessed=8 * parts * half_rows * cols, transcendentals=0
        ),
        name="in_place",
    )(small_index(), *[h.reshape(all_parts, half, rows, cols) for h in halves])
    return whole.reshape(parts * 2 * half_rows, cols)


def store_blocks(blocks, index, total_ref, keep_ref, give_ref):
    half = len(blocks) // 2
    rows = total_ref.shape[0] // len(blocks)
    for place, bits in enumerate(blocks):
        target = keep_ref if place < half else give_ref
        start = pl.multiple_of((index ^ bits) * rows, 8)
        target[0, place % half] = total_ref[pl.ds(start, rows), :].astype(bf16)


def weight_grads_kernel(blocks, plan, index_ref, *refs):
    operands, (keep_ref, give_ref, total_ref) = refs[:-3], refs[-3:]
    width = total_ref.shape[0]
    for step, (left, left_at, right, right_at) in enumerate(plan):

        @pl.when(pl.program_id(0) == step)
        def _():
            rows = operands[left][:, left_at * width : (left_at + 1) * width]
            grads = operands[right][:, right_at * width : (right_at + 1) * width]
            total_ref[...] = weight_grad(rows, grads)

    store_blocks(blocks, index_ref[0], total_ref, keep_ref, give_ref)


def turned(whole):
    bits = axis_bits()
    cols = whole.shape[1]
    split = whole.reshape((2,) * len(bits) + (-1, cols))
    for place, (axis, step) in enumerate(bits):
        mine = (lax.axis_index(axis) // step) % 2
        split = jnp.where(mine == 1, jnp.flip(split, place), split)
    order = [bits.index(bit) for bit in block_order()]
    split = split.transpose(*order, len(bits), len(bits) + 1)
    return split.reshape(1, 2, -1, cols)


def weight_grads(operands, plan, width, stacked=False):
    blocks = relative_blocks()
    half = len(blocks) // 2
    rows = width // len(blocks)
    count = len(plan)
    if rows % 8:
        pieces = []
        for left, left_at, right, right_at in plan:
            left_rows = operands[left][:, left_at * width : (left_at + 1) * width]
            grads = operands[right][:, right_at * width : (right_at + 1) * width]
            pieces.append(turned(weight_grad(left_rows, grads).astype(bf16)))
        joined = jnp.concatenate(pieces, axis=0 if stacked else 3)
        return joined[:, 0], joined[:, 1]
    if stacked:
        shape, spec = (count, half, rows, width), lambda j, index: (j, 0, 0, 0)
    else:
        shape, spec = (1, half, rows, count * width), lambda j, index: (0, 0, 0, j)
    out = jax.ShapeDtypeStruct(shape, bf16)
    spec = pl.BlockSpec((1, half, rows, width), spec)
    tokens = operands[0].shape[0]
    pair = pl.pallas_call(
        functools.partial(weight_grads_kernel, blocks, plan),
        grid_spec=pltpu.PrefetchScalarGridSpec(
            num_scalar_prefetch=1,
            grid=(count,),
            in_specs=[pl.BlockSpec(a.shape, lambda j, index: (0, 0)) for a in operands],
            out_specs=[spec, spec],
            scratch_shapes=[pltpu.VMEM((width, width), f32)],
        ),
        out_shape=[out, out],
        compiler_params=pltpu.CompilerParams(vmem_limit_bytes=VMEM_LIMIT),
        cost_estimate=pl.CostEstimate(
            flops=2 * tokens * width * width * count,
            bytes_accessed=2 * sum(a.size for a in operands) + 2 * count * width * width,
            transcendentals=0,
        ),
        name="weight_grads",
    )(small_index(), *operands)
    return [side.reshape(shape[0], half * rows, shape[3]) for side in pair]


ROWS = 128
EDGES = ("output_bias", "down_bias", "mixer_gain", "mixer_shift", "feed_gain", "feed_shift")


def by_rows(count, body, rows=ROWS):
    for first in range(0, count, rows):
        body(slice(first, first + rows))


def feed_kernel(x_ref, mixed_ref, vectors_ref, bias_ref, out_ref, up_ref, down_ref,
                norm_ref, inverse_ref, low_ref, act_ref, slope_ref, norm_two_ref, inverse_two_ref,
                y_ref, hidden_ref, total_ref):
    step, last = pl.program_id(0), pl.num_programs(0) - 1
    count = x_ref.shape[0]

    def vector(name):
        at = EDGES.index(name)
        return vectors_ref[at : at + 1, :]

    @pl.when(step == 0)
    def _():
        total_ref[...] = dot_nn(mixed_ref[...], out_ref[...])

        def body(at):
            norm, inverse = normalised(x_ref[at, :] + total_ref[at, :] + vector("output_bias"))
            hidden = norm * vector("mixer_gain") + vector("mixer_shift")
            norm_ref[at, :], inverse_ref[at, :] = norm, inverse
            hidden_ref[at, :] = hidden
            low_ref[at, :] = hidden.astype(bf16)
            total_ref[at, :] = jnp.zeros_like(hidden)

        by_rows(count, body)

    def units(at):
        act, slope = gelu_both(dot_nn(low_ref[at, :], up_ref[...]) + bias_ref[...])
        act = act.astype(bf16)
        act_ref[at, :], slope_ref[at, :] = act, slope.astype(bf16)
        total_ref[at, :] += dot_nn(act, down_ref[...])

    by_rows(count, units, 256)

    @pl.when(step == last)
    def _():
        def body(at):
            rows = hidden_ref[at, :] + total_ref[at, :] + vector("down_bias")
            norm, inverse = normalised(rows)
            norm_two_ref[at, :], inverse_two_ref[at, :] = norm, inverse
            y_ref[at, :] = norm * vector("feed_gain") + vector("feed_shift")

        by_rows(count, body)


def feed_forward(x, mixed, small, whole, ratio):
    count, width = x.shape
    rows = pl.BlockSpec((count, width), lambda j: (0, 0))
    line = pl.BlockSpec((count, 1), lambda j: (0, 0))
    part = pl.BlockSpec((count, width), lambda j: (0, j))

    def weight(shift, moves):
        return pl.BlockSpec((width, width), lambda j: (0, shift + moves * j))

    def shape(cols, kind):
        return jax.ShapeDtypeStruct((count, cols), kind)

    return pl.pallas_call(
        feed_kernel,
        grid=(ratio,),
        in_specs=[
            rows, rows, pl.BlockSpec((8, width), lambda j: (0, 0)),
            pl.BlockSpec((1, width), lambda j: (0, j)),
            weight(0, 0), weight(1, 1), weight(1 + ratio, 1),
        ],
        out_specs=[rows, line, rows, part, part, rows, line, rows],
        out_shape=[
            shape(width, f32), shape(1, f32), shape(width, bf16), shape(ratio * width, bf16),
            shape(ratio * width, bf16), shape(width, f32), shape(1, f32), shape(width, f32),
        ],
        scratch_shapes=[pltpu.VMEM((count, width), f32)] * 2,
        compiler_params=pltpu.CompilerParams(vmem_limit_bytes=VMEM_LIMIT),
        cost_estimate=pl.CostEstimate(
            flops=2 * count * width * width * (1 + 2 * ratio), transcendentals=count * width * ratio,
            bytes_accessed=2 * whole.size + 4 * count * width * ratio + 20 * count * width,
        ),
        name="feed_forward",
    )(x, mixed, small["vectors"], small["up_bias"], whole, whole, whole)


def feed_back_kernel(blocks, index_ref, grads_ref, norm_ref, inverse_ref, norm_two_ref,
                     inverse_two_ref, vectors_ref, low_ref, act_ref, slope_ref, out_ref, up_ref,
                     down_ref, one_ref, attention_ref, mixed_ref, sums_ref, bias_ref, *rest):
    outs, (feed_ref, hidden_ref, total_ref, pre_ref, turn_ref) = rest[:-5], rest[-5:]
    step, last = pl.program_id(0), pl.num_programs(0) - 1
    count, width = grads_ref.shape

    def vector(name):
        at = EDGES.index(name)
        return vectors_ref[at : at + 1, :]

    def add(name, rows):
        at = EDGES.index(name)
        sums_ref[at : at + 1, :] += jnp.sum(rows, axis=0, keepdims=True)

    def store(pair):
        if blocks is None:
            pair[0][0] = total_ref[...].astype(bf16)
        else:
            store_blocks(blocks, index_ref[0], total_ref, *pair)

    @pl.when(step == 0)
    def _():
        sums_ref[...] = jnp.zeros_like(sums_ref)
        turn_ref[...] = jnp.transpose(low_ref[...])

        def body(at):
            grads, norm = grads_ref[at, :], norm_two_ref[at, :]
            add("feed_gain", grads * norm)
            add("feed_shift", grads)
            back = normalised_back(grads, vector("feed_gain"), norm, inverse_two_ref[at, :])
            hidden_ref[at, :] = back
            back = back.astype(bf16)
            feed_ref[at, :] = back
            add("down_bias", back.astype(f32))

        by_rows(count, body)

    pre_ref[...] = (
        slope_ref[...].astype(f32) * dot_nt(feed_ref[...], down_ref[...])
    ).astype(bf16)
    bias_ref[...] = jnp.sum(pre_ref[...].astype(f32), axis=0, keepdims=True)
    hidden_ref[...] += dot_nt(pre_ref[...], up_ref[...])
    total_ref[...] = weight_grad(act_ref[...], feed_ref[...])
    store(outs[: len(outs) // 2])
    total_ref[...] = dot_nn(turn_ref[...], pre_ref[...])
    store(outs[len(outs) // 2 :])

    @pl.when(step == last)
    def _():
        def body(at):
            grads, norm = hidden_ref[at, :], norm_ref[at, :]
            add("mixer_gain", grads * norm)
            add("mixer_shift", grads)
            back = normalised_back(grads, vector("mixer_gain"), norm, inverse_ref[at, :])
            one_ref[at, :] = back
            back = back.astype(bf16)
            attention_ref[at, :] = back
            add("output_bias", back.astype(f32))

        by_rows(count, body)
        mixed_ref[...] = dot_nt(attention_ref[...], out_ref[...]).astype(bf16)


def feed_back(grads, kept, small, whole, ratio):
    norm, inverse, low, act, slope, norm_two, inverse_two = kept
    count, width = grads.shape
    blocks = relative_blocks()
    half = len(blocks) // 2
    shard = width // len(blocks)
    rows = pl.BlockSpec((count, width), lambda j, index: (0, 0))
    line = pl.BlockSpec((count, 1), lambda j, index: (0, 0))
    part = pl.BlockSpec((count, width), lambda j, index: (0, j))
    edge = pl.BlockSpec((8, width), lambda j, index: (0, 0))

    def weight(shift, moves):
        return pl.BlockSpec((width, width), lambda j, index: (0, shift + moves * j))

    if shard % 8:
        blocks = None
        out = [jax.ShapeDtypeStruct((ratio, width, width), bf16)] * 2
        specs = [pl.BlockSpec((1, width, width), lambda j, index: (j, 0, 0))] * 2
    else:
        block = (1, half, shard, width)
        out = [jax.ShapeDtypeStruct((ratio, half, shard, width), bf16)] * 2
        out += [jax.ShapeDtypeStruct((1, half, shard, ratio * width), bf16)] * 2
        specs = [pl.BlockSpec(block, lambda j, index: (j, 0, 0, 0))] * 2
        specs += [pl.BlockSpec(block, lambda j, index: (0, 0, 0, j))] * 2
    results = pl.pallas_call(
        functools.partial(feed_back_kernel, blocks),
        grid_spec=pltpu.PrefetchScalarGridSpec(
            num_scalar_prefetch=1,
            grid=(ratio,),
            in_specs=[
                rows, rows, line, rows, line, edge, rows, part, part,
                weight(0, 0), weight(1, 1), weight(1 + ratio, 1),
            ],
            out_specs=[
                rows, rows, rows, edge, pl.BlockSpec((1, width), lambda j, index: (0, j)), *specs
            ],
            scratch_shapes=[
                pltpu.VMEM((count, width), bf16), pltpu.VMEM((count, width), f32),
                pltpu.VMEM((width, width), f32), pltpu.VMEM((count, width), bf16),
                pltpu.VMEM((width, count), bf16),
            ],
        ),
        out_shape=[
            jax.ShapeDtypeStruct((count, width), f32), jax.ShapeDtypeStruct((count, width), bf16),
            jax.ShapeDtypeStruct((count, width), bf16), jax.ShapeDtypeStruct((8, width), f32),
            jax.ShapeDtypeStruct((1, ratio * width), f32), *out,
        ],
        compiler_params=pltpu.CompilerParams(vmem_limit_bytes=VMEM_LIMIT),
        cost_estimate=pl.CostEstimate(
            flops=2 * count * width * width * (1 + 4 * ratio), transcendentals=0,
            bytes_accessed=4 * whole.size + 4 * count * width * ratio + 20 * count * width,
        ),
        name="feed_back",
    )(small_index(), grads, norm, inverse, norm_two, inverse_two, small["vectors"], low, act, slope,
      whole, whole, whole)
    one, attention_low, grad_mixed, sums, up_sums, *out = results
    if blocks is None:
        down = [turned(out[0][i]) for i in range(ratio)]
        down = [jnp.concatenate([d[:, side] for d in down]) for side in range(2)]
        up = [turned(out[1][i]) for i in range(ratio)]
        up = [jnp.concatenate([u[:, side] for u in up], axis=2) for side in range(2)]
    else:
        down = [side.reshape(ratio, half * shard, width) for side in out[:2]]
        up = [side.reshape(1, half * shard, ratio * width) for side in out[2:]]
    return one, attention_low, grad_mixed, sums, up_sums, down, up


def units_back_kernel(spread_ref, *refs):
    parts, out_ref = refs[:-1], refs[-1]
    total = None
    for part, rows_ref in enumerate(parts):
        left = rows_ref[...]
        for _ in range(3):
            piece = left.astype(bf16)
            left = left - piece.astype(f32)
            term = dot_nn(piece, spread_ref[part])
            total = term if total is None else total + term
    out_ref[...] = total


def units_back(rows, ratio, shard_rows):
    count, cols = rows.shape
    block = cols // ratio // 2
    source = jnp.arange(block, dtype=jnp.int32)
    target = jnp.arange(ratio * block, dtype=jnp.int32)
    device, rest = target // (ratio * shard_rows), target % (ratio * shard_rows)
    wanted = device * shard_rows + rest % shard_rows
    spread = jnp.stack([
        (source[:, None] == wanted[None, :]) & (rest[None, :] // shard_rows == part)
        for part in range(ratio)
    ]).astype(bf16)
    return pl.pallas_call(
        units_back_kernel,
        grid=(2,),
        in_specs=[pl.BlockSpec(spread.shape, lambda j: (0, 0, 0))] + [
            pl.BlockSpec((count, block), functools.partial(lambda part, j: (0, 2 * part + j), part))
            for part in range(ratio)
        ],
        out_specs=pl.BlockSpec((count, ratio * block), lambda j: (0, j)),
        out_shape=jax.ShapeDtypeStruct((count, cols), f32),
        compiler_params=pltpu.CompilerParams(vmem_limit_bytes=VMEM_LIMIT),
        name="units_back",
    )(spread, *[rows] * ratio)


SMALL_COLUMNS = 128


def small_grads_kernel(blocks, layers, index_ref, *refs):
    sources, (keep_ref, give_ref, lines_ref, columns_ref) = refs[:-4], refs[-4:]
    lines_ref[...] = jnp.zeros_like(lines_ref)
    width = lines_ref.shape[1]
    each = len(sources) // layers
    at = 0
    for layer in range(layers):
        query_ref, value_ref, sums_ref, up_ref, taps_ref = sources[layer * each : (layer + 1) * each]
        lines_ref[at : at + 1, :] = query_ref[...]
        lines_ref[at + 1 : at + 2, :] = value_ref[...]
        lines_ref[at + 2 : at + 2 + len(EDGES), :] = sums_ref[: len(EDGES), :]
        at += 2 + len(EDGES)
        for kind in range(2):
            lines_ref[at : at + TAPS, :] = taps_ref[kind, :TAPS]
            at += TAPS
        for part in range(up_ref.shape[1] // width):
            lines_ref[at : at + 1, :] = up_ref[:, part * width : (part + 1) * width]
            at += 1
    columns_ref[...] = jnp.transpose(lines_ref[...])
    store_blocks(blocks, index_ref[0], columns_ref, keep_ref, give_ref)


def small_grads(per_layer, width):
    blocks = relative_blocks()
    half = len(blocks) // 2
    rows = width // len(blocks)
    if rows % 8:
        lines = []
        for query, value, sums, up, taps in per_layer:
            lines += [query, value, sums[: len(EDGES)], taps[0, :TAPS], taps[1, :TAPS]]
            lines.append(up.reshape(-1, width))
        lines = jnp.concatenate(lines, axis=0)
        lines = jnp.pad(lines, ((0, SMALL_COLUMNS - lines.shape[0]), (0, 0))).T.astype(bf16)
        lines = turned(lines)
        return lines[:, 0], lines[:, 1]
    flat = [a for arrays in per_layer for a in arrays]
    out = jax.ShapeDtypeStruct((1, half, rows, SMALL_COLUMNS), bf16)
    pair = pl.pallas_call(
        functools.partial(small_grads_kernel, blocks, len(per_layer)),
        in_specs=[pl.BlockSpec(memory_space=pltpu.SMEM)]
        + [pl.BlockSpec(memory_space=pltpu.VMEM)] * len(flat),
        out_specs=[pl.BlockSpec(memory_space=pltpu.VMEM)] * 2,
        out_shape=[out, out],
        scratch_shapes=[pltpu.VMEM((SMALL_COLUMNS, width), f32), pltpu.VMEM((width, SMALL_COLUMNS), f32)],
        compiler_params=pltpu.CompilerParams(vmem_limit_bytes=VMEM_LIMIT),
        name="small_grads",
    )(small_index(), *flat)
    return [side.reshape(1, half * rows, SMALL_COLUMNS) for side in pair]


def layer_forward(x, weights, masks, select, count, at):
    qkv_weight, feed_weights, small = weights
    width = x.shape[1]
    length = x.shape[0] // count
    x_low = x.astype(bf16)
    bias = jnp.concatenate([small["query_bias"], jnp.zeros((width,), f32), small["value_bias"]])
    qkv = matmul(x_low, qkv_weight)
    qkv = at("projected", (qkv + bias).astype(bf16).reshape(count, length, -1))
    rows_low = passed_along(qkv[:, length - WIN :, width:], 1)
    rows_up = passed_along(qkv[:, :WIN, width:], -1)
    rows_low, rows_up = tied([rows_low, rows_up])
    pooled = at("pooled", pool(select, small["taps"], qkv, rows_low, width))
    pooled_low, pooled_up = pooled_rims(pooled)
    pooled_up = at("attending", pooled_up)
    operands = attend_operands(qkv, rows_low, rows_up, pooled, pooled_low, pooled_up)
    mixed, stats = attend(masks, operands, width)
    mixed = at("attended", mixed.reshape(count * length, width))
    ratio = small["up_bias"].shape[1] // width
    norm, inverse, hidden_low, act_low, slope, norm_two, inverse_two, y = feed_forward(
        x, mixed, small, feed_weights, ratio
    )
    y = at("fed", y)
    kept = (x_low, operands, stats, mixed, (norm, inverse, hidden_low, act_low, slope, norm_two, inverse_two))
    return y, kept


def layer_backward(grads, kept, weights, masks, select, count, at):
    qkv_weight, feed_weights, small = weights
    x_low, operands, stats, mixed, feed_kept = kept
    rows, width = grads.shape
    length = rows // count
    ratio = small["up_bias"].shape[1] // width

    def total(value):
        return jnp.sum(value.astype(f32), axis=0, keepdims=True)

    grad_one, attention_low, grad_mixed, sums, up_sums, down_halves, up_halves = feed_back(
        grads, feed_kept, small, feed_weights, ratio
    )
    grad_mixed = at("attending", grad_mixed, (down_halves, up_halves))
    grad_mixed = grad_mixed.reshape(count, length, width)
    part = max(count // 2, 1)
    pieces = list(attend_back(masks, stats, grad_mixed, operands, 0, part))
    if part < count:
        pieces[0] = at("halfway", pieces[0])
        pieces = attend_back(masks, stats, grad_mixed, operands, part, count - part, pieces)
    grad_query, own, pooled_own, rim_low, rim_up = pieces
    rim_up = at("rims", rim_up)
    grad_query = grad_query.reshape(rows, width)
    from_low, from_up, second, pooled_own = rims_return(rim_low, rim_up, pooled_own)
    own, *tail, taps = pool_back(
        select, small["taps"], operands[0], operands[3], own, pooled_own, from_low, from_up,
        rim_up, second,
    )
    if tail:
        tail = passed_along(tail[0], -1).astype(f32)
        own = own + jnp.pad(tail, ((0, 0), (0, 0), (length - 16, 0), (0, 0)))
    own = at("pooled", own, (x_low, grad_query, mixed, attention_low))
    own = own.astype(bf16).reshape(2, rows, width)
    grad_qkv = (grad_query, own[0], own[1])
    grad_x = grad_one + matmul_t(jnp.concatenate(grad_qkv, axis=1), qkv_weight)
    small_sums = [total(grad_query), total(own[1]), sums, up_sums, taps]
    return grad_x, (x_low, *grad_qkv, mixed, attention_low), small_sums


def pack_small(vectors, up_biases, taps):
    columns = []
    for layer in range(vectors[0].shape[0]):
        rows = vectors[0].shape[1]
        columns.append(jnp.stack([v[layer] for v in vectors]))
        columns.append(taps[0][layer])
        columns.append(taps[1][layer])
        columns.append(up_biases[layer].reshape(-1, rows))
    packed = jnp.concatenate(columns, axis=0)
    return jnp.pad(packed, ((0, SMALL_COLUMNS - packed.shape[0]), (0, 0))).T


def unpack_small(columns, layers, ratio):
    width = columns.shape[0]
    lines = columns.astype(f32).T
    per_layer = 8 + 2 * TAPS + ratio
    pad = ((0, 8 - TAPS), (0, 0))
    result = []
    for layer in range(layers):
        piece = lines[layer * per_layer : (layer + 1) * per_layer]
        result.append({
            "query_bias": piece[0],
            "value_bias": piece[1],
            "vectors": piece[2:10],
            "taps": jnp.stack([
                jnp.pad(piece[8 : 8 + TAPS], pad), jnp.pad(piece[8 + TAPS : 8 + 2 * TAPS], pad),
            ]),
            "up_bias": piece[8 + 2 * TAPS :].reshape(1, ratio * width),
        })
    return result


def on_device(
    tokens, cotangent, masked, query_weight, key_weight, value_weight, output_weight, up_weight,
    down_weight, query_bias, value_bias, output_bias, up_bias, down_bias, mixer_gain, mixer_shift,
    feed_gain, feed_shift, pool_key, pool_value,
):
    micro, seqs, length, width = tokens.shape
    count = micro * seqs
    layers = query_weight.shape[0]
    devices = lax.axis_size("seq") * lax.axis_size("batch")
    shard_rows = width // devices
    small_shard = pack_small(
        (query_bias, value_bias, output_bias, down_bias, mixer_gain, mixer_shift, feed_gain,
         feed_shift), up_bias, (pool_key, pool_value),
    )
    masks = window_masks(length)
    select = tap_select(length)
    ratio = up_weight.shape[2] // width

    def units_apart(rows):
        split = rows.reshape(rows.shape[0], devices, ratio, shard_rows)
        return split.transpose(0, 2, 1, 3).reshape(rows.shape)

    shard = jnp.concatenate(
        [query_weight[0], key_weight[0], value_weight[0], small_shard], axis=1
    )
    first = Gather(shard[None], path("y"))

    later = [
        Gather(jnp.concatenate(
            [query_weight[layer], key_weight[layer], value_weight[layer]], axis=1
        )[None], path("x"))
        for layer in range(1, layers)
    ]
    x = tokens.reshape(count * length, width).astype(f32)
    feeds = []

    def gather_feed(layer, after):
        out, up, down, after = tied(
            [output_weight[layer], up_weight[layer], down_weight[layer], after]
        )
        parts = down.reshape(ratio, shard_rows, width)
        shard = jnp.concatenate([out, units_apart(up), *parts], axis=1)
        feeds.append(lax.all_gather(shard, ("seq", "batch"), axis=0, tiled=True))
        return after

    x = checkpoint(x, [], [first])
    x = gather_feed(0, checkpoint(x, [first]))
    while first.left > 2:
        x = checkpoint(x, [first])
    for layer in range(1, layers):
        x = gather_feed(layer, x)
    x = checkpoint(x, [first])
    x = checkpoint(x, [first], later)
    first_whole = in_place(first.halves, first.cols)
    smalls = unpack_small(first_whole[:, 3 * width :], layers, ratio)

    def landed(value, flows, left):
        while True:
            behind = [flow for flow in flows if flow.left > left]
            if not behind:
                return value
            value = checkpoint(value, behind)

    def forward_at(layer):
        following = later[layer : layer + 1]

        def at(name, value):
            if name in ("projected", "pooled", "attended"):
                return checkpoint(value, following)
            if name == "fed":
                return landed(value, following, 0)
            return value

        return at

    states, weights = [], []
    for layer in range(layers):
        if layer == 0:
            qkv_weight = first_whole[:, : 3 * width]
        else:
            qkv_weight = in_place(later[layer - 1].halves, width)
        whole = (qkv_weight, feeds[layer], smalls[layer])
        x, kept = layer_forward(x, whole, masks, select, count, forward_at(layer))
        states.append(kept)
        weights.append(whole)
    layer_output = x.astype(bf16).reshape(tokens.shape)
    grads = cotangent.astype(f32) * masked.astype(f32)[..., None]
    grads = grads.reshape(count * length, width)
    flows = {}
    plans = {
        "down": ["rims", "next attending", "next halfway", "next rims", "never"],
        "up": ["rims", "next attending", "next halfway", "next rims", "never"],
        "in": ["next attending", "next rims", "never"],
        "query": ["never"],
    }
    last_plans = {
        "down": ["halfway", "rims", "never"],
        "up": ["halfway", "rims", "never"],
    }
    waiting = []

    def due(layer, name):
        result = []
        for (kind, owner), flow in flows.items():
            plan = last_plans[kind] if owner == 0 and kind in last_plans else plans[kind]
            when = plan[min(flow.stage, len(plan) - 1)]
            if flow.done or flow in waiting:
                continue
            if when == ("next " if owner > layer else "") + name or owner > layer + 1:
                result.append(flow)
        return result

    def backward_at(layer):
        def at(name, value, given=None):
            landing, begin = due(layer, name), []
            if name == "attending":
                for kind, halves, last in zip(("down", "up"), given, "yx"):
                    flows[kind, layer] = Scatter(halves, path(last)[::-1])
                    begin.append(flows[kind, layer])
            if name == "pooled" and layer == 0:
                plan = [(0, 0, 1, 0), (2, 0, 3, 0)]
                flow = Scatter(weight_grads(given, plan, width), path("z")[::-1])
                flows["query", layer] = flow
            if name in ("rims", "pooled"):
                waiting.extend(flow for flow in landing if len(flow.order) - flow.stage > 2)
            return checkpoint(value, landing, [] if name == "pooled" else begin, waiting)

        return at

    small_sums = [None] * layers
    for layer in reversed(range(layers)):
        grads, given, small_sums[layer] = layer_backward(
            grads, states[layer], weights[layer], masks, select, count, backward_at(layer)
        )
        if layer > 0:
            plan = [(0, 0, 1 + i, 0) for i in range(3)] + [(4, 0, 5, 0)]
            flow = Scatter(weight_grads(given, plan, width), path("z")[::-1])
            flows["in", layer] = flow
            grads = checkpoint(grads, due(layer, "end"), [flow] + waiting)
            waiting.clear()
    halves = weight_grads((given[0], *given[2:4]), [(0, 0, 1, 0), (0, 0, 2, 0)], width)
    sides = small_grads(small_sums, width)
    joined = [jnp.concatenate(parts, axis=2) for parts in zip(halves, sides)]
    last = Scatter(joined, path("x")[::-1])
    flows["last", 0] = last
    ends = [last, flows["query", 0]]
    marker = checkpoint(last.keep[:1, :1, :1], [], ends)
    marker = checkpoint(marker, ends, waiting)
    while True:
        ends = [flow for flow in ends if not flow.done]
        others = [flow for flow in flows.values() if not flow.done and flow not in ends]
        if not ends + others:
            break
        if ends:
            marker = checkpoint(marker, ends)
        if others:
            marker = checkpoint(marker, others)
    totals = []
    for layer in range(layers):
        if layer > 0:
            whole = flows["in", layer].total[0]
            parts = [whole[:, i * width : (i + 1) * width] for i in range(4)]
        else:
            whole = flows["query", 0].total[0]
            end = last.total[0]
            parts = [whole[:, :width], end[:, :width], end[:, width : 2 * width], whole[:, width:]]
        parts.append(flows["up", layer].total[0])
        parts.append(flows["down", layer].total.reshape(ratio * shard_rows, width))
        totals.append(parts)
    up_totals = units_back(
        jnp.concatenate([parts[4] for parts in totals]), ratio, shard_rows
    ).reshape(layers, shard_rows, ratio * width)
    input_grad = grads.astype(bf16).reshape(tokens.shape)
    lines = last.total[0, :, 2 * width :].T
    per_layer = 8 + 2 * TAPS + ratio
    lines = lines[: layers * per_layer].reshape(layers, per_layer, shard_rows)
    vectors = [lines[:, i] for i in range(8)]
    after = 8 + 2 * TAPS
    grad_up_bias = lines[:, after:].reshape(layers, -1)
    return (
        layer_output, input_grad,
        *[jnp.stack([t[i] for t in totals]) if i != 4 else up_totals for i in range(6)],
        vectors[0], vectors[1], vectors[2], grad_up_bias, *vectors[3:],
        lines[:, 8 : 8 + TAPS], lines[:, 8 + TAPS : after],
    )


def solution(mesh):
    rows = P(None, "batch", "seq", None)
    matrix = P(None, ("seq", "batch"), None)
    vector = P(None, ("seq", "batch"))
    taps = P(None, None, ("seq", "batch"))
    params = (matrix,) * 6 + (vector,) * 9 + (taps,) * 2
    return jax.shard_map(
        on_device,
        mesh=mesh,
        in_specs=(rows, rows, P(None, "batch", "seq")) + params,
        out_specs=(rows, rows) + params,
        check_vma=False,
    )
```

```python
import functools

import jax
import jax.numpy as jnp
from jax import lax
from jax.experimental import pallas as pl
from jax.experimental.pallas import tpu as pltpu
from jax.sharding import PartitionSpec as P

HEADS = 12
WIN = 64
PWIN = 256
TAPS = 5
REACH = PWIN // 4
QROWS = 128
norm_eps = 1e-05
gelu_coef = 0.7978845608028654
masked_score = -1e30
f32 = jnp.float32
bf16 = jnp.bfloat16
VMEM_LIMIT = 48 * 1024 * 1024


def axis_bits():
    bits = []
    for axis in ("seq", "batch"):
        step = lax.axis_size(axis) // 2
        while step:
            bits.append((axis, step))
            step //= 2
    return bits


def path(name):
    bits = axis_bits()
    core, row = ("seq", 1), ("seq", 2)
    column = [bit for bit in bits if bit[0] == "seq" and bit[1] > 2]
    across = [bit for bit in bits if bit[0] == "batch"]
    order = {
        "y": column + across + [row],
        "x": column + [row] + across,
        "z": column[:-1] + across + [row] + column[-1:],
        "w": [row] + column + across,
    }[name]
    return order + [core]


def exchange(value, axis, step):
    pairs = [(i, i ^ step) for i in range(lax.axis_size(axis))]
    return lax.ppermute(value, axis, pairs)


def block_order():
    bits = axis_bits()
    return [("seq", 1), ("seq", 2)] + [b for b in bits if b[0] == "batch"] + [
        b for b in bits if b[0] == "seq" and b[1] > 2
    ]


def flat_index():
    return lax.axis_index("seq") * lax.axis_size("batch") + lax.axis_index("batch")


def relative_blocks():
    spread = []
    for axis, step in block_order():
        spread.append(step * lax.axis_size("batch") if axis == "seq" else step)
    count = len(spread)
    return [
        sum(spread[k] for k in range(count) if place >> (count - 1 - k) & 1)
        for place in range(2**count)
    ]


def tied(values):
    return list(lax.optimization_barrier(tuple(values)))


class Gather:
    def __init__(self, shard, order):
        self.current, self.order = shard, order
        self.have, self.halves, self.flying = [], None, None
        self.parts, self.rows, self.cols = shard.shape

    def ready(self):
        return self.current

    def hold(self, value):
        self.current = value

    def launch(self):
        self.flying = exchange(self.current, *self.order[len(self.have)])

    def land(self):
        stage = self.order[len(self.have)]
        if stage == self.order[-1]:
            self.halves = (self.current, self.flying)
            return
        significance = block_order()
        place = significance.index(stage)
        before = sum(1 for p in self.have if p < place)
        split = (self.parts * 2**before, 1, 2 ** (len(self.have) - before) * self.rows, self.cols)
        self.have.append(place)
        joined = jnp.concatenate([self.current.reshape(split), self.flying.reshape(split)], axis=1)
        self.current = joined.reshape(self.parts, 2 ** len(self.have) * self.rows, self.cols)

    @property
    def left(self):
        return 0 if self.halves is not None else len(self.order) - len(self.have)

    @property
    def done(self):
        return self.halves is not None


class Scatter:
    def __init__(self, halves, order):
        self.keep, self.give = halves
        self.order, self.stage, self.total, self.flying = order, 0, None, None
        self.have = list(range(1, len(order)))
        self.parts, half_rows, self.cols = self.keep.shape
        self.rows = half_rows // 2 ** len(self.have)

    def ready(self):
        return self.give

    def hold(self, value):
        self.give = value

    def launch(self):
        self.flying = exchange(self.give, *self.order[self.stage])

    def land(self):
        self.stage += 1
        if self.stage == len(self.order):
            total = self.keep.astype(f32) + self.flying.astype(f32)
            self.total = total.reshape(self.parts, self.rows, self.cols)
            return
        place = self.have.index(block_order().index(self.order[self.stage]))
        self.have.pop(place)
        left = 2 ** len(self.have) * self.rows
        split = (self.parts * 2**place, 2, left >> place, self.cols)
        keep, got = self.keep.reshape(split), self.flying.reshape(split)
        self.keep, self.give = [
            (keep[:, side].astype(f32) + got[:, side].astype(f32)).astype(bf16).reshape(
                self.parts, left, self.cols
            ) for side in range(2)
        ]

    @property
    def done(self):
        return self.total is not None


def checkpoint(value, flows, begin=(), waiting=()):
    value, *flying = tied([value] + [flow.flying for flow in flows])
    for flow, arrived in zip(flows, flying):
        flow.flying = arrived
        flow.land()
    going = [flow for flow in flows if not flow.done and flow not in waiting] + list(begin)
    value, *ready = tied([value] + [flow.ready() for flow in going])
    for flow, part in zip(going, ready):
        flow.hold(part)
        flow.launch()
    return value


def passed_along(value, steps):
    count = lax.axis_size("seq")
    pairs = [(i, i + steps) for i in range(count) if 0 <= i + steps < count]
    return lax.ppermute(value, "seq", pairs)


def pooled_hops(size):
    return -(-REACH // size)


def pooled_rims(pooled):
    size = pooled.shape[1]
    hops = range(1, pooled_hops(size) + 1)
    low = [passed_along(pooled, hop) for hop in reversed(hops)]
    up = [passed_along(pooled, -hop) for hop in hops]
    low = low[0] if len(low) == 1 else jnp.concatenate(low, axis=1)
    up = up[0] if len(up) == 1 else jnp.concatenate(up, axis=1)
    return low[:, low.shape[1] - REACH :], up[:, :REACH]


def rims_return(rim_low, rim_up, pooled_own):
    size = pooled_own.shape[2]
    hops = pooled_hops(size)
    if hops == 1:
        second = passed_along(rim_low[:, :, WIN : WIN + 16], -2)
        return tied([passed_along(rim_up, 1), passed_along(rim_low, -1), second]) + [pooled_own]
    far_low, far_up = rim_low[:, :, WIN : WIN + REACH], rim_up[:, :, WIN:]
    for hop in range(2, hops + 1):
        start = REACH - hop * size
        pooled_own = pooled_own + passed_along(far_low[:, :, start : start + size], -hop).astype(f32)
        start = (hop - 1) * size
        pooled_own = pooled_own + passed_along(far_up[:, :, start : start + size], hop).astype(f32)
    near_low, near_up = rim_low[:, :, :WIN], rim_up[:, :, :WIN]
    rim_low = jnp.concatenate([near_low, far_low[:, :, REACH - size :]], axis=2)
    rim_up = jnp.concatenate([near_up, far_up[:, :, :size]], axis=2)
    return passed_along(rim_up, 1), passed_along(rim_low, -1), None, pooled_own


def dot_nt(a, b):
    return lax.dot_general(a, b, (((1,), (1,)), ((), ())), preferred_element_type=f32)


def dot_nn(a, b):
    return lax.dot_general(a, b, (((1,), (0,)), ((), ())), preferred_element_type=f32)


def flipped(block):
    return jnp.transpose(block.astype(f32)).astype(bf16)


def two_heads(rows):
    lane = lax.broadcasted_iota(jnp.int32, rows.shape, 1)
    none = jnp.zeros_like(rows)
    half = rows.shape[1] // 2
    return jnp.concatenate(
        [jnp.where(lane < half, rows, none), jnp.where(lane < half, none, rows)], axis=0
    )


def heads_apart(block):
    half, queries = block.shape[0] // 2, block.shape[1] // 2
    return jnp.transpose(
        jnp.concatenate([block[:half, :queries], block[half:, queries:]], axis=0)
    )


def attend_kernel(near_ref, far_ref, q_ref, k_ref, v_ref, kl_ref, vl_ref, ku_ref, vu_ref,
                  pk_ref, pv_ref, pkl_ref, pvl_ref, pku_ref, pvu_ref, mixed_ref, stat_ref):
    blocks = q_ref.shape[1] // QROWS
    pairs = q_ref.shape[2] // 128
    for pair in range(pairs):
        at = slice(128 * pair, 128 * pair + 128)
        keys = jnp.concatenate([kl_ref[0, :, at], k_ref[0, :, at], ku_ref[0, :, at]], axis=0)
        values = jnp.concatenate([vl_ref[0, :, at], v_ref[0, :, at], vu_ref[0, :, at]], axis=0)
        far_keys = jnp.concatenate([pkl_ref[0, :, at], pk_ref[0, :, at], pku_ref[0, :, at]], axis=0)
        far_values = jnp.concatenate(
            [pvl_ref[0, :, at], pv_ref[0, :, at], pvu_ref[0, :, at]], axis=0
        )
        values_t, far_values_t = flipped(values), flipped(far_values)
        for block in range(blocks):
            first = QROWS * block
            query = two_heads(q_ref[0, first : first + QROWS, at] * 0.125)
            stop = first + QROWS + 2 * WIN
            score = dot_nt(keys[first:stop], query) + near_ref[block]
            top = jnp.max(score, axis=0, keepdims=True)
            prob = jnp.exp(score - top)
            total = jnp.sum(prob, axis=0, keepdims=True)
            near_low = (prob * (1.0 / total)).astype(bf16)
            row = (pair * blocks + block) * 2
            stat_ref[0, 0, row : row + 1, :] = top + jnp.log(total)
            score = dot_nt(far_keys, query) + far_ref[block]
            top = jnp.max(score, axis=0, keepdims=True)
            prob = jnp.exp(score - top)
            total = jnp.sum(prob, axis=0, keepdims=True)
            far_low = (prob * (1.0 / total)).astype(bf16)
            stat_ref[0, 0, row + 1 : row + 2, :] = top + jnp.log(total)
            mixed = dot_nn(values_t[:, first:stop], near_low) + dot_nn(far_values_t, far_low)
            mixed_ref[0, first : first + QROWS, at] = heads_apart(mixed).astype(bf16)


def attend_back_kernel(near_ref, far_ref, stat_ref, g_ref, q_ref, k_ref, v_ref, kl_ref, vl_ref,
                       ku_ref, vu_ref, pk_ref, pv_ref, pkl_ref, pvl_ref, pku_ref, pvu_ref,
                       dq_ref, own_ref, pool_ref, low_ref, up_ref):
    blocks = q_ref.shape[1] // QROWS
    pairs = q_ref.shape[2] // 128
    length = q_ref.shape[1]
    for pair in range(pairs):
        at = slice(128 * pair, 128 * pair + 128)
        keys = jnp.concatenate([kl_ref[0, :, at], k_ref[0, :, at], ku_ref[0, :, at]], axis=0)
        values = jnp.concatenate([vl_ref[0, :, at], v_ref[0, :, at], vu_ref[0, :, at]], axis=0)
        far_keys = jnp.concatenate([pkl_ref[0, :, at], pk_ref[0, :, at], pku_ref[0, :, at]], axis=0)
        far_values = jnp.concatenate(
            [pvl_ref[0, :, at], pv_ref[0, :, at], pvu_ref[0, :, at]], axis=0
        )
        keys_t, far_keys_t = flipped(keys), flipped(far_keys)
        near_parts = ([], [])
        far_totals = [None, None]
        for block in range(blocks):
            first = QROWS * block
            query = two_heads(q_ref[0, first : first + QROWS, at] * 0.125)
            grads = two_heads(g_ref[0, first : first + QROWS, at])
            stop = first + QROWS + 2 * WIN
            row = (pair * blocks + block) * 2
            prob = jnp.exp(
                dot_nt(keys[first:stop], query) + near_ref[block] - stat_ref[0, 0, row : row + 1, :]
            )
            grad_prob = dot_nt(values[first:stop], grads)
            inner = jnp.sum(prob * grad_prob, axis=0, keepdims=True)
            grad_score = (prob * (grad_prob - inner)).astype(bf16)
            near_parts[0].append(dot_nn(grad_score, query))
            near_parts[1].append(dot_nn(prob.astype(bf16), grads))
            grad_query = dot_nn(keys_t[:, first:stop], grad_score)
            prob = jnp.exp(
                dot_nt(far_keys, query) + far_ref[block] - stat_ref[0, 0, row + 1 : row + 2, :]
            )
            grad_prob = dot_nt(far_values, grads)
            inner = jnp.sum(prob * grad_prob, axis=0, keepdims=True)
            grad_score = (prob * (grad_prob - inner)).astype(bf16)
            parts = (dot_nn(grad_score, query), dot_nn(prob.astype(bf16), grads))
            grad_query = grad_query + dot_nn(far_keys_t, grad_score)
            dq_ref[0, first : first + QROWS, at] = (heads_apart(grad_query) * 0.125).astype(bf16)
            for kind in range(2):
                far_totals[kind] = parts[kind] if block == 0 else far_totals[kind] + parts[kind]
        for kind in range(2):
            rows = []
            for chunk in range(blocks + 1):
                terms = []
                if chunk < blocks:
                    terms.append(near_parts[kind][chunk][:QROWS])
                if chunk > 0:
                    terms.append(near_parts[kind][chunk - 1][QROWS:])
                rows.append(functools.reduce(jnp.add, terms))
            rows = jnp.concatenate(rows, axis=0)
            own_ref[kind, 0, :, at] = rows[WIN : WIN + length]
            low_ref[kind, 0, :WIN, at] = rows[:WIN].astype(bf16)
            up_ref[kind, 0, :WIN, at] = rows[WIN + length :].astype(bf16)
            far = far_totals[kind]
            pool_ref[kind, 0, :, at] = far[REACH : far.shape[0] - REACH]
            low_ref[kind, 0, WIN : WIN + REACH, at] = far[:REACH].astype(bf16)
            low_ref[kind, 0, WIN + REACH :, at] = far[REACH : REACH + 16].astype(bf16)
            up_ref[kind, 0, WIN:, at] = far[far.shape[0] - REACH :].astype(bf16)


LANES = 256


def attend_specs(length, width):
    groups = width // LANES
    pooled = length // 4

    def spec(rows, shift):
        return pl.BlockSpec((1, rows, LANES), lambda g, j: (g, 0, j + shift))

    def whole(count, rows):
        return pl.BlockSpec((count, rows, 2 * QROWS), lambda g, j: (0, 0, 0))

    blocks = length // QROWS
    masks = [whole(blocks, QROWS + 2 * WIN), whole(blocks, pooled + 2 * REACH)]
    stat_rows = LANES // 128 * blocks * 2
    stat = pl.BlockSpec((1, 1, stat_rows, 2 * QROWS), lambda g, j: (g, j, 0, 0))
    operands = [spec(length, 0), spec(length, groups), spec(length, 2 * groups)]
    operands += [spec(WIN, 0), spec(WIN, groups)] * 2
    operands += [spec(pooled, 0), spec(pooled, groups)]
    operands += [spec(REACH, 0), spec(REACH, groups)] * 2
    return groups, masks, stat, stat_rows, operands, spec


def attend_operands(qkv, rows_low, rows_up, pooled, pooled_low, pooled_up):
    return (
        qkv, qkv, qkv, rows_low, rows_low, rows_up, rows_up,
        pooled, pooled, pooled_low, pooled_low, pooled_up, pooled_up,
    )


def attend(masks, operands, width):
    qkv = operands[0]
    count, length = qkv.shape[:2]
    groups, mask_specs, stat, stat_rows, specs, spec = attend_specs(length, width)
    return pl.pallas_call(
        attend_kernel,
        grid=(count, groups),
        in_specs=mask_specs + specs,
        out_specs=[spec(length, 0), stat],
        out_shape=[
            jax.ShapeDtypeStruct((count, length, width), bf16),
            jax.ShapeDtypeStruct((count, groups, stat_rows, 2 * QROWS), f32),
        ],
        compiler_params=pltpu.CompilerParams(vmem_limit_bytes=VMEM_LIMIT),
        cost_estimate=pl.CostEstimate(
            flops=count * length * width * 2000, bytes_accessed=8000000, transcendentals=3000000
        ),
        name="attend",
    )(*masks, *operands)


def attend_back(masks, stats, grad_mixed, operands, first, count, before=None):
    every, length, width = grad_mixed.shape
    groups, mask_specs, stat, stat_rows, specs, spec = attend_specs(length, width)
    pooled = length // 4

    def pair_spec(rows):
        return pl.BlockSpec((2, 1, rows, LANES), lambda g, j: (0, g, 0, j))

    def moved(block):
        index_map = block.index_map
        return pl.BlockSpec(block.block_shape, lambda g, j: index_map(g + first, j))

    in_specs = [stat, spec(length, 0)] + specs
    out_specs = [
        spec(length, 0), pair_spec(length), pair_spec(pooled),
        pair_spec(WIN + REACH + 16), pair_spec(WIN + REACH),
    ]
    out_specs = [moved(block) for block in out_specs[:1]] + [
        pl.BlockSpec(
            block.block_shape, functools.partial(lambda g, j: (0, g + first, 0, j))
        ) for block in out_specs[1:]
    ]
    before = before or []
    kernel_inputs = len(mask_specs) + len(in_specs)

    def kernel(*refs):
        attend_back_kernel(*refs[:kernel_inputs], *refs[kernel_inputs + len(before) :])

    return pl.pallas_call(
        kernel,
        grid=(count, groups),
        in_specs=mask_specs + [moved(block) for block in in_specs]
        + [pl.BlockSpec(memory_space=pl.ANY)] * len(before),
        out_specs=out_specs,
        out_shape=[
            jax.ShapeDtypeStruct((every, length, width), bf16),
            jax.ShapeDtypeStruct((2, every, length, width), f32),
            jax.ShapeDtypeStruct((2, every, pooled, width), f32),
            jax.ShapeDtypeStruct((2, every, WIN + REACH + 16, width), bf16),
            jax.ShapeDtypeStruct((2, every, WIN + REACH, width), bf16),
        ],
        input_output_aliases={kernel_inputs + i: i for i in range(len(before))},
        compiler_params=pltpu.CompilerParams(vmem_limit_bytes=VMEM_LIMIT),
        cost_estimate=pl.CostEstimate(
            flops=count * length * width * 5000, bytes_accessed=6000000 * count,
            transcendentals=1500000 * count,
        ),
        name="attend_back",
    )(*masks, stats, grad_mixed, *operands, *before)


def window_masks(length):
    blocks = length // QROWS
    index, devices = lax.axis_index("seq"), lax.axis_size("seq")

    def bias(width, offset, scale, reach):
        key = lax.broadcasted_iota(jnp.int32, (blocks, width, QROWS), 1)
        query = lax.broadcasted_iota(jnp.int32, (blocks, width, QROWS), 2)
        block = lax.broadcasted_iota(jnp.int32, (blocks, width, QROWS), 0)
        key = key - offset + (block * QROWS if scale == 1 else 0)
        query = query + block * QROWS
        size = length // scale
        allowed = jnp.abs(query - scale * key) <= reach
        place = key + index * size
        allowed &= (place >= 0) & (place < size * devices)
        one = jnp.where(allowed, 0.0, masked_score).astype(f32)
        return jnp.concatenate([one, one], axis=2)

    return bias(QROWS + 2 * WIN, WIN, 1, WIN), bias(length // 4 + 2 * REACH, REACH, 4, PWIN)


def tap_select(length):
    pooled = length // 4
    row = jnp.arange(TAPS * pooled, dtype=jnp.int32)
    column = jnp.arange(length, dtype=jnp.int32)
    source = 4 * (row % pooled) + row // pooled - 2
    return (source[:, None] == column[None, :]).astype(bf16)


def pool_kernel(select_ref, kernel_ref, rows_ref, low_ref, pooled_ref):
    pooled = pooled_ref.shape[1]
    for group in range(rows_ref.shape[0]):
        taps = dot_nn(select_ref[...], rows_ref[group])
        total = kernel_ref[0, 0:1, :] * taps[:pooled]
        for tap in range(1, TAPS):
            total = total + kernel_ref[0, tap : tap + 1, :] * taps[tap * pooled : (tap + 1) * pooled]
        low = low_ref[group].astype(f32)
        edge = kernel_ref[0, 0:1, :] * low[14:15] + kernel_ref[0, 1:2, :] * low[15:16]
        row = lax.broadcasted_iota(jnp.int32, total.shape, 0)
        pooled_ref[group] = (total + jnp.where(row == 0, edge, 0.0)).astype(bf16)


def pool(select, kernel, qkv, rows_low, width):
    count, length = qkv.shape[:2]
    groups = width // LANES
    return pl.pallas_call(
        pool_kernel,
        grid=(2 * groups,),
        in_specs=[
            pl.BlockSpec(select.shape, lambda j: (0, 0)),
            pl.BlockSpec((1, 8, LANES), lambda j: (j // groups, 0, j % groups)),
            pl.BlockSpec((count, length, LANES), lambda j: (0, 0, j + groups)),
            pl.BlockSpec((count, 16, LANES), lambda j: (0, WIN // 16 - 1, j)),
        ],
        out_specs=pl.BlockSpec((count, length // 4, LANES), lambda j: (0, 0, j)),
        out_shape=jax.ShapeDtypeStruct((count, length // 4, 2 * width), bf16),
        compiler_params=pltpu.CompilerParams(vmem_limit_bytes=VMEM_LIMIT),
        cost_estimate=pl.CostEstimate(
            flops=count * length * width * 1300, bytes_accessed=2500000, transcendentals=0
        ),
        name="pool",
    )(select, kernel, qkv, rows_low)


def pool_messages_kernel(select_ref, kernel_ref, rows_ref, up_ref, down_ref, head_ref):
    pooled = up_ref.shape[1] - WIN
    length = rows_ref.shape[1]
    for group in range(rows_ref.shape[0]):
        taps = dot_nn(select_ref[...], rows_ref[group])
        total = kernel_ref[0, 0:1, :] * taps[:pooled]
        for tap in range(1, TAPS):
            total = total + kernel_ref[0, tap : tap + 1, :] * taps[tap * pooled : (tap + 1) * pooled]
        head_ref[group] = total[:16]
        total = total.astype(bf16)
        up_ref[group, :WIN] = rows_ref[group, length - WIN :]
        up_ref[group, WIN:] = total
        down_ref[group, :WIN] = rows_ref[group, :WIN]
        down_ref[group, WIN:] = total


def pool_messages(select, kernel, qkv, width):
    count, length = qkv.shape[:2]
    groups = width // LANES

    def spec(rows):
        return pl.BlockSpec((count, rows, LANES), lambda j: (0, 0, j))

    message = jax.ShapeDtypeStruct((count, WIN + length // 4, 2 * width), bf16)
    return pl.pallas_call(
        pool_messages_kernel,
        grid=(2 * groups,),
        in_specs=[
            pl.BlockSpec(select.shape, lambda j: (0, 0)),
            pl.BlockSpec((1, 8, LANES), lambda j: (j // groups, 0, j % groups)),
            pl.BlockSpec((count, length, LANES), lambda j: (0, 0, j + groups)),
        ],
        out_specs=[spec(WIN + length // 4), spec(WIN + length // 4), spec(16)],
        out_shape=[message, message, jax.ShapeDtypeStruct((count, 16, 2 * width), f32)],
        compiler_params=pltpu.CompilerParams(vmem_limit_bytes=VMEM_LIMIT),
        cost_estimate=pl.CostEstimate(
            flops=count * length * width * 1300, bytes_accessed=2500000, transcendentals=0
        ),
        name="pool_messages",
    )(select, kernel, qkv)


def pool_join_kernel(kernel_ref, head_ref, mine_ref, tail_ref, low_ref, second_ref, up_ref,
                     out_low_ref, out_ref, out_up_ref):
    first, last = kernel_ref[0, 0:1, :], kernel_ref[0, 1:2, :]
    row = lax.broadcasted_iota(jnp.int32, (16, LANES), 0)

    def completed(block, before):
        before = before.astype(f32)
        edge = first * before[14:15] + last * before[15:16]
        return (block + jnp.where(row == 0, edge, 0.0)).astype(bf16)

    for group in range(mine_ref.shape[0]):
        out_low_ref[group] = low_ref[group, WIN:]
        out_ref[group] = mine_ref[group]
        out_up_ref[group] = up_ref[group, WIN:]
        out_low_ref[group, :16] = completed(
            low_ref[group, WIN : WIN + 16].astype(f32), second_ref[group]
        )
        out_ref[group, :16] = completed(head_ref[group], low_ref[group, WIN - 16 : WIN])
        out_up_ref[group, :16] = completed(
            up_ref[group, WIN : WIN + 16].astype(f32), tail_ref[group]
        )


def pool_join(kernel, head, own_message, qkv, from_low, second, from_up, width):
    count, length = qkv.shape[:2]
    groups = width // LANES
    pooled = length // 4

    def spec(rows, at=0, shift=0):
        return pl.BlockSpec((count, rows, LANES), lambda j: (0, at, j + shift))

    out = jax.ShapeDtypeStruct((count, pooled, 2 * width), bf16)
    return pl.pallas_call(
        pool_join_kernel,
        grid=(2 * groups,),
        in_specs=[
            pl.BlockSpec((1, 8, LANES), lambda j: (j // groups, 0, j % groups)),
            spec(16), spec(pooled, WIN // pooled), spec(16, length // 16 - 1, groups),
            spec(WIN + pooled), spec(16), spec(WIN + pooled),
        ],
        out_specs=[spec(pooled)] * 3,
        out_shape=[out] * 3,
        compiler_params=pltpu.CompilerParams(vmem_limit_bytes=VMEM_LIMIT),
        cost_estimate=pl.CostEstimate(flops=0, bytes_accessed=5000000, transcendentals=0),
        name="pool_join",
    )(kernel, head, own_message, qkv, from_low, second, from_up)


def pool_back_kernel(select_ref, spread_ref, kernel_ref, rows_ref, low_rows_ref, own_ref, pool_ref,
                     low_ref, up_ref, *rest):
    *rims, grad_ref, tail_ref, taps_ref = rest if len(rest) == 3 else (*rest[:3], None, rest[3])
    pooled = pool_ref.shape[2]
    length = rows_ref.shape[1]
    tap_row = lax.broadcasted_iota(jnp.int32, (8, LANES), 0)
    tail_row = lax.broadcasted_iota(jnp.int32, (16, LANES), 0)
    taps_total = jnp.zeros((8, LANES), f32)
    for group in range(rows_ref.shape[0]):
        grads = pool_ref[0, group] + low_ref[0, group, WIN : WIN + pooled].astype(f32)
        grads = (grads + up_ref[0, group, WIN : WIN + pooled].astype(f32)).astype(bf16).astype(f32)
        taps = dot_nn(select_ref[...], rows_ref[group])
        low_rows = low_rows_ref[group].astype(f32)
        edge = grads[0:1]
        spread = []
        for tap in range(TAPS):
            line = jnp.sum(grads * taps[tap * pooled : (tap + 1) * pooled], axis=0, keepdims=True)
            if tap < 2:
                line = line + edge * low_rows[14 + tap : 15 + tap]
            taps_total = taps_total + jnp.where(tap_row == tap, line, 0.0)
            spread.append(grads * kernel_ref[0, tap : tap + 1, :])
        spread = jnp.concatenate(spread, axis=0)
        high = spread.astype(bf16)
        rest = (spread - high.astype(f32)).astype(bf16)
        total = own_ref[0, group] + dot_nn(spread_ref[...], high) + dot_nn(spread_ref[...], rest)
        first, last = kernel_ref[0, 0:1, :], kernel_ref[0, 1:2, :]
        if rims:
            mine_ref, second_ref = rims
            edge = up_ref[0, group, WIN + pooled : WIN + pooled + 1].astype(f32)
            edge = edge + mine_ref[0, group, 0:1].astype(f32) + second_ref[0, group, 0:1].astype(f32)
            edge = edge.astype(bf16).astype(f32)
        tail = jnp.where(tail_row == 14, edge * first, 0.0)
        tail = tail + jnp.where(tail_row == 15, edge * last, 0.0)
        kind = grad_ref.dtype
        upper = total[length - WIN :] + up_ref[0, group, :WIN].astype(f32)
        if length > 2 * WIN:
            grad_ref[0, group, WIN : length - WIN] = total[WIN : length - WIN].astype(kind)
        grad_ref[0, group, :WIN] = (total[:WIN] + low_ref[0, group, :WIN].astype(f32)).astype(kind)
        if rims:
            grad_ref[0, group, length - WIN : length - 16] = upper[: WIN - 16].astype(kind)
            grad_ref[0, group, length - 16 :] = (upper[WIN - 16 :] + tail).astype(kind)
        else:
            grad_ref[0, group, length - WIN :] = upper.astype(kind)
            tail_ref[0, group] = tail.astype(bf16)
    taps_ref[0] = taps_total


def pool_back(select, kernel, qkv, rows_low, own, pooled_own, from_low, from_up, rim_up, second):
    count, length, width = own.shape[1:]
    groups = width // LANES
    pooled = length // 4

    def pair_spec(rows):
        return pl.BlockSpec((1, count, rows, LANES), lambda j: (j // groups, 0, 0, j % groups))

    joined = second is not None
    tail_shape = jax.ShapeDtypeStruct((2, count, 16, width), bf16)
    tail_specs, tail_shapes = ([], []) if joined else ([pair_spec(16)], [tail_shape])
    rim_spec = pl.BlockSpec(
        (1, count, 16, LANES), lambda j: (j // groups, 0, WIN // 16, j % groups)
    )
    extra_specs, extra = ([rim_spec, pair_spec(16)], [rim_up, second]) if joined else ([], [])
    return pl.pallas_call(
        pool_back_kernel,
        grid=(2 * groups,),
        in_specs=[
            pl.BlockSpec(select.shape, lambda j: (0, 0)),
            pl.BlockSpec(select.shape[::-1], lambda j: (0, 0)),
            pl.BlockSpec((1, 8, LANES), lambda j: (j // groups, 0, j % groups)),
            pl.BlockSpec((count, length, LANES), lambda j: (0, 0, j + groups)),
            pl.BlockSpec((count, 16, LANES), lambda j: (0, WIN // 16 - 1, j)),
            pair_spec(length), pair_spec(pooled),
            pair_spec(from_low.shape[2]), pair_spec(from_up.shape[2]),
        ] + extra_specs,
        out_specs=[pair_spec(length)] + tail_specs + [
            pl.BlockSpec((1, 8, LANES), lambda j: (j // groups, 0, j % groups)),
        ],
        out_shape=[
            jax.ShapeDtypeStruct((2, count, length, width), bf16 if joined else f32),
            *tail_shapes,
            jax.ShapeDtypeStruct((2, 8, width), f32),
        ],
        compiler_params=pltpu.CompilerParams(vmem_limit_bytes=VMEM_LIMIT),
        cost_estimate=pl.CostEstimate(
            flops=count * length * width * 4000, bytes_accessed=9000000, transcendentals=0
        ),
        name="pool_back",
    )(select, select.T, kernel, qkv, rows_low, own, pooled_own, from_low, from_up, *extra)


def matmul(a, b):
    return jnp.dot(a, b, preferred_element_type=f32)


def matmul_t(a, b):
    return lax.dot_general(a, b, (((1,), (1,)), ((), ())), preferred_element_type=f32)


def weight_grad(a, b):
    return lax.dot_general(a, b, (((0,), (0,)), ((), ())), preferred_element_type=f32)


def normalised(rows):
    centre = rows - jnp.mean(rows, axis=-1, keepdims=True)
    inverse = lax.rsqrt(jnp.mean(centre * centre, axis=-1, keepdims=True) + norm_eps)
    return centre * inverse, inverse


def normalised_back(grads, gain, norm, inverse):
    scaled = grads * gain
    mean = jnp.mean(scaled, axis=-1, keepdims=True)
    inner = jnp.mean(scaled * norm, axis=-1, keepdims=True)
    return (scaled - mean - norm * inner) * inverse


def gelu_both(value):
    square = value * value
    inside = jnp.tanh(value * (gelu_coef + (gelu_coef * 0.044715) * square))
    half = 0.5 * value
    bend = gelu_coef + (3 * 0.044715 * gelu_coef) * square
    return half + half * inside, 0.5 + 0.5 * inside + half * (1.0 - inside * inside) * bend


def small_index():
    return flat_index().reshape(1).astype(jnp.int32)


def place_kernel(blocks, index_ref, mine_ref, other_ref, out_ref):
    half = len(blocks) // 2
    for place, bits in enumerate(blocks):
        source = mine_ref if place < half else other_ref
        out_ref[0, index_ref[0] ^ bits] = source[0, place % half]


def in_place(halves, block_cols, skip=0, take=None):
    blocks = relative_blocks()
    half = len(blocks) // 2
    all_parts, half_rows, cols = halves[0].shape
    parts = take or all_parts
    rows = half_rows // half
    spec = pl.BlockSpec((1, half, rows, block_cols), lambda p, j, index: (p + skip, 0, 0, j))
    whole = pl.pallas_call(
        functools.partial(place_kernel, blocks),
        grid_spec=pltpu.PrefetchScalarGridSpec(
            num_scalar_prefetch=1,
            grid=(parts, cols // block_cols),
            in_specs=[spec, spec],
            out_specs=pl.BlockSpec(
                (1, 2 * half, rows, block_cols), lambda p, j, index: (p, 0, 0, j)
            ),
        ),
        out_shape=jax.ShapeDtypeStruct((parts, 2 * half, rows, cols), halves[0].dtype),
        compiler_params=pltpu.CompilerParams(vmem_limit_bytes=VMEM_LIMIT),
        cost_estimate=pl.CostEstimate(
            flops=0, bytes_accessed=8 * parts * half_rows * cols, transcendentals=0
        ),
        name="in_place",
    )(small_index(), *[h.reshape(all_parts, half, rows, cols) for h in halves])
    return whole.reshape(parts * 2 * half_rows, cols)


def store_blocks(blocks, index, total_ref, keep_ref, give_ref):
    half = len(blocks) // 2
    rows = total_ref.shape[0] // len(blocks)
    for place, bits in enumerate(blocks):
        target = keep_ref if place < half else give_ref
        start = pl.multiple_of((index ^ bits) * rows, 8)
        target[0, place % half] = total_ref[pl.ds(start, rows), :].astype(bf16)


def weight_grads_kernel(blocks, plan, index_ref, *refs):
    operands, (keep_ref, give_ref, total_ref) = refs[:-3], refs[-3:]
    width = total_ref.shape[0]
    for step, (left, left_at, right, right_at) in enumerate(plan):

        @pl.when(pl.program_id(0) == step)
        def _():
            rows = operands[left][:, left_at * width : (left_at + 1) * width]
            grads = operands[right][:, right_at * width : (right_at + 1) * width]
            total_ref[...] = weight_grad(rows, grads)

    store_blocks(blocks, index_ref[0], total_ref, keep_ref, give_ref)


def turned(whole):
    bits = axis_bits()
    cols = whole.shape[1]
    split = whole.reshape((2,) * len(bits) + (-1, cols))
    for place, (axis, step) in enumerate(bits):
        mine = (lax.axis_index(axis) // step) % 2
        split = jnp.where(mine == 1, jnp.flip(split, place), split)
    order = [bits.index(bit) for bit in block_order()]
    split = split.transpose(*order, len(bits), len(bits) + 1)
    return split.reshape(1, 2, -1, cols)


def weight_grads(operands, plan, width, stacked=False):
    blocks = relative_blocks()
    half = len(blocks) // 2
    rows = width // len(blocks)
    count = len(plan)
    if rows % 8:
        pieces = []
        for left, left_at, right, right_at in plan:
            left_rows = operands[left][:, left_at * width : (left_at + 1) * width]
            grads = operands[right][:, right_at * width : (right_at + 1) * width]
            pieces.append(turned(weight_grad(left_rows, grads).astype(bf16)))
        joined = jnp.concatenate(pieces, axis=0 if stacked else 3)
        return joined[:, 0], joined[:, 1]
    if stacked:
        shape, spec = (count, half, rows, width), lambda j, index: (j, 0, 0, 0)
    else:
        shape, spec = (1, half, rows, count * width), lambda j, index: (0, 0, 0, j)
    out = jax.ShapeDtypeStruct(shape, bf16)
    spec = pl.BlockSpec((1, half, rows, width), spec)
    tokens = operands[0].shape[0]
    pair = pl.pallas_call(
        functools.partial(weight_grads_kernel, blocks, plan),
        grid_spec=pltpu.PrefetchScalarGridSpec(
            num_scalar_prefetch=1,
            grid=(count,),
            in_specs=[pl.BlockSpec(a.shape, lambda j, index: (0, 0)) for a in operands],
            out_specs=[spec, spec],
            scratch_shapes=[pltpu.VMEM((width, width), f32)],
        ),
        out_shape=[out, out],
        compiler_params=pltpu.CompilerParams(vmem_limit_bytes=VMEM_LIMIT),
        cost_estimate=pl.CostEstimate(
            flops=2 * tokens * width * width * count,
            bytes_accessed=2 * sum(a.size for a in operands) + 2 * count * width * width,
            transcendentals=0,
        ),
        name="weight_grads",
    )(small_index(), *operands)
    return [side.reshape(shape[0], half * rows, shape[3]) for side in pair]


ROWS = 128
EDGES = ("output_bias", "down_bias", "mixer_gain", "mixer_shift", "feed_gain", "feed_shift")


def by_rows(count, body, rows=ROWS):
    for first in range(0, count, rows):
        body(slice(first, first + rows))


def feed_kernel(x_ref, mixed_ref, vectors_ref, bias_ref, out_ref, up_ref, down_ref,
                norm_ref, inverse_ref, low_ref, act_ref, slope_ref, norm_two_ref, inverse_two_ref,
                y_ref, hidden_ref, total_ref):
    step, last = pl.program_id(0), pl.num_programs(0) - 1
    count = x_ref.shape[0]

    def vector(name):
        at = EDGES.index(name)
        return vectors_ref[at : at + 1, :]

    @pl.when(step == 0)
    def _():
        total_ref[...] = dot_nn(mixed_ref[...], out_ref[...])

        def body(at):
            norm, inverse = normalised(x_ref[at, :] + total_ref[at, :] + vector("output_bias"))
            hidden = norm * vector("mixer_gain") + vector("mixer_shift")
            norm_ref[at, :], inverse_ref[at, :] = norm, inverse
            hidden_ref[at, :] = hidden
            low_ref[at, :] = hidden.astype(bf16)
            total_ref[at, :] = jnp.zeros_like(hidden)

        by_rows(count, body)

    def units(at):
        act, slope = gelu_both(dot_nn(low_ref[at, :], up_ref[...]) + bias_ref[...])
        act = act.astype(bf16)
        act_ref[at, :], slope_ref[at, :] = act, slope.astype(bf16)
        total_ref[at, :] += dot_nn(act, down_ref[...])

    by_rows(count, units, 256)

    @pl.when(step == last)
    def _():
        def body(at):
            rows = hidden_ref[at, :] + total_ref[at, :] + vector("down_bias")
            norm, inverse = normalised(rows)
            norm_two_ref[at, :], inverse_two_ref[at, :] = norm, inverse
            y_ref[at, :] = norm * vector("feed_gain") + vector("feed_shift")

        by_rows(count, body)


def feed_forward(x, mixed, small, feed, ratio):
    out_weight, out_at, whole, up_at = feed
    count, width = x.shape
    rows = pl.BlockSpec((count, width), lambda j: (0, 0))
    line = pl.BlockSpec((count, 1), lambda j: (0, 0))
    part = pl.BlockSpec((count, width), lambda j: (0, j))

    def weight(shift, moves):
        return pl.BlockSpec((width, width), lambda j: (0, shift + moves * j))

    def shape(cols, kind):
        return jax.ShapeDtypeStruct((count, cols), kind)

    return pl.pallas_call(
        feed_kernel,
        grid=(ratio,),
        in_specs=[
            rows, rows, pl.BlockSpec((8, width), lambda j: (0, 0)),
            pl.BlockSpec((1, width), lambda j: (0, j)),
            weight(out_at, 0), weight(up_at, 1), weight(up_at + ratio, 1),
        ],
        out_specs=[rows, line, rows, part, part, rows, line, rows],
        out_shape=[
            shape(width, f32), shape(1, f32), shape(width, bf16), shape(ratio * width, bf16),
            shape(ratio * width, bf16), shape(width, f32), shape(1, f32), shape(width, f32),
        ],
        scratch_shapes=[pltpu.VMEM((count, width), f32)] * 2,
        compiler_params=pltpu.CompilerParams(vmem_limit_bytes=VMEM_LIMIT),
        cost_estimate=pl.CostEstimate(
            flops=2 * count * width * width * (1 + 2 * ratio), transcendentals=count * width * ratio,
            bytes_accessed=2 * whole.size + 4 * count * width * ratio + 20 * count * width,
        ),
        name="feed_forward",
    )(x, mixed, small["vectors"], small["up_bias"], out_weight, whole, whole)


def feed_back_kernel(blocks, index_ref, grads_ref, norm_ref, inverse_ref, norm_two_ref,
                     inverse_two_ref, vectors_ref, low_ref, act_ref, slope_ref, out_ref, up_ref,
                     down_ref, one_ref, attention_ref, mixed_ref, sums_ref, bias_ref, *rest):
    outs, (feed_ref, hidden_ref, total_ref, pre_ref, turn_ref) = rest[:-5], rest[-5:]
    step, last = pl.program_id(0), pl.num_programs(0) - 1
    count, width = grads_ref.shape

    def vector(name):
        at = EDGES.index(name)
        return vectors_ref[at : at + 1, :]

    def add(name, rows):
        at = EDGES.index(name)
        sums_ref[at : at + 1, :] += jnp.sum(rows, axis=0, keepdims=True)

    def store(pair):
        if blocks is None:
            pair[0][0] = total_ref[...].astype(bf16)
        else:
            store_blocks(blocks, index_ref[0], total_ref, *pair)

    @pl.when(step == 0)
    def _():
        sums_ref[...] = jnp.zeros_like(sums_ref)
        turn_ref[...] = jnp.transpose(low_ref[...])

        def body(at):
            grads, norm = grads_ref[at, :], norm_two_ref[at, :]
            add("feed_gain", grads * norm)
            add("feed_shift", grads)
            back = normalised_back(grads, vector("feed_gain"), norm, inverse_two_ref[at, :])
            hidden_ref[at, :] = back
            back = back.astype(bf16)
            feed_ref[at, :] = back
            add("down_bias", back.astype(f32))

        by_rows(count, body)

    pre_ref[...] = (
        slope_ref[...].astype(f32) * dot_nt(feed_ref[...], down_ref[...])
    ).astype(bf16)
    bias_ref[...] = jnp.sum(pre_ref[...].astype(f32), axis=0, keepdims=True)
    hidden_ref[...] += dot_nt(pre_ref[...], up_ref[...])
    total_ref[...] = weight_grad(act_ref[...], feed_ref[...])
    store(outs[: len(outs) // 2])
    total_ref[...] = dot_nn(turn_ref[...], pre_ref[...])
    store(outs[len(outs) // 2 :])

    @pl.when(step == last)
    def _():
        def body(at):
            grads, norm = hidden_ref[at, :], norm_ref[at, :]
            add("mixer_gain", grads * norm)
            add("mixer_shift", grads)
            back = normalised_back(grads, vector("mixer_gain"), norm, inverse_ref[at, :])
            one_ref[at, :] = back
            back = back.astype(bf16)
            attention_ref[at, :] = back
            add("output_bias", back.astype(f32))

        by_rows(count, body)
        mixed_ref[...] = dot_nt(attention_ref[...], out_ref[...]).astype(bf16)


def feed_back(grads, kept, small, feed, ratio):
    norm, inverse, low, act, slope, norm_two, inverse_two = kept
    out_weight, out_at, whole, up_at = feed
    count, width = grads.shape
    blocks = relative_blocks()
    half = len(blocks) // 2
    shard = width // len(blocks)
    rows = pl.BlockSpec((count, width), lambda j, index: (0, 0))
    line = pl.BlockSpec((count, 1), lambda j, index: (0, 0))
    part = pl.BlockSpec((count, width), lambda j, index: (0, j))
    edge = pl.BlockSpec((8, width), lambda j, index: (0, 0))

    def weight(shift, moves):
        return pl.BlockSpec((width, width), lambda j, index: (0, shift + moves * j))

    if shard % 8:
        blocks = None
        out = [jax.ShapeDtypeStruct((ratio, width, width), bf16)] * 2
        specs = [pl.BlockSpec((1, width, width), lambda j, index: (j, 0, 0))] * 2
    else:
        block = (1, half, shard, width)
        out = [jax.ShapeDtypeStruct((ratio, half, shard, width), bf16)] * 2
        out += [jax.ShapeDtypeStruct((1, half, shard, ratio * width), bf16)] * 2
        specs = [pl.BlockSpec(block, lambda j, index: (j, 0, 0, 0))] * 2
        specs += [pl.BlockSpec(block, lambda j, index: (0, 0, 0, j))] * 2
    results = pl.pallas_call(
        functools.partial(feed_back_kernel, blocks),
        grid_spec=pltpu.PrefetchScalarGridSpec(
            num_scalar_prefetch=1,
            grid=(ratio,),
            in_specs=[
                rows, rows, line, rows, line, edge, rows, part, part,
                weight(out_at, 0), weight(up_at, 1), weight(up_at + ratio, 1),
            ],
            out_specs=[
                rows, rows, rows, edge, pl.BlockSpec((1, width), lambda j, index: (0, j)), *specs
            ],
            scratch_shapes=[
                pltpu.VMEM((count, width), bf16), pltpu.VMEM((count, width), f32),
                pltpu.VMEM((width, width), f32), pltpu.VMEM((count, width), bf16),
                pltpu.VMEM((width, count), bf16),
            ],
        ),
        out_shape=[
            jax.ShapeDtypeStruct((count, width), f32), jax.ShapeDtypeStruct((count, width), bf16),
            jax.ShapeDtypeStruct((count, width), bf16), jax.ShapeDtypeStruct((8, width), f32),
            jax.ShapeDtypeStruct((1, ratio * width), f32), *out,
        ],
        compiler_params=pltpu.CompilerParams(vmem_limit_bytes=VMEM_LIMIT),
        cost_estimate=pl.CostEstimate(
            flops=2 * count * width * width * (1 + 4 * ratio), transcendentals=0,
            bytes_accessed=4 * whole.size + 4 * count * width * ratio + 20 * count * width,
        ),
        name="feed_back",
    )(small_index(), grads, norm, inverse, norm_two, inverse_two, small["vectors"], low, act, slope,
      out_weight, whole, whole)
    one, attention_low, grad_mixed, sums, up_sums, *out = results
    if blocks is None:
        down = [turned(out[0][i]) for i in range(ratio)]
        down = [jnp.concatenate([d[:, side] for d in down]) for side in range(2)]
        up = [turned(out[1][i]) for i in range(ratio)]
        up = [jnp.concatenate([u[:, side] for u in up], axis=2) for side in range(2)]
    else:
        down = [side.reshape(ratio, half * shard, width) for side in out[:2]]
        up = [side.reshape(1, half * shard, ratio * width) for side in out[2:]]
    return one, attention_low, grad_mixed, sums, up_sums, down, up


def units_back_kernel(spread_ref, *refs):
    parts, out_ref = refs[:-1], refs[-1]
    total = None
    for part, rows_ref in enumerate(parts):
        left = rows_ref[...]
        for _ in range(3):
            piece = left.astype(bf16)
            left = left - piece.astype(f32)
            term = dot_nn(piece, spread_ref[part])
            total = term if total is None else total + term
    out_ref[...] = total


def units_back(rows, ratio, shard_rows):
    count, cols = rows.shape
    block = cols // ratio // 2
    source = jnp.arange(block, dtype=jnp.int32)
    target = jnp.arange(ratio * block, dtype=jnp.int32)
    device, rest = target // (ratio * shard_rows), target % (ratio * shard_rows)
    wanted = device * shard_rows + rest % shard_rows
    spread = jnp.stack([
        (source[:, None] == wanted[None, :]) & (rest[None, :] // shard_rows == part)
        for part in range(ratio)
    ]).astype(bf16)
    return pl.pallas_call(
        units_back_kernel,
        grid=(2,),
        in_specs=[pl.BlockSpec(spread.shape, lambda j: (0, 0, 0))] + [
            pl.BlockSpec((count, block), functools.partial(lambda part, j: (0, 2 * part + j), part))
            for part in range(ratio)
        ],
        out_specs=pl.BlockSpec((count, ratio * block), lambda j: (0, j)),
        out_shape=jax.ShapeDtypeStruct((count, cols), f32),
        compiler_params=pltpu.CompilerParams(vmem_limit_bytes=VMEM_LIMIT),
        name="units_back",
    )(spread, *[rows] * ratio)


SMALL_COLUMNS = 128


def small_grads_kernel(blocks, layers, index_ref, *refs):
    sources, (keep_ref, give_ref, lines_ref, columns_ref) = refs[:-4], refs[-4:]
    lines_ref[...] = jnp.zeros_like(lines_ref)
    width = lines_ref.shape[1]
    each = len(sources) // layers
    at = 0
    for layer in range(layers):
        query_ref, value_ref, sums_ref, up_ref, taps_ref = sources[layer * each : (layer + 1) * each]
        lines_ref[at : at + 1, :] = query_ref[...]
        lines_ref[at + 1 : at + 2, :] = value_ref[...]
        lines_ref[at + 2 : at + 2 + len(EDGES), :] = sums_ref[: len(EDGES), :]
        at += 2 + len(EDGES)
        for kind in range(2):
            lines_ref[at : at + TAPS, :] = taps_ref[kind, :TAPS]
            at += TAPS
        for part in range(up_ref.shape[1] // width):
            lines_ref[at : at + 1, :] = up_ref[:, part * width : (part + 1) * width]
            at += 1
    columns_ref[...] = jnp.transpose(lines_ref[...])
    store_blocks(blocks, index_ref[0], columns_ref, keep_ref, give_ref)


def small_grads(per_layer, width):
    blocks = relative_blocks()
    half = len(blocks) // 2
    rows = width // len(blocks)
    if rows % 8:
        lines = []
        for query, value, sums, up, taps in per_layer:
            lines += [query, value, sums[: len(EDGES)], taps[0, :TAPS], taps[1, :TAPS]]
            lines.append(up.reshape(-1, width))
        lines = jnp.concatenate(lines, axis=0)
        lines = jnp.pad(lines, ((0, SMALL_COLUMNS - lines.shape[0]), (0, 0))).T.astype(bf16)
        lines = turned(lines)
        return lines[:, 0], lines[:, 1]
    flat = [a for arrays in per_layer for a in arrays]
    out = jax.ShapeDtypeStruct((1, half, rows, SMALL_COLUMNS), bf16)
    pair = pl.pallas_call(
        functools.partial(small_grads_kernel, blocks, len(per_layer)),
        in_specs=[pl.BlockSpec(memory_space=pltpu.SMEM)]
        + [pl.BlockSpec(memory_space=pltpu.VMEM)] * len(flat),
        out_specs=[pl.BlockSpec(memory_space=pltpu.VMEM)] * 2,
        out_shape=[out, out],
        scratch_shapes=[pltpu.VMEM((SMALL_COLUMNS, width), f32), pltpu.VMEM((width, SMALL_COLUMNS), f32)],
        compiler_params=pltpu.CompilerParams(vmem_limit_bytes=VMEM_LIMIT),
        name="small_grads",
    )(small_index(), *flat)
    return [side.reshape(1, half * rows, SMALL_COLUMNS) for side in pair]


def layer_forward(x, weights, masks, select, count, at):
    qkv_weight, feed_weights, small = weights
    width = x.shape[1]
    length = x.shape[0] // count
    x_low = x.astype(bf16)
    bias = jnp.concatenate([small["query_bias"], jnp.zeros((width,), f32), small["value_bias"]])
    qkv = matmul(x_low, qkv_weight)
    qkv = at("projected", (qkv + bias).astype(bf16).reshape(count, length, -1))
    if pooled_hops(length // 4) == 1 and length // 4 == WIN:
        up_message, down_message, head = pool_messages(select, small["taps"], qkv, width)
        rows_low, rows_up, second = tied([
            passed_along(up_message, 1), passed_along(down_message, -1),
            passed_along(qkv[:, length - 16 :, width:], 2),
        ])
        rows_low = at("pooled", rows_low)
        pooled_low, pooled, pooled_up = pool_join(
            small["taps"], head, up_message, qkv, rows_low, second, rows_up, width
        )
    else:
        rows_low = passed_along(qkv[:, length - WIN :, width:], 1)
        rows_up = passed_along(qkv[:, :WIN, width:], -1)
        pooled = at("pooled", pool(select, small["taps"], qkv, rows_low, width))
        pooled_low, pooled_up = pooled_rims(pooled)
    pooled_up = at("attending", pooled_up)
    operands = attend_operands(qkv, rows_low, rows_up, pooled, pooled_low, pooled_up)
    mixed, stats = attend(masks, operands, width)
    mixed = at("attended", mixed.reshape(count * length, width))
    ratio = small["up_bias"].shape[1] // width
    norm, inverse, hidden_low, act_low, slope, norm_two, inverse_two, y = feed_forward(
        x, mixed, small, feed_weights, ratio
    )
    y = at("fed", y)
    kept = (x_low, operands, stats, mixed, (norm, inverse, hidden_low, act_low, slope, norm_two, inverse_two))
    return y, kept


def layer_backward(grads, kept, weights, masks, select, count, at):
    qkv_weight, feed_weights, small = weights
    x_low, operands, stats, mixed, feed_kept = kept
    rows, width = grads.shape
    length = rows // count
    ratio = small["up_bias"].shape[1] // width

    def total(value):
        return jnp.sum(value.astype(f32), axis=0, keepdims=True)

    grad_one, attention_low, grad_mixed, sums, up_sums, down_halves, up_halves = feed_back(
        grads, feed_kept, small, feed_weights, ratio
    )
    grad_mixed = at("attending", grad_mixed, (down_halves, up_halves))
    grad_mixed = grad_mixed.reshape(count, length, width)
    part = max(count // 2, 1)
    pieces = list(attend_back(masks, stats, grad_mixed, operands, 0, part))
    if part < count:
        pieces[0] = at("halfway", pieces[0])
        pieces = attend_back(masks, stats, grad_mixed, operands, part, count - part, pieces)
    grad_query, own, pooled_own, rim_low, rim_up = pieces
    rim_up = at("rims", rim_up)
    grad_query = grad_query.reshape(rows, width)
    from_low, from_up, second, pooled_own = rims_return(rim_low, rim_up, pooled_own)
    own, *tail, taps = pool_back(
        select, small["taps"], operands[0], operands[3], own, pooled_own, from_low, from_up,
        rim_up, second,
    )
    if tail:
        tail = passed_along(tail[0], -1).astype(f32)
        own = own + jnp.pad(tail, ((0, 0), (0, 0), (length - 16, 0), (0, 0)))
    own = at("pooled", own, (x_low, grad_query, mixed, attention_low))
    own = own.astype(bf16).reshape(2, rows, width)
    grad_qkv = (grad_query, own[0], own[1])
    grad_x = grad_one + matmul_t(jnp.concatenate(grad_qkv, axis=1), qkv_weight)
    small_sums = [total(grad_query), total(own[1]), sums, up_sums, taps]
    return grad_x, (x_low, *grad_qkv, mixed, attention_low), small_sums


def pack_small(vectors, up_biases, taps):
    columns = []
    for layer in range(vectors[0].shape[0]):
        rows = vectors[0].shape[1]
        columns.append(jnp.stack([v[layer] for v in vectors]))
        columns.append(taps[0][layer])
        columns.append(taps[1][layer])
        columns.append(up_biases[layer].reshape(-1, rows))
    packed = jnp.concatenate(columns, axis=0)
    return jnp.pad(packed, ((0, SMALL_COLUMNS - packed.shape[0]), (0, 0))).T


def unpack_small(columns, layers, ratio):
    width = columns.shape[0]
    lines = columns.astype(f32).T
    per_layer = 8 + 2 * TAPS + ratio
    pad = ((0, 8 - TAPS), (0, 0))
    result = []
    for layer in range(layers):
        piece = lines[layer * per_layer : (layer + 1) * per_layer]
        result.append({
            "query_bias": piece[0],
            "value_bias": piece[1],
            "vectors": piece[2:10],
            "taps": jnp.stack([
                jnp.pad(piece[8 : 8 + TAPS], pad), jnp.pad(piece[8 + TAPS : 8 + 2 * TAPS], pad),
            ]),
            "up_bias": piece[8 + 2 * TAPS :].reshape(1, ratio * width),
        })
    return result


def on_device(
    tokens, cotangent, masked, query_weight, key_weight, value_weight, output_weight, up_weight,
    down_weight, query_bias, value_bias, output_bias, up_bias, down_bias, mixer_gain, mixer_shift,
    feed_gain, feed_shift, pool_key, pool_value,
):
    micro, seqs, length, width = tokens.shape
    count = micro * seqs
    layers = query_weight.shape[0]
    devices = lax.axis_size("seq") * lax.axis_size("batch")
    shard_rows = width // devices
    small_shard = pack_small(
        (query_bias, value_bias, output_bias, down_bias, mixer_gain, mixer_shift, feed_gain,
         feed_shift), up_bias, (pool_key, pool_value),
    )
    masks = window_masks(length)
    select = tap_select(length)
    ratio = up_weight.shape[2] // width

    def units_apart(rows):
        split = rows.reshape(rows.shape[0], devices, ratio, shard_rows)
        return split.transpose(0, 2, 1, 3).reshape(rows.shape)

    shard = jnp.concatenate(
        [query_weight[0], key_weight[0], value_weight[0], small_shard], axis=1
    )
    first = Gather(shard[None], path("y"))

    later = [
        Gather(jnp.concatenate(
            [query_weight[layer], key_weight[layer], value_weight[layer], output_weight[layer]],
            axis=1,
        )[None], path("x"))
        for layer in range(1, layers)
    ]
    x = tokens.reshape(count * length, width).astype(f32)
    feeds = []

    def gather_feed(layer, after):
        out, up, down, after = tied(
            [output_weight[layer], up_weight[layer], down_weight[layer], after]
        )
        parts = [units_apart(up), *down.reshape(ratio, shard_rows, width)]
        shard = jnp.concatenate([out] * (layer == 0) + parts, axis=1)
        feeds.append(lax.all_gather(shard, ("seq", "batch"), axis=0, tiled=True))
        return after

    x = checkpoint(x, [], [first])
    x = gather_feed(0, checkpoint(x, [first]))
    while first.left > 2:
        x = checkpoint(x, [first])
    x = checkpoint(x, [], later)
    for layer in range(1, layers):
        x = gather_feed(layer, x)
    if later:
        x = checkpoint(x, later)
        x = checkpoint(x, later, [], later)
    x = checkpoint(x, [first])
    x = checkpoint(x, [first])
    first_whole = in_place(first.halves, first.cols)
    smalls = unpack_small(first_whole[:, 3 * width :], layers, ratio)

    def landed(value, flows, left):
        while True:
            behind = [flow for flow in flows if flow.left > left]
            if not behind:
                return value
            value = checkpoint(value, behind)

    def forward_at(layer):
        following = later[layer : layer + 1]

        def at(name, value):
            if name == "pooled":
                return checkpoint(value, [], following)
            if name == "attended":
                return checkpoint(value, following)
            if name == "fed":
                return landed(value, following, 0)
            return value

        return at

    states, weights = [], []
    for layer in range(layers):
        if layer == 0:
            qkv_weight = first_whole[:, : 3 * width]
        else:
            qkv_weight = in_place(later[layer - 1].halves, width)
        feed = (feeds[0], 0, feeds[0], 1) if layer == 0 else (qkv_weight, 3, feeds[layer], 0)
        whole = (qkv_weight[:, : 3 * width], feed, smalls[layer])
        x, kept = layer_forward(x, whole, masks, select, count, forward_at(layer))
        states.append(kept)
        weights.append(whole)
    layer_output = x.astype(bf16).reshape(tokens.shape)
    grads = cotangent.astype(f32) * masked.astype(f32)[..., None]
    grads = grads.reshape(count * length, width)
    flows = {}
    plans = {
        "down": ["rims", "next attending", "next halfway", "next rims", "never"],
        "up": ["rims", "next attending", "next halfway", "next rims", "never"],
        "in": ["next attending", "next rims", "never"],
        "query": ["never"],
    }
    last_plans = {
        "down": ["halfway", "rims", "never"],
        "up": ["halfway", "rims", "never"],
    }
    waiting = []

    def due(layer, name):
        result = []
        for (kind, owner), flow in flows.items():
            plan = last_plans[kind] if owner == 0 and kind in last_plans else plans[kind]
            when = plan[min(flow.stage, len(plan) - 1)]
            if flow.done or flow in waiting:
                continue
            if when == ("next " if owner > layer else "") + name or owner > layer + 1:
                result.append(flow)
        return result

    def backward_at(layer):
        def at(name, value, given=None):
            landing, begin = due(layer, name), []
            if name == "attending":
                for kind, halves, last in zip(("down", "up"), given, "yx"):
                    flows[kind, layer] = Scatter(halves, path(last)[::-1])
                    begin.append(flows[kind, layer])
            if name == "pooled" and layer == 0:
                plan = [(0, 0, 1, 0), (2, 0, 3, 0)]
                flow = Scatter(weight_grads(given, plan, width), path("z")[::-1])
                flows["query", layer] = flow
            if name in ("rims", "pooled"):
                waiting.extend(flow for flow in landing if len(flow.order) - flow.stage > 2)
            return checkpoint(value, landing, [] if name == "pooled" else begin, waiting)

        return at

    small_sums = [None] * layers
    for layer in reversed(range(layers)):
        grads, given, small_sums[layer] = layer_backward(
            grads, states[layer], weights[layer], masks, select, count, backward_at(layer)
        )
        if layer > 0:
            plan = [(0, 0, 1 + i, 0) for i in range(3)] + [(4, 0, 5, 0)]
            flow = Scatter(weight_grads(given, plan, width), path("z")[::-1])
            flows["in", layer] = flow
            grads = checkpoint(grads, due(layer, "end"), [flow] + waiting)
            waiting.clear()
    halves = weight_grads((given[0], *given[2:4]), [(0, 0, 1, 0), (0, 0, 2, 0)], width)
    sides = small_grads(small_sums, width)
    joined = [jnp.concatenate(parts, axis=2) for parts in zip(halves, sides)]
    last = Scatter(joined, path("x")[::-1])
    flows["last", 0] = last
    ends = [last, flows["query", 0]]
    marker = checkpoint(last.keep[:1, :1, :1], [], ends)
    marker = checkpoint(marker, ends, waiting)
    while True:
        ends = [flow for flow in ends if not flow.done]
        others = [flow for flow in flows.values() if not flow.done and flow not in ends]
        if not ends + others:
            break
        if ends:
            marker = checkpoint(marker, ends)
        if others:
            marker = checkpoint(marker, others)
    totals = []
    for layer in range(layers):
        if layer > 0:
            whole = flows["in", layer].total[0]
            parts = [whole[:, i * width : (i + 1) * width] for i in range(4)]
        else:
            whole = flows["query", 0].total[0]
            end = last.total[0]
            parts = [whole[:, :width], end[:, :width], end[:, width : 2 * width], whole[:, width:]]
        parts.append(flows["up", layer].total[0])
        parts.append(flows["down", layer].total.reshape(ratio * shard_rows, width))
        totals.append(parts)
    up_totals = units_back(
        jnp.concatenate([parts[4] for parts in totals]), ratio, shard_rows
    ).reshape(layers, shard_rows, ratio * width)
    input_grad = grads.astype(bf16).reshape(tokens.shape)
    lines = last.total[0, :, 2 * width :].T
    per_layer = 8 + 2 * TAPS + ratio
    lines = lines[: layers * per_layer].reshape(layers, per_layer, shard_rows)
    vectors = [lines[:, i] for i in range(8)]
    after = 8 + 2 * TAPS
    grad_up_bias = lines[:, after:].reshape(layers, -1)
    return (
        layer_output, input_grad,
        *[jnp.stack([t[i] for t in totals]) if i != 4 else up_totals for i in range(6)],
        vectors[0], vectors[1], vectors[2], grad_up_bias, *vectors[3:],
        lines[:, 8 : 8 + TAPS], lines[:, 8 + TAPS : after],
    )


def solution(mesh):
    rows = P(None, "batch", "seq", None)
    matrix = P(None, ("seq", "batch"), None)
    vector = P(None, ("seq", "batch"))
    taps = P(None, None, ("seq", "batch"))
    params = (matrix,) * 6 + (vector,) * 9 + (taps,) * 2
    return jax.shard_map(
        on_device,
        mesh=mesh,
        in_specs=(rows, rows, P(None, "batch", "seq")) + params,
        out_specs=(rows, rows) + params,
        check_vma=False,
    )
```

```python
import functools

import jax
import jax.numpy as jnp
from jax import lax
from jax.experimental import pallas as pl
from jax.experimental.pallas import tpu as pltpu
from jax.sharding import PartitionSpec as P

HEADS = 12
WIN = 64
PWIN = 256
TAPS = 5
REACH = PWIN // 4
QROWS = 128
norm_eps = 1e-05
gelu_coef = 0.7978845608028654
masked_score = -1e30
f32 = jnp.float32
bf16 = jnp.bfloat16
VMEM_LIMIT = 48 * 1024 * 1024


def axis_bits():
    bits = []
    for axis in ("seq", "batch"):
        step = lax.axis_size(axis) // 2
        while step:
            bits.append((axis, step))
            step //= 2
    return bits


def path(name):
    bits = axis_bits()
    core, row = ("seq", 1), ("seq", 2)
    column = [bit for bit in bits if bit[0] == "seq" and bit[1] > 2]
    across = [bit for bit in bits if bit[0] == "batch"]
    order = {
        "y": column + across + [row],
        "x": column + [row] + across,
        "z": column[:-1] + across + [row] + column[-1:],
        "w": [row] + column + across,
    }[name]
    return order + [core]


def exchange(value, axis, step):
    pairs = [(i, i ^ step) for i in range(lax.axis_size(axis))]
    return lax.ppermute(value, axis, pairs)


def block_order():
    bits = axis_bits()
    return [("seq", 1), ("seq", 2)] + [b for b in bits if b[0] == "batch"] + [
        b for b in bits if b[0] == "seq" and b[1] > 2
    ]


def flat_index():
    return lax.axis_index("seq") * lax.axis_size("batch") + lax.axis_index("batch")


def relative_blocks():
    spread = []
    for axis, step in block_order():
        spread.append(step * lax.axis_size("batch") if axis == "seq" else step)
    count = len(spread)
    return [
        sum(spread[k] for k in range(count) if place >> (count - 1 - k) & 1)
        for place in range(2**count)
    ]


def tied(values):
    return list(lax.optimization_barrier(tuple(values)))


class Gather:
    def __init__(self, shard, order):
        self.current, self.order = shard, order
        self.have, self.halves, self.flying = [], None, None
        self.parts, self.rows, self.cols = shard.shape

    def ready(self):
        return self.current

    def hold(self, value):
        self.current = value

    def launch(self):
        self.flying = exchange(self.current, *self.order[len(self.have)])

    def land(self):
        stage = self.order[len(self.have)]
        if stage == self.order[-1]:
            self.halves = (self.current, self.flying)
            return
        significance = block_order()
        place = significance.index(stage)
        before = sum(1 for p in self.have if p < place)
        split = (self.parts * 2**before, 1, 2 ** (len(self.have) - before) * self.rows, self.cols)
        self.have.append(place)
        joined = jnp.concatenate([self.current.reshape(split), self.flying.reshape(split)], axis=1)
        self.current = joined.reshape(self.parts, 2 ** len(self.have) * self.rows, self.cols)

    @property
    def left(self):
        return 0 if self.halves is not None else len(self.order) - len(self.have)

    @property
    def done(self):
        return self.halves is not None


class Scatter:
    def __init__(self, halves, order):
        self.keep, self.give = halves
        self.order, self.stage, self.total, self.flying = order, 0, None, None
        self.have = list(range(1, len(order)))
        self.parts, half_rows, self.cols = self.keep.shape
        self.rows = half_rows // 2 ** len(self.have)

    def ready(self):
        return self.give

    def hold(self, value):
        self.give = value

    def launch(self):
        self.flying = exchange(self.give, *self.order[self.stage])

    def land(self):
        self.stage += 1
        if self.stage == len(self.order):
            total = self.keep.astype(f32) + self.flying.astype(f32)
            self.total = total.reshape(self.parts, self.rows, self.cols)
            return
        place = self.have.index(block_order().index(self.order[self.stage]))
        self.have.pop(place)
        left = 2 ** len(self.have) * self.rows
        split = (self.parts * 2**place, 2, left >> place, self.cols)
        keep, got = self.keep.reshape(split), self.flying.reshape(split)
        self.keep, self.give = [
            (keep[:, side].astype(f32) + got[:, side].astype(f32)).astype(bf16).reshape(
                self.parts, left, self.cols
            ) for side in range(2)
        ]

    @property
    def done(self):
        return self.total is not None


def checkpoint(value, flows, begin=(), waiting=()):
    value, *flying = tied([value] + [flow.flying for flow in flows])
    for flow, arrived in zip(flows, flying):
        flow.flying = arrived
        flow.land()
    going = [flow for flow in flows if not flow.done and flow not in waiting] + list(begin)
    value, *ready = tied([value] + [flow.ready() for flow in going])
    for flow, part in zip(going, ready):
        flow.hold(part)
        flow.launch()
    return value


def passed_along(value, steps):
    count = lax.axis_size("seq")
    pairs = [(i, i + steps) for i in range(count) if 0 <= i + steps < count]
    return lax.ppermute(value, "seq", pairs)


def pooled_hops(size):
    return -(-REACH // size)


def pooled_rims(pooled):
    size = pooled.shape[1]
    hops = range(1, pooled_hops(size) + 1)
    low = [passed_along(pooled, hop) for hop in reversed(hops)]
    up = [passed_along(pooled, -hop) for hop in hops]
    low = low[0] if len(low) == 1 else jnp.concatenate(low, axis=1)
    up = up[0] if len(up) == 1 else jnp.concatenate(up, axis=1)
    return low[:, low.shape[1] - REACH :], up[:, :REACH]


def rims_return(rim_low, rim_up, pooled_own):
    size = pooled_own.shape[2]
    hops = pooled_hops(size)
    if hops == 1:
        second = passed_along(rim_low[:, :, WIN : WIN + 16], -2)
        return tied([passed_along(rim_up, 1), passed_along(rim_low, -1), second]) + [pooled_own]
    far_low, far_up = rim_low[:, :, WIN : WIN + REACH], rim_up[:, :, WIN:]
    for hop in range(2, hops + 1):
        start = REACH - hop * size
        pooled_own = pooled_own + passed_along(far_low[:, :, start : start + size], -hop).astype(f32)
        start = (hop - 1) * size
        pooled_own = pooled_own + passed_along(far_up[:, :, start : start + size], hop).astype(f32)
    near_low, near_up = rim_low[:, :, :WIN], rim_up[:, :, :WIN]
    rim_low = jnp.concatenate([near_low, far_low[:, :, REACH - size :]], axis=2)
    rim_up = jnp.concatenate([near_up, far_up[:, :, :size]], axis=2)
    return passed_along(rim_up, 1), passed_along(rim_low, -1), None, pooled_own


def dot_nt(a, b):
    return lax.dot_general(a, b, (((1,), (1,)), ((), ())), preferred_element_type=f32)


def dot_nn(a, b):
    return lax.dot_general(a, b, (((1,), (0,)), ((), ())), preferred_element_type=f32)


def flipped(block):
    return jnp.transpose(block.astype(f32)).astype(bf16)


def two_heads(rows):
    lane = lax.broadcasted_iota(jnp.int32, rows.shape, 1)
    none = jnp.zeros_like(rows)
    half = rows.shape[1] // 2
    return jnp.concatenate(
        [jnp.where(lane < half, rows, none), jnp.where(lane < half, none, rows)], axis=0
    )


def heads_apart(block):
    half, queries = block.shape[0] // 2, block.shape[1] // 2
    return jnp.transpose(
        jnp.concatenate([block[:half, :queries], block[half:, queries:]], axis=0)
    )


def attend_kernel(near_ref, far_ref, q_ref, k_ref, v_ref, kl_ref, vl_ref, ku_ref, vu_ref,
                  pk_ref, pv_ref, pkl_ref, pvl_ref, pku_ref, pvu_ref, mixed_ref, stat_ref):
    blocks = q_ref.shape[1] // QROWS
    pairs = q_ref.shape[2] // 128
    for pair in range(pairs):
        at = slice(128 * pair, 128 * pair + 128)
        keys = jnp.concatenate([kl_ref[0, :, at], k_ref[0, :, at], ku_ref[0, :, at]], axis=0)
        values = jnp.concatenate([vl_ref[0, :, at], v_ref[0, :, at], vu_ref[0, :, at]], axis=0)
        far_keys = jnp.concatenate([pkl_ref[0, :, at], pk_ref[0, :, at], pku_ref[0, :, at]], axis=0)
        far_values = jnp.concatenate(
            [pvl_ref[0, :, at], pv_ref[0, :, at], pvu_ref[0, :, at]], axis=0
        )
        values_t, far_values_t = flipped(values), flipped(far_values)
        for block in range(blocks):
            first = QROWS * block
            query = two_heads(q_ref[0, first : first + QROWS, at] * 0.125)
            stop = first + QROWS + 2 * WIN
            score = dot_nt(keys[first:stop], query) + near_ref[block]
            top = jnp.max(score, axis=0, keepdims=True)
            prob = jnp.exp(score - top)
            total = jnp.sum(prob, axis=0, keepdims=True)
            near_low = (prob * (1.0 / total)).astype(bf16)
            row = (pair * blocks + block) * 2
            stat_ref[0, 0, row : row + 1, :] = top + jnp.log(total)
            score = dot_nt(far_keys, query) + far_ref[block]
            top = jnp.max(score, axis=0, keepdims=True)
            prob = jnp.exp(score - top)
            total = jnp.sum(prob, axis=0, keepdims=True)
            far_low = (prob * (1.0 / total)).astype(bf16)
            stat_ref[0, 0, row + 1 : row + 2, :] = top + jnp.log(total)
            mixed = dot_nn(values_t[:, first:stop], near_low) + dot_nn(far_values_t, far_low)
            mixed_ref[0, first : first + QROWS, at] = heads_apart(mixed).astype(bf16)


def attend_back_kernel(near_ref, far_ref, stat_ref, g_ref, q_ref, k_ref, v_ref, kl_ref, vl_ref,
                       ku_ref, vu_ref, pk_ref, pv_ref, pkl_ref, pvl_ref, pku_ref, pvu_ref,
                       dq_ref, own_ref, pool_ref, low_ref, up_ref):
    blocks = q_ref.shape[1] // QROWS
    pairs = q_ref.shape[2] // 128
    length = q_ref.shape[1]
    for pair in range(pairs):
        at = slice(128 * pair, 128 * pair + 128)
        keys = jnp.concatenate([kl_ref[0, :, at], k_ref[0, :, at], ku_ref[0, :, at]], axis=0)
        values = jnp.concatenate([vl_ref[0, :, at], v_ref[0, :, at], vu_ref[0, :, at]], axis=0)
        far_keys = jnp.concatenate([pkl_ref[0, :, at], pk_ref[0, :, at], pku_ref[0, :, at]], axis=0)
        far_values = jnp.concatenate(
            [pvl_ref[0, :, at], pv_ref[0, :, at], pvu_ref[0, :, at]], axis=0
        )
        keys_t, far_keys_t = flipped(keys), flipped(far_keys)
        near_parts = ([], [])
        far_totals = [None, None]
        for block in range(blocks):
            first = QROWS * block
            query = two_heads(q_ref[0, first : first + QROWS, at] * 0.125)
            grads = two_heads(g_ref[0, first : first + QROWS, at])
            stop = first + QROWS + 2 * WIN
            row = (pair * blocks + block) * 2
            prob = jnp.exp(
                dot_nt(keys[first:stop], query) + near_ref[block] - stat_ref[0, 0, row : row + 1, :]
            )
            grad_prob = dot_nt(values[first:stop], grads)
            inner = jnp.sum(prob * grad_prob, axis=0, keepdims=True)
            grad_score = (prob * (grad_prob - inner)).astype(bf16)
            near_parts[0].append(dot_nn(grad_score, query))
            near_parts[1].append(dot_nn(prob.astype(bf16), grads))
            grad_query = dot_nn(keys_t[:, first:stop], grad_score)
            prob = jnp.exp(
                dot_nt(far_keys, query) + far_ref[block] - stat_ref[0, 0, row + 1 : row + 2, :]
            )
            grad_prob = dot_nt(far_values, grads)
            inner = jnp.sum(prob * grad_prob, axis=0, keepdims=True)
            grad_score = (prob * (grad_prob - inner)).astype(bf16)
            parts = (dot_nn(grad_score, query), dot_nn(prob.astype(bf16), grads))
            grad_query = grad_query + dot_nn(far_keys_t, grad_score)
            dq_ref[0, first : first + QROWS, at] = (heads_apart(grad_query) * 0.125).astype(bf16)
            for kind in range(2):
                far_totals[kind] = parts[kind] if block == 0 else far_totals[kind] + parts[kind]
        for kind in range(2):
            rows = []
            for chunk in range(blocks + 1):
                terms = []
                if chunk < blocks:
                    terms.append(near_parts[kind][chunk][:QROWS])
                if chunk > 0:
                    terms.append(near_parts[kind][chunk - 1][QROWS:])
                rows.append(functools.reduce(jnp.add, terms))
            rows = jnp.concatenate(rows, axis=0)
            own_ref[kind, 0, :, at] = rows[WIN : WIN + length]
            low_ref[kind, 0, :WIN, at] = rows[:WIN].astype(bf16)
            up_ref[kind, 0, :WIN, at] = rows[WIN + length :].astype(bf16)
            far = far_totals[kind]
            pool_ref[kind, 0, :, at] = far[REACH : far.shape[0] - REACH]
            low_ref[kind, 0, WIN : WIN + REACH, at] = far[:REACH].astype(bf16)
            low_ref[kind, 0, WIN + REACH :, at] = far[REACH : REACH + 16].astype(bf16)
            up_ref[kind, 0, WIN:, at] = far[far.shape[0] - REACH :].astype(bf16)


LANES = 256


def attend_specs(length, width):
    groups = width // LANES
    pooled = length // 4

    def spec(rows, shift):
        return pl.BlockSpec((1, rows, LANES), lambda g, j: (g, 0, j + shift))

    def whole(count, rows):
        return pl.BlockSpec((count, rows, 2 * QROWS), lambda g, j: (0, 0, 0))

    blocks = length // QROWS
    masks = [whole(blocks, QROWS + 2 * WIN), whole(blocks, pooled + 2 * REACH)]
    stat_rows = LANES // 128 * blocks * 2
    stat = pl.BlockSpec((1, 1, stat_rows, 2 * QROWS), lambda g, j: (g, j, 0, 0))
    operands = [spec(length, 0), spec(length, groups), spec(length, 2 * groups)]
    operands += [spec(WIN, 0), spec(WIN, groups)] * 2
    operands += [spec(pooled, 0), spec(pooled, groups)]
    operands += [spec(REACH, 0), spec(REACH, groups)] * 2
    return groups, masks, stat, stat_rows, operands, spec


def attend_operands(qkv, rows_low, rows_up, pooled, pooled_low, pooled_up):
    return (
        qkv, qkv, qkv, rows_low, rows_low, rows_up, rows_up,
        pooled, pooled, pooled_low, pooled_low, pooled_up, pooled_up,
    )


def attend(masks, operands, width):
    qkv = operands[0]
    count, length = qkv.shape[:2]
    groups, mask_specs, stat, stat_rows, specs, spec = attend_specs(length, width)
    return pl.pallas_call(
        attend_kernel,
        grid=(count, groups),
        in_specs=mask_specs + specs,
        out_specs=[spec(length, 0), stat],
        out_shape=[
            jax.ShapeDtypeStruct((count, length, width), bf16),
            jax.ShapeDtypeStruct((count, groups, stat_rows, 2 * QROWS), f32),
        ],
        compiler_params=pltpu.CompilerParams(vmem_limit_bytes=VMEM_LIMIT),
        cost_estimate=pl.CostEstimate(
            flops=count * length * width * 2000, bytes_accessed=8000000, transcendentals=3000000
        ),
        name="attend",
    )(*masks, *operands)


def attend_back(masks, stats, grad_mixed, operands, first, count, before=None):
    every, length, width = grad_mixed.shape
    groups, mask_specs, stat, stat_rows, specs, spec = attend_specs(length, width)
    pooled = length // 4

    def pair_spec(rows):
        return pl.BlockSpec((2, 1, rows, LANES), lambda g, j: (0, g, 0, j))

    def moved(block):
        index_map = block.index_map
        return pl.BlockSpec(block.block_shape, lambda g, j: index_map(g + first, j))

    in_specs = [stat, spec(length, 0)] + specs
    out_specs = [
        spec(length, 0), pair_spec(length), pair_spec(pooled),
        pair_spec(WIN + REACH + 16), pair_spec(WIN + REACH),
    ]
    out_specs = [moved(block) for block in out_specs[:1]] + [
        pl.BlockSpec(
            block.block_shape, functools.partial(lambda g, j: (0, g + first, 0, j))
        ) for block in out_specs[1:]
    ]
    before = before or []
    kernel_inputs = len(mask_specs) + len(in_specs)

    def kernel(*refs):
        attend_back_kernel(*refs[:kernel_inputs], *refs[kernel_inputs + len(before) :])

    return pl.pallas_call(
        kernel,
        grid=(count, groups),
        in_specs=mask_specs + [moved(block) for block in in_specs]
        + [pl.BlockSpec(memory_space=pl.ANY)] * len(before),
        out_specs=out_specs,
        out_shape=[
            jax.ShapeDtypeStruct((every, length, width), bf16),
            jax.ShapeDtypeStruct((2, every, length, width), f32),
            jax.ShapeDtypeStruct((2, every, pooled, width), f32),
            jax.ShapeDtypeStruct((2, every, WIN + REACH + 16, width), bf16),
            jax.ShapeDtypeStruct((2, every, WIN + REACH, width), bf16),
        ],
        input_output_aliases={kernel_inputs + i: i for i in range(len(before))},
        compiler_params=pltpu.CompilerParams(vmem_limit_bytes=VMEM_LIMIT),
        cost_estimate=pl.CostEstimate(
            flops=count * length * width * 5000, bytes_accessed=6000000 * count,
            transcendentals=1500000 * count,
        ),
        name="attend_back",
    )(*masks, stats, grad_mixed, *operands, *before)


def window_masks(length):
    blocks = length // QROWS
    index, devices = lax.axis_index("seq"), lax.axis_size("seq")

    def bias(width, offset, scale, reach):
        key = lax.broadcasted_iota(jnp.int32, (blocks, width, QROWS), 1)
        query = lax.broadcasted_iota(jnp.int32, (blocks, width, QROWS), 2)
        block = lax.broadcasted_iota(jnp.int32, (blocks, width, QROWS), 0)
        key = key - offset + (block * QROWS if scale == 1 else 0)
        query = query + block * QROWS
        size = length // scale
        allowed = jnp.abs(query - scale * key) <= reach
        place = key + index * size
        allowed &= (place >= 0) & (place < size * devices)
        one = jnp.where(allowed, 0.0, masked_score).astype(f32)
        return jnp.concatenate([one, one], axis=2)

    return bias(QROWS + 2 * WIN, WIN, 1, WIN), bias(length // 4 + 2 * REACH, REACH, 4, PWIN)


def tap_select(length):
    pooled = length // 4
    row = jnp.arange(TAPS * pooled, dtype=jnp.int32)
    column = jnp.arange(length, dtype=jnp.int32)
    source = 4 * (row % pooled) + row // pooled - 2
    return (source[:, None] == column[None, :]).astype(bf16)


def pool_kernel(select_ref, kernel_ref, rows_ref, low_ref, pooled_ref):
    pooled = pooled_ref.shape[1]
    for group in range(rows_ref.shape[0]):
        taps = dot_nn(select_ref[...], rows_ref[group])
        total = kernel_ref[0, 0:1, :] * taps[:pooled]
        for tap in range(1, TAPS):
            total = total + kernel_ref[0, tap : tap + 1, :] * taps[tap * pooled : (tap + 1) * pooled]
        low = low_ref[group].astype(f32)
        edge = kernel_ref[0, 0:1, :] * low[14:15] + kernel_ref[0, 1:2, :] * low[15:16]
        row = lax.broadcasted_iota(jnp.int32, total.shape, 0)
        pooled_ref[group] = (total + jnp.where(row == 0, edge, 0.0)).astype(bf16)


def pool(select, kernel, qkv, rows_low, width):
    count, length = qkv.shape[:2]
    groups = width // LANES
    return pl.pallas_call(
        pool_kernel,
        grid=(2 * groups,),
        in_specs=[
            pl.BlockSpec(select.shape, lambda j: (0, 0)),
            pl.BlockSpec((1, 8, LANES), lambda j: (j // groups, 0, j % groups)),
            pl.BlockSpec((count, length, LANES), lambda j: (0, 0, j + groups)),
            pl.BlockSpec((count, 16, LANES), lambda j: (0, WIN // 16 - 1, j)),
        ],
        out_specs=pl.BlockSpec((count, length // 4, LANES), lambda j: (0, 0, j)),
        out_shape=jax.ShapeDtypeStruct((count, length // 4, 2 * width), bf16),
        compiler_params=pltpu.CompilerParams(vmem_limit_bytes=VMEM_LIMIT),
        cost_estimate=pl.CostEstimate(
            flops=count * length * width * 1300, bytes_accessed=2500000, transcendentals=0
        ),
        name="pool",
    )(select, kernel, qkv, rows_low)


def pool_messages_kernel(select_ref, kernel_ref, rows_ref, up_ref, down_ref, head_ref):
    pooled = up_ref.shape[1] - WIN
    length = rows_ref.shape[1]
    for group in range(rows_ref.shape[0]):
        taps = dot_nn(select_ref[...], rows_ref[group])
        total = kernel_ref[0, 0:1, :] * taps[:pooled]
        for tap in range(1, TAPS):
            total = total + kernel_ref[0, tap : tap + 1, :] * taps[tap * pooled : (tap + 1) * pooled]
        head_ref[group] = total[:16]
        total = total.astype(bf16)
        up_ref[group, :WIN] = rows_ref[group, length - WIN :]
        up_ref[group, WIN:] = total
        down_ref[group, :WIN] = rows_ref[group, :WIN]
        down_ref[group, WIN:] = total


def pool_messages(select, kernel, qkv, width):
    count, length = qkv.shape[:2]
    groups = width // LANES

    def spec(rows):
        return pl.BlockSpec((count, rows, LANES), lambda j: (0, 0, j))

    message = jax.ShapeDtypeStruct((count, WIN + length // 4, 2 * width), bf16)
    return pl.pallas_call(
        pool_messages_kernel,
        grid=(2 * groups,),
        in_specs=[
            pl.BlockSpec(select.shape, lambda j: (0, 0)),
            pl.BlockSpec((1, 8, LANES), lambda j: (j // groups, 0, j % groups)),
            pl.BlockSpec((count, length, LANES), lambda j: (0, 0, j + groups)),
        ],
        out_specs=[spec(WIN + length // 4), spec(WIN + length // 4), spec(16)],
        out_shape=[message, message, jax.ShapeDtypeStruct((count, 16, 2 * width), f32)],
        compiler_params=pltpu.CompilerParams(vmem_limit_bytes=VMEM_LIMIT),
        cost_estimate=pl.CostEstimate(
            flops=count * length * width * 1300, bytes_accessed=2500000, transcendentals=0
        ),
        name="pool_messages",
    )(select, kernel, qkv)


def pool_join_kernel(kernel_ref, head_ref, mine_ref, tail_ref, low_ref, second_ref, up_ref,
                     out_low_ref, out_ref, out_up_ref):
    first, last = kernel_ref[0, 0:1, :], kernel_ref[0, 1:2, :]
    row = lax.broadcasted_iota(jnp.int32, (16, LANES), 0)

    def completed(block, before):
        before = before.astype(f32)
        edge = first * before[14:15] + last * before[15:16]
        return (block + jnp.where(row == 0, edge, 0.0)).astype(bf16)

    for group in range(mine_ref.shape[0]):
        out_low_ref[group] = low_ref[group, WIN:]
        out_ref[group] = mine_ref[group]
        out_up_ref[group] = up_ref[group, WIN:]
        out_low_ref[group, :16] = completed(
            low_ref[group, WIN : WIN + 16].astype(f32), second_ref[group]
        )
        out_ref[group, :16] = completed(head_ref[group], low_ref[group, WIN - 16 : WIN])
        out_up_ref[group, :16] = completed(
            up_ref[group, WIN : WIN + 16].astype(f32), tail_ref[group]
        )


def pool_join(kernel, head, own_message, qkv, from_low, second, from_up, width):
    count, length = qkv.shape[:2]
    groups = width // LANES
    pooled = length // 4

    def spec(rows, at=0, shift=0):
        return pl.BlockSpec((count, rows, LANES), lambda j: (0, at, j + shift))

    out = jax.ShapeDtypeStruct((count, pooled, 2 * width), bf16)
    return pl.pallas_call(
        pool_join_kernel,
        grid=(2 * groups,),
        in_specs=[
            pl.BlockSpec((1, 8, LANES), lambda j: (j // groups, 0, j % groups)),
            spec(16), spec(pooled, WIN // pooled), spec(16, length // 16 - 1, groups),
            spec(WIN + pooled), spec(16), spec(WIN + pooled),
        ],
        out_specs=[spec(pooled)] * 3,
        out_shape=[out] * 3,
        compiler_params=pltpu.CompilerParams(vmem_limit_bytes=VMEM_LIMIT),
        cost_estimate=pl.CostEstimate(flops=0, bytes_accessed=5000000, transcendentals=0),
        name="pool_join",
    )(kernel, head, own_message, qkv, from_low, second, from_up)


def pool_back_kernel(select_ref, spread_ref, kernel_ref, rows_ref, low_rows_ref, own_ref, pool_ref,
                     low_ref, up_ref, *rest):
    *rims, grad_ref, tail_ref, taps_ref = rest if len(rest) == 3 else (*rest[:3], None, rest[3])
    pooled = pool_ref.shape[2]
    length = rows_ref.shape[1]
    tap_row = lax.broadcasted_iota(jnp.int32, (8, LANES), 0)
    tail_row = lax.broadcasted_iota(jnp.int32, (16, LANES), 0)
    taps_total = jnp.zeros((8, LANES), f32)
    for group in range(rows_ref.shape[0]):
        grads = pool_ref[0, group] + low_ref[0, group, WIN : WIN + pooled].astype(f32)
        grads = (grads + up_ref[0, group, WIN : WIN + pooled].astype(f32)).astype(bf16).astype(f32)
        taps = dot_nn(select_ref[...], rows_ref[group])
        low_rows = low_rows_ref[group].astype(f32)
        edge = grads[0:1]
        spread = []
        for tap in range(TAPS):
            line = jnp.sum(grads * taps[tap * pooled : (tap + 1) * pooled], axis=0, keepdims=True)
            if tap < 2:
                line = line + edge * low_rows[14 + tap : 15 + tap]
            taps_total = taps_total + jnp.where(tap_row == tap, line, 0.0)
            spread.append(grads * kernel_ref[0, tap : tap + 1, :])
        spread = jnp.concatenate(spread, axis=0)
        high = spread.astype(bf16)
        rest = (spread - high.astype(f32)).astype(bf16)
        total = own_ref[0, group] + dot_nn(spread_ref[...], high) + dot_nn(spread_ref[...], rest)
        first, last = kernel_ref[0, 0:1, :], kernel_ref[0, 1:2, :]
        if rims:
            mine_ref, second_ref = rims
            edge = up_ref[0, group, WIN + pooled : WIN + pooled + 1].astype(f32)
            edge = edge + mine_ref[0, group, 0:1].astype(f32) + second_ref[0, group, 0:1].astype(f32)
            edge = edge.astype(bf16).astype(f32)
        tail = jnp.where(tail_row == 14, edge * first, 0.0)
        tail = tail + jnp.where(tail_row == 15, edge * last, 0.0)
        kind = grad_ref.dtype
        upper = total[length - WIN :] + up_ref[0, group, :WIN].astype(f32)
        if length > 2 * WIN:
            grad_ref[0, group, WIN : length - WIN] = total[WIN : length - WIN].astype(kind)
        grad_ref[0, group, :WIN] = (total[:WIN] + low_ref[0, group, :WIN].astype(f32)).astype(kind)
        if rims:
            grad_ref[0, group, length - WIN : length - 16] = upper[: WIN - 16].astype(kind)
            grad_ref[0, group, length - 16 :] = (upper[WIN - 16 :] + tail).astype(kind)
        else:
            grad_ref[0, group, length - WIN :] = upper.astype(kind)
            tail_ref[0, group] = tail.astype(bf16)
    taps_ref[0] = taps_total


def pool_back(select, kernel, qkv, rows_low, own, pooled_own, from_low, from_up, rim_up, second):
    count, length, width = own.shape[1:]
    groups = width // LANES
    pooled = length // 4

    def pair_spec(rows):
        return pl.BlockSpec((1, count, rows, LANES), lambda j: (j // groups, 0, 0, j % groups))

    joined = second is not None
    tail_shape = jax.ShapeDtypeStruct((2, count, 16, width), bf16)
    tail_specs, tail_shapes = ([], []) if joined else ([pair_spec(16)], [tail_shape])
    rim_spec = pl.BlockSpec(
        (1, count, 16, LANES), lambda j: (j // groups, 0, WIN // 16, j % groups)
    )
    extra_specs, extra = ([rim_spec, pair_spec(16)], [rim_up, second]) if joined else ([], [])
    return pl.pallas_call(
        pool_back_kernel,
        grid=(2 * groups,),
        in_specs=[
            pl.BlockSpec(select.shape, lambda j: (0, 0)),
            pl.BlockSpec(select.shape[::-1], lambda j: (0, 0)),
            pl.BlockSpec((1, 8, LANES), lambda j: (j // groups, 0, j % groups)),
            pl.BlockSpec((count, length, LANES), lambda j: (0, 0, j + groups)),
            pl.BlockSpec((count, 16, LANES), lambda j: (0, WIN // 16 - 1, j)),
            pair_spec(length), pair_spec(pooled),
            pair_spec(from_low.shape[2]), pair_spec(from_up.shape[2]),
        ] + extra_specs,
        out_specs=[pair_spec(length)] + tail_specs + [
            pl.BlockSpec((1, 8, LANES), lambda j: (j // groups, 0, j % groups)),
        ],
        out_shape=[
            jax.ShapeDtypeStruct((2, count, length, width), bf16 if joined else f32),
            *tail_shapes,
            jax.ShapeDtypeStruct((2, 8, width), f32),
        ],
        compiler_params=pltpu.CompilerParams(vmem_limit_bytes=VMEM_LIMIT),
        cost_estimate=pl.CostEstimate(
            flops=count * length * width * 4000, bytes_accessed=9000000, transcendentals=0
        ),
        name="pool_back",
    )(select, select.T, kernel, qkv, rows_low, own, pooled_own, from_low, from_up, *extra)


def matmul(a, b):
    return jnp.dot(a, b, preferred_element_type=f32)


def matmul_t(a, b):
    return lax.dot_general(a, b, (((1,), (1,)), ((), ())), preferred_element_type=f32)


def weight_grad(a, b):
    return lax.dot_general(a, b, (((0,), (0,)), ((), ())), preferred_element_type=f32)


def normalised(rows):
    centre = rows - jnp.mean(rows, axis=-1, keepdims=True)
    inverse = lax.rsqrt(jnp.mean(centre * centre, axis=-1, keepdims=True) + norm_eps)
    return centre * inverse, inverse


def normalised_back(grads, gain, norm, inverse):
    scaled = grads * gain
    mean = jnp.mean(scaled, axis=-1, keepdims=True)
    inner = jnp.mean(scaled * norm, axis=-1, keepdims=True)
    return (scaled - mean - norm * inner) * inverse


def gelu_both(value):
    square = value * value
    inside = jnp.tanh(value * (gelu_coef + (gelu_coef * 0.044715) * square))
    half = 0.5 * value
    bend = gelu_coef + (3 * 0.044715 * gelu_coef) * square
    return half + half * inside, 0.5 + 0.5 * inside + half * (1.0 - inside * inside) * bend


def small_index():
    return flat_index().reshape(1).astype(jnp.int32)


def place_kernel(blocks, index_ref, mine_ref, other_ref, out_ref):
    half = len(blocks) // 2
    for place, bits in enumerate(blocks):
        source = mine_ref if place < half else other_ref
        out_ref[0, index_ref[0] ^ bits] = source[0, place % half]


def in_place(halves, block_cols, skip=0, take=None):
    blocks = relative_blocks()
    half = len(blocks) // 2
    all_parts, half_rows, cols = halves[0].shape
    parts = take or all_parts
    rows = half_rows // half
    spec = pl.BlockSpec((1, half, rows, block_cols), lambda p, j, index: (p + skip, 0, 0, j))
    whole = pl.pallas_call(
        functools.partial(place_kernel, blocks),
        grid_spec=pltpu.PrefetchScalarGridSpec(
            num_scalar_prefetch=1,
            grid=(parts, cols // block_cols),
            in_specs=[spec, spec],
            out_specs=pl.BlockSpec(
                (1, 2 * half, rows, block_cols), lambda p, j, index: (p, 0, 0, j)
            ),
        ),
        out_shape=jax.ShapeDtypeStruct((parts, 2 * half, rows, cols), halves[0].dtype),
        compiler_params=pltpu.CompilerParams(vmem_limit_bytes=VMEM_LIMIT),
        cost_estimate=pl.CostEstimate(
            flops=0, bytes_accessed=8 * parts * half_rows * cols, transcendentals=0
        ),
        name="in_place",
    )(small_index(), *[h.reshape(all_parts, half, rows, cols) for h in halves])
    return whole.reshape(parts * 2 * half_rows, cols)


def store_blocks(blocks, index, total_ref, keep_ref, give_ref):
    half = len(blocks) // 2
    rows = total_ref.shape[0] // len(blocks)
    for place, bits in enumerate(blocks):
        target = keep_ref if place < half else give_ref
        start = pl.multiple_of((index ^ bits) * rows, 8)
        target[0, place % half] = total_ref[pl.ds(start, rows), :].astype(bf16)


def weight_grads_kernel(blocks, plan, index_ref, *refs):
    operands, (keep_ref, give_ref, total_ref) = refs[:-3], refs[-3:]
    width = total_ref.shape[0]
    for step, (left, left_at, right, right_at) in enumerate(plan):

        @pl.when(pl.program_id(0) == step)
        def _():
            rows = operands[left][:, left_at * width : (left_at + 1) * width]
            grads = operands[right][:, right_at * width : (right_at + 1) * width]
            total_ref[...] = weight_grad(rows, grads)

    store_blocks(blocks, index_ref[0], total_ref, keep_ref, give_ref)


def turned(whole):
    bits = axis_bits()
    cols = whole.shape[1]
    split = whole.reshape((2,) * len(bits) + (-1, cols))
    for place, (axis, step) in enumerate(bits):
        mine = (lax.axis_index(axis) // step) % 2
        split = jnp.where(mine == 1, jnp.flip(split, place), split)
    order = [bits.index(bit) for bit in block_order()]
    split = split.transpose(*order, len(bits), len(bits) + 1)
    return split.reshape(1, 2, -1, cols)


def weight_grads(operands, plan, width, stacked=False):
    blocks = relative_blocks()
    half = len(blocks) // 2
    rows = width // len(blocks)
    count = len(plan)
    if rows % 8:
        pieces = []
        for left, left_at, right, right_at in plan:
            left_rows = operands[left][:, left_at * width : (left_at + 1) * width]
            grads = operands[right][:, right_at * width : (right_at + 1) * width]
            pieces.append(turned(weight_grad(left_rows, grads).astype(bf16)))
        joined = jnp.concatenate(pieces, axis=0 if stacked else 3)
        return joined[:, 0], joined[:, 1]
    if stacked:
        shape, spec = (count, half, rows, width), lambda j, index: (j, 0, 0, 0)
    else:
        shape, spec = (1, half, rows, count * width), lambda j, index: (0, 0, 0, j)
    out = jax.ShapeDtypeStruct(shape, bf16)
    spec = pl.BlockSpec((1, half, rows, width), spec)
    tokens = operands[0].shape[0]
    pair = pl.pallas_call(
        functools.partial(weight_grads_kernel, blocks, plan),
        grid_spec=pltpu.PrefetchScalarGridSpec(
            num_scalar_prefetch=1,
            grid=(count,),
            in_specs=[pl.BlockSpec(a.shape, lambda j, index: (0, 0)) for a in operands],
            out_specs=[spec, spec],
            scratch_shapes=[pltpu.VMEM((width, width), f32)],
        ),
        out_shape=[out, out],
        compiler_params=pltpu.CompilerParams(vmem_limit_bytes=VMEM_LIMIT),
        cost_estimate=pl.CostEstimate(
            flops=2 * tokens * width * width * count,
            bytes_accessed=2 * sum(a.size for a in operands) + 2 * count * width * width,
            transcendentals=0,
        ),
        name="weight_grads",
    )(small_index(), *operands)
    return [side.reshape(shape[0], half * rows, shape[3]) for side in pair]


ROWS = 128
EDGES = ("output_bias", "down_bias", "mixer_gain", "mixer_shift", "feed_gain", "feed_shift")


def by_rows(count, body, rows=ROWS):
    for first in range(0, count, rows):
        body(slice(first, first + rows))


def feed_kernel(x_ref, mixed_ref, vectors_ref, bias_ref, out_ref, up_ref, down_ref,
                norm_ref, inverse_ref, low_ref, act_ref, slope_ref, norm_two_ref, inverse_two_ref,
                y_ref, hidden_ref, total_ref):
    step, last = pl.program_id(0), pl.num_programs(0) - 1
    count = x_ref.shape[0]

    def vector(name):
        at = EDGES.index(name)
        return vectors_ref[at : at + 1, :]

    @pl.when(step == 0)
    def _():
        total_ref[...] = dot_nn(mixed_ref[...], out_ref[...])

        def body(at):
            norm, inverse = normalised(x_ref[at, :] + total_ref[at, :] + vector("output_bias"))
            hidden = norm * vector("mixer_gain") + vector("mixer_shift")
            norm_ref[at, :], inverse_ref[at, :] = norm, inverse
            hidden_ref[at, :] = hidden
            low_ref[at, :] = hidden.astype(bf16)
            total_ref[at, :] = jnp.zeros_like(hidden)

        by_rows(count, body)

    def units(at):
        act, slope = gelu_both(dot_nn(low_ref[at, :], up_ref[...]) + bias_ref[...])
        act = act.astype(bf16)
        act_ref[at, :], slope_ref[at, :] = act, slope.astype(bf16)
        total_ref[at, :] += dot_nn(act, down_ref[...])

    by_rows(count, units, 256)

    @pl.when(step == last)
    def _():
        def body(at):
            rows = hidden_ref[at, :] + total_ref[at, :] + vector("down_bias")
            norm, inverse = normalised(rows)
            norm_two_ref[at, :], inverse_two_ref[at, :] = norm, inverse
            y_ref[at, :] = norm * vector("feed_gain") + vector("feed_shift")

        by_rows(count, body)


def feed_forward(x, mixed, small, feed, ratio):
    out_weight, out_at, whole, up_at = feed
    count, width = x.shape
    rows = pl.BlockSpec((count, width), lambda j: (0, 0))
    line = pl.BlockSpec((count, 1), lambda j: (0, 0))
    part = pl.BlockSpec((count, width), lambda j: (0, j))

    def weight(shift, moves):
        return pl.BlockSpec((width, width), lambda j: (0, shift + moves * j))

    def shape(cols, kind):
        return jax.ShapeDtypeStruct((count, cols), kind)

    return pl.pallas_call(
        feed_kernel,
        grid=(ratio,),
        in_specs=[
            rows, rows, pl.BlockSpec((8, width), lambda j: (0, 0)),
            pl.BlockSpec((1, width), lambda j: (0, j)),
            weight(out_at, 0), weight(up_at, 1), weight(up_at + ratio, 1),
        ],
        out_specs=[rows, line, rows, part, part, rows, line, rows],
        out_shape=[
            shape(width, f32), shape(1, f32), shape(width, bf16), shape(ratio * width, bf16),
            shape(ratio * width, bf16), shape(width, f32), shape(1, f32), shape(width, f32),
        ],
        scratch_shapes=[pltpu.VMEM((count, width), f32)] * 2,
        compiler_params=pltpu.CompilerParams(vmem_limit_bytes=VMEM_LIMIT),
        cost_estimate=pl.CostEstimate(
            flops=2 * count * width * width * (1 + 2 * ratio), transcendentals=count * width * ratio,
            bytes_accessed=2 * whole.size + 4 * count * width * ratio + 20 * count * width,
        ),
        name="feed_forward",
    )(x, mixed, small["vectors"], small["up_bias"], out_weight, whole, whole)


def feed_back_kernel(blocks, index_ref, grads_ref, norm_ref, inverse_ref, norm_two_ref,
                     inverse_two_ref, vectors_ref, low_ref, act_ref, slope_ref, out_ref, up_ref,
                     down_ref, one_ref, attention_ref, mixed_ref, sums_ref, bias_ref, *rest):
    outs, (feed_ref, hidden_ref, total_ref, pre_ref, turn_ref) = rest[:-5], rest[-5:]
    step, last = pl.program_id(0), pl.num_programs(0) - 1
    count, width = grads_ref.shape

    def vector(name):
        at = EDGES.index(name)
        return vectors_ref[at : at + 1, :]

    def add(name, rows):
        at = EDGES.index(name)
        sums_ref[at : at + 1, :] += jnp.sum(rows, axis=0, keepdims=True)

    def store(pair):
        if blocks is None:
            pair[0][0] = total_ref[...].astype(bf16)
        else:
            store_blocks(blocks, index_ref[0], total_ref, *pair)

    @pl.when(step == 0)
    def _():
        sums_ref[...] = jnp.zeros_like(sums_ref)
        turn_ref[...] = jnp.transpose(low_ref[...])

        def body(at):
            grads, norm = grads_ref[at, :], norm_two_ref[at, :]
            add("feed_gain", grads * norm)
            add("feed_shift", grads)
            back = normalised_back(grads, vector("feed_gain"), norm, inverse_two_ref[at, :])
            hidden_ref[at, :] = back
            back = back.astype(bf16)
            feed_ref[at, :] = back
            add("down_bias", back.astype(f32))

        by_rows(count, body)

    pre_ref[...] = (
        slope_ref[...].astype(f32) * dot_nt(feed_ref[...], down_ref[...])
    ).astype(bf16)
    bias_ref[...] = jnp.sum(pre_ref[...].astype(f32), axis=0, keepdims=True)
    hidden_ref[...] += dot_nt(pre_ref[...], up_ref[...])
    total_ref[...] = weight_grad(act_ref[...], feed_ref[...])
    store(outs[: len(outs) // 2])
    total_ref[...] = dot_nn(turn_ref[...], pre_ref[...])
    store(outs[len(outs) // 2 :])

    @pl.when(step == last)
    def _():
        def body(at):
            grads, norm = hidden_ref[at, :], norm_ref[at, :]
            add("mixer_gain", grads * norm)
            add("mixer_shift", grads)
            back = normalised_back(grads, vector("mixer_gain"), norm, inverse_ref[at, :])
            one_ref[at, :] = back
            back = back.astype(bf16)
            attention_ref[at, :] = back
            add("output_bias", back.astype(f32))

        by_rows(count, body)
        mixed_ref[...] = dot_nt(attention_ref[...], out_ref[...]).astype(bf16)


def feed_back(grads, kept, small, feed, ratio):
    norm, inverse, low, act, slope, norm_two, inverse_two = kept
    out_weight, out_at, whole, up_at = feed
    count, width = grads.shape
    blocks = relative_blocks()
    half = len(blocks) // 2
    shard = width // len(blocks)
    rows = pl.BlockSpec((count, width), lambda j, index: (0, 0))
    line = pl.BlockSpec((count, 1), lambda j, index: (0, 0))
    part = pl.BlockSpec((count, width), lambda j, index: (0, j))
    edge = pl.BlockSpec((8, width), lambda j, index: (0, 0))

    def weight(shift, moves):
        return pl.BlockSpec((width, width), lambda j, index: (0, shift + moves * j))

    if shard % 8:
        blocks = None
        out = [jax.ShapeDtypeStruct((ratio, width, width), bf16)] * 2
        specs = [pl.BlockSpec((1, width, width), lambda j, index: (j, 0, 0))] * 2
    else:
        block = (1, half, shard, width)
        out = [jax.ShapeDtypeStruct((ratio, half, shard, width), bf16)] * 2
        out += [jax.ShapeDtypeStruct((1, half, shard, ratio * width), bf16)] * 2
        specs = [pl.BlockSpec(block, lambda j, index: (j, 0, 0, 0))] * 2
        specs += [pl.BlockSpec(block, lambda j, index: (0, 0, 0, j))] * 2
    results = pl.pallas_call(
        functools.partial(feed_back_kernel, blocks),
        grid_spec=pltpu.PrefetchScalarGridSpec(
            num_scalar_prefetch=1,
            grid=(ratio,),
            in_specs=[
                rows, rows, line, rows, line, edge, rows, part, part,
                weight(out_at, 0), weight(up_at, 1), weight(up_at + ratio, 1),
            ],
            out_specs=[
                rows, rows, rows, edge, pl.BlockSpec((1, width), lambda j, index: (0, j)), *specs
            ],
            scratch_shapes=[
                pltpu.VMEM((count, width), bf16), pltpu.VMEM((count, width), f32),
                pltpu.VMEM((width, width), f32), pltpu.VMEM((count, width), bf16),
                pltpu.VMEM((width, count), bf16),
            ],
        ),
        out_shape=[
            jax.ShapeDtypeStruct((count, width), f32), jax.ShapeDtypeStruct((count, width), bf16),
            jax.ShapeDtypeStruct((count, width), bf16), jax.ShapeDtypeStruct((8, width), f32),
            jax.ShapeDtypeStruct((1, ratio * width), f32), *out,
        ],
        compiler_params=pltpu.CompilerParams(vmem_limit_bytes=VMEM_LIMIT),
        cost_estimate=pl.CostEstimate(
            flops=2 * count * width * width * (1 + 4 * ratio), transcendentals=0,
            bytes_accessed=4 * whole.size + 4 * count * width * ratio + 20 * count * width,
        ),
        name="feed_back",
    )(small_index(), grads, norm, inverse, norm_two, inverse_two, small["vectors"], low, act, slope,
      out_weight, whole, whole)
    one, attention_low, grad_mixed, sums, up_sums, *out = results
    if blocks is None:
        down = [turned(out[0][i]) for i in range(ratio)]
        down = [jnp.concatenate([d[:, side] for d in down]) for side in range(2)]
        up = [turned(out[1][i]) for i in range(ratio)]
        up = [jnp.concatenate([u[:, side] for u in up], axis=2) for side in range(2)]
    else:
        down = [side.reshape(ratio, half * shard, width) for side in out[:2]]
        up = [side.reshape(1, half * shard, ratio * width) for side in out[2:]]
    return one, attention_low, grad_mixed, sums, up_sums, down, up


def units_back_kernel(spread_ref, *refs):
    parts, out_ref = refs[:-1], refs[-1]
    total = None
    for part, rows_ref in enumerate(parts):
        left = rows_ref[...]
        for _ in range(3):
            piece = left.astype(bf16)
            left = left - piece.astype(f32)
            term = dot_nn(piece, spread_ref[part])
            total = term if total is None else total + term
    out_ref[...] = total


def units_back(rows, ratio, shard_rows):
    count, cols = rows.shape
    block = cols // ratio // 2
    source = jnp.arange(block, dtype=jnp.int32)
    target = jnp.arange(ratio * block, dtype=jnp.int32)
    device, rest = target // (ratio * shard_rows), target % (ratio * shard_rows)
    wanted = device * shard_rows + rest % shard_rows
    spread = jnp.stack([
        (source[:, None] == wanted[None, :]) & (rest[None, :] // shard_rows == part)
        for part in range(ratio)
    ]).astype(bf16)
    return pl.pallas_call(
        units_back_kernel,
        grid=(2,),
        in_specs=[pl.BlockSpec(spread.shape, lambda j: (0, 0, 0))] + [
            pl.BlockSpec((count, block), functools.partial(lambda part, j: (0, 2 * part + j), part))
            for part in range(ratio)
        ],
        out_specs=pl.BlockSpec((count, ratio * block), lambda j: (0, j)),
        out_shape=jax.ShapeDtypeStruct((count, cols), f32),
        compiler_params=pltpu.CompilerParams(vmem_limit_bytes=VMEM_LIMIT),
        name="units_back",
    )(spread, *[rows] * ratio)


SMALL_COLUMNS = 128


def small_grads_kernel(blocks, layers, index_ref, *refs):
    sources, (keep_ref, give_ref, lines_ref, columns_ref) = refs[:-4], refs[-4:]
    lines_ref[...] = jnp.zeros_like(lines_ref)
    width = lines_ref.shape[1]
    each = len(sources) // layers
    at = 0
    for layer in range(layers):
        query_ref, value_ref, sums_ref, up_ref, taps_ref = sources[layer * each : (layer + 1) * each]
        lines_ref[at : at + 1, :] = query_ref[...]
        lines_ref[at + 1 : at + 2, :] = value_ref[...]
        lines_ref[at + 2 : at + 2 + len(EDGES), :] = sums_ref[: len(EDGES), :]
        at += 2 + len(EDGES)
        for kind in range(2):
            lines_ref[at : at + TAPS, :] = taps_ref[kind, :TAPS]
            at += TAPS
        for part in range(up_ref.shape[1] // width):
            lines_ref[at : at + 1, :] = up_ref[:, part * width : (part + 1) * width]
            at += 1
    columns_ref[...] = jnp.transpose(lines_ref[...])
    store_blocks(blocks, index_ref[0], columns_ref, keep_ref, give_ref)


def small_grads(per_layer, width):
    blocks = relative_blocks()
    half = len(blocks) // 2
    rows = width // len(blocks)
    if rows % 8:
        lines = []
        for query, value, sums, up, taps in per_layer:
            lines += [query, value, sums[: len(EDGES)], taps[0, :TAPS], taps[1, :TAPS]]
            lines.append(up.reshape(-1, width))
        lines = jnp.concatenate(lines, axis=0)
        lines = jnp.pad(lines, ((0, SMALL_COLUMNS - lines.shape[0]), (0, 0))).T.astype(bf16)
        lines = turned(lines)
        return lines[:, 0], lines[:, 1]
    flat = [a for arrays in per_layer for a in arrays]
    out = jax.ShapeDtypeStruct((1, half, rows, SMALL_COLUMNS), bf16)
    pair = pl.pallas_call(
        functools.partial(small_grads_kernel, blocks, len(per_layer)),
        in_specs=[pl.BlockSpec(memory_space=pltpu.SMEM)]
        + [pl.BlockSpec(memory_space=pltpu.VMEM)] * len(flat),
        out_specs=[pl.BlockSpec(memory_space=pltpu.VMEM)] * 2,
        out_shape=[out, out],
        scratch_shapes=[pltpu.VMEM((SMALL_COLUMNS, width), f32), pltpu.VMEM((width, SMALL_COLUMNS), f32)],
        compiler_params=pltpu.CompilerParams(vmem_limit_bytes=VMEM_LIMIT),
        name="small_grads",
    )(small_index(), *flat)
    return [side.reshape(1, half * rows, SMALL_COLUMNS) for side in pair]


def layer_forward(x, weights, masks, select, count, at):
    qkv_weight, feed_weights, small = weights
    width = x.shape[1]
    length = x.shape[0] // count
    x_low = x.astype(bf16)
    bias = jnp.concatenate([small["query_bias"], jnp.zeros((width,), f32), small["value_bias"]])
    qkv = matmul(x_low, qkv_weight)
    qkv = at("projected", (qkv + bias).astype(bf16).reshape(count, length, -1))
    if pooled_hops(length // 4) == 1 and length // 4 == WIN:
        up_message, down_message, head = pool_messages(select, small["taps"], qkv, width)
        rows_low, rows_up, second = tied([
            passed_along(up_message, 1), passed_along(down_message, -1),
            passed_along(qkv[:, length - 16 :, width:], 2),
        ])
        rows_low = at("pooled", rows_low)
        pooled_low, pooled, pooled_up = pool_join(
            small["taps"], head, up_message, qkv, rows_low, second, rows_up, width
        )
    else:
        rows_low = passed_along(qkv[:, length - WIN :, width:], 1)
        rows_up = passed_along(qkv[:, :WIN, width:], -1)
        pooled = at("pooled", pool(select, small["taps"], qkv, rows_low, width))
        pooled_low, pooled_up = pooled_rims(pooled)
    pooled_up = at("attending", pooled_up)
    operands = attend_operands(qkv, rows_low, rows_up, pooled, pooled_low, pooled_up)
    mixed, stats = attend(masks, operands, width)
    mixed = at("attended", mixed.reshape(count * length, width))
    ratio = small["up_bias"].shape[1] // width
    norm, inverse, hidden_low, act_low, slope, norm_two, inverse_two, y = feed_forward(
        x, mixed, small, feed_weights, ratio
    )
    y = at("fed", y)
    kept = (x_low, operands, stats, mixed, (norm, inverse, hidden_low, act_low, slope, norm_two, inverse_two))
    return y, kept


def layer_backward(grads, kept, weights, masks, select, count, at):
    qkv_weight, feed_weights, small = weights
    x_low, operands, stats, mixed, feed_kept = kept
    rows, width = grads.shape
    length = rows // count
    ratio = small["up_bias"].shape[1] // width

    def total(value):
        return jnp.sum(value.astype(f32), axis=0, keepdims=True)

    grad_one, attention_low, grad_mixed, sums, up_sums, down_halves, up_halves = feed_back(
        grads, feed_kept, small, feed_weights, ratio
    )
    grad_mixed = at("attending", grad_mixed, (down_halves, up_halves))
    grad_mixed = grad_mixed.reshape(count, length, width)
    part = max(count // 2, 1)
    pieces = list(attend_back(masks, stats, grad_mixed, operands, 0, part))
    if part < count:
        pieces[0] = at("halfway", pieces[0])
        pieces = attend_back(masks, stats, grad_mixed, operands, part, count - part, pieces)
    grad_query, own, pooled_own, rim_low, rim_up = pieces
    rim_up = at("rims", rim_up)
    grad_query = grad_query.reshape(rows, width)
    from_low, from_up, second, pooled_own = rims_return(rim_low, rim_up, pooled_own)
    own, *tail, taps = pool_back(
        select, small["taps"], operands[0], operands[3], own, pooled_own, from_low, from_up,
        rim_up, second,
    )
    if tail:
        tail = passed_along(tail[0], -1).astype(f32)
        own = own + jnp.pad(tail, ((0, 0), (0, 0), (length - 16, 0), (0, 0)))
    own = at("pooled", own, (x_low, grad_query, mixed, attention_low))
    own = own.astype(bf16).reshape(2, rows, width)
    grad_qkv = (grad_query, own[0], own[1])
    grad_x = grad_one + matmul_t(jnp.concatenate(grad_qkv, axis=1), qkv_weight)
    small_sums = [total(grad_query), total(own[1]), sums, up_sums, taps]
    return grad_x, (x_low, *grad_qkv, mixed, attention_low), small_sums


def pack_small(vectors, up_biases, taps):
    columns = []
    for layer in range(vectors[0].shape[0]):
        rows = vectors[0].shape[1]
        columns.append(jnp.stack([v[layer] for v in vectors]))
        columns.append(taps[0][layer])
        columns.append(taps[1][layer])
        columns.append(up_biases[layer].reshape(-1, rows))
    packed = jnp.concatenate(columns, axis=0)
    return jnp.pad(packed, ((0, SMALL_COLUMNS - packed.shape[0]), (0, 0))).T


def unpack_small(columns, layers, ratio):
    width = columns.shape[0]
    lines = columns.astype(f32).T
    per_layer = 8 + 2 * TAPS + ratio
    pad = ((0, 8 - TAPS), (0, 0))
    result = []
    for layer in range(layers):
        piece = lines[layer * per_layer : (layer + 1) * per_layer]
        result.append({
            "query_bias": piece[0],
            "value_bias": piece[1],
            "vectors": piece[2:10],
            "taps": jnp.stack([
                jnp.pad(piece[8 : 8 + TAPS], pad), jnp.pad(piece[8 + TAPS : 8 + 2 * TAPS], pad),
            ]),
            "up_bias": piece[8 + 2 * TAPS :].reshape(1, ratio * width),
        })
    return result


def on_device(
    tokens, cotangent, masked, query_weight, key_weight, value_weight, output_weight, up_weight,
    down_weight, query_bias, value_bias, output_bias, up_bias, down_bias, mixer_gain, mixer_shift,
    feed_gain, feed_shift, pool_key, pool_value,
):
    micro, seqs, length, width = tokens.shape
    count = micro * seqs
    layers = query_weight.shape[0]
    devices = lax.axis_size("seq") * lax.axis_size("batch")
    shard_rows = width // devices
    small_shard = pack_small(
        (query_bias, value_bias, output_bias, down_bias, mixer_gain, mixer_shift, feed_gain,
         feed_shift), up_bias, (pool_key, pool_value),
    )
    masks = window_masks(length)
    select = tap_select(length)
    ratio = up_weight.shape[2] // width

    def units_apart(rows):
        split = rows.reshape(rows.shape[0], devices, ratio, shard_rows)
        return split.transpose(0, 2, 1, 3).reshape(rows.shape)

    shard = jnp.concatenate(
        [query_weight[0], key_weight[0], value_weight[0], small_shard], axis=1
    )
    first = Gather(shard[None], path("y"))

    later = [
        Gather(jnp.concatenate(
            [query_weight[layer], key_weight[layer], value_weight[layer], output_weight[layer]],
            axis=1,
        )[None], path("x"))
        for layer in range(1, layers)
    ]
    x = tokens.reshape(count * length, width).astype(f32)
    feeds = []

    def gather_feed(layer, after):
        out, up, down, after = tied(
            [output_weight[layer], up_weight[layer], down_weight[layer], after]
        )
        parts = [units_apart(up), *down.reshape(ratio, shard_rows, width)]
        shard = jnp.concatenate([out] * (layer == 0) + parts, axis=1)
        feeds.append(lax.all_gather(shard, ("seq", "batch"), axis=0, tiled=True))
        return after

    x = checkpoint(x, [], [first])
    x = gather_feed(0, checkpoint(x, [first]))
    while first.left > 2:
        x = checkpoint(x, [first])
    x = checkpoint(x, [], later)
    for layer in range(1, layers):
        x = gather_feed(layer, x)
    if later:
        x = checkpoint(x, later)
        x = checkpoint(x, later, [], later)
    x = checkpoint(x, [first])
    x = checkpoint(x, [first])
    first_whole = in_place(first.halves, first.cols)
    smalls = unpack_small(first_whole[:, 3 * width :], layers, ratio)

    def landed(value, flows, left):
        while True:
            behind = [flow for flow in flows if flow.left > left]
            if not behind:
                return value
            value = checkpoint(value, behind)

    def forward_at(layer):
        following = later[layer : layer + 1]

        def at(name, value):
            if name == "pooled":
                return checkpoint(value, [], following)
            if name == "attended":
                return checkpoint(value, following)
            if name == "fed":
                return landed(value, following, 0)
            return value

        return at

    states, weights = [], []
    for layer in range(layers):
        if layer == 0:
            qkv_weight = first_whole[:, : 3 * width]
        else:
            qkv_weight = in_place(later[layer - 1].halves, width)
        feed = (feeds[0], 0, feeds[0], 1) if layer == 0 else (qkv_weight, 3, feeds[layer], 0)
        whole = (qkv_weight[:, : 3 * width], feed, smalls[layer])
        x, kept = layer_forward(x, whole, masks, select, count, forward_at(layer))
        states.append(kept)
        weights.append(whole)
    layer_output = x.astype(bf16).reshape(tokens.shape)
    grads = cotangent.astype(f32) * masked.astype(f32)[..., None]
    grads = grads.reshape(count * length, width)
    flows = {}
    plans = {
        "down": ["rims", "next attending", "next halfway", "next rims", "never"],
        "up": ["rims", "next attending", "next halfway", "next rims", "never"],
        "in": ["next attending", "next rims", "never"],
        "query": ["never"],
    }
    last_plans = {
        "down": ["halfway", "rims", "never"],
        "up": ["halfway", "rims", "never"],
    }
    waiting = []

    def due(layer, name):
        result = []
        for (kind, owner), flow in flows.items():
            plan = last_plans[kind] if owner == 0 and kind in last_plans else plans[kind]
            when = plan[min(flow.stage, len(plan) - 1)]
            if flow.done or flow in waiting:
                continue
            if when == ("next " if owner > layer else "") + name or owner > layer + 1:
                result.append(flow)
        return result

    def backward_at(layer):
        def at(name, value, given=None):
            landing, begin = due(layer, name), []
            if name == "attending":
                for kind, halves, last in zip(("down", "up"), given, "yx"):
                    flows[kind, layer] = Scatter(halves, path(last)[::-1])
                    begin.append(flows[kind, layer])
            if name == "pooled" and layer == 0:
                plan = [(0, 0, 1, 0), (2, 0, 3, 0)]
                flow = Scatter(weight_grads(given, plan, width), path("z")[::-1])
                flows["query", layer] = flow
            if name in ("rims", "pooled"):
                waiting.extend(flow for flow in landing if len(flow.order) - flow.stage > 2)
            return checkpoint(value, landing, [] if name == "pooled" else begin, waiting)

        return at

    small_sums = [None] * layers
    for layer in reversed(range(layers)):
        grads, given, small_sums[layer] = layer_backward(
            grads, states[layer], weights[layer], masks, select, count, backward_at(layer)
        )
        if layer > 0:
            plan = [(0, 0, 1 + i, 0) for i in range(3)] + [(4, 0, 5, 0)]
            flow = Scatter(weight_grads(given, plan, width), path("z")[::-1])
            flows["in", layer] = flow
            grads = checkpoint(grads, due(layer, "end"), [flow] + waiting)
            waiting.clear()
    halves = weight_grads((given[0], *given[2:4]), [(0, 0, 1, 0), (0, 0, 2, 0)], width)
    sides = small_grads(small_sums, width)
    joined = [jnp.concatenate(parts, axis=2) for parts in zip(halves, sides)]
    last = Scatter(joined, path("x")[::-1])
    flows["last", 0] = last
    ends = [last, flows["query", 0]]
    marker = checkpoint(last.keep[:1, :1, :1], [], ends)
    marker = checkpoint(marker, ends, waiting)
    while True:
        ends = [flow for flow in ends if not flow.done]
        others = [flow for flow in flows.values() if not flow.done and flow not in ends]
        if not ends + others:
            break
        if ends:
            marker = checkpoint(marker, ends)
        if others:
            marker = checkpoint(marker, others)
    totals = []
    for layer in range(layers):
        if layer > 0:
            whole = flows["in", layer].total[0]
            parts = [whole[:, i * width : (i + 1) * width] for i in range(4)]
        else:
            whole = flows["query", 0].total[0]
            end = last.total[0]
            parts = [whole[:, :width], end[:, :width], end[:, width : 2 * width], whole[:, width:]]
        parts.append(flows["up", layer].total[0])
        parts.append(flows["down", layer].total.reshape(ratio * shard_rows, width))
        totals.append(parts)
    up_totals, _ = tied([jnp.concatenate([parts[4] for parts in totals]), last.keep])
    up_totals = units_back(up_totals, ratio, shard_rows).reshape(layers, shard_rows, ratio * width)
    input_grad = grads.astype(bf16).reshape(tokens.shape)
    lines = last.total[0, :, 2 * width :].T
    per_layer = 8 + 2 * TAPS + ratio
    lines = lines[: layers * per_layer].reshape(layers, per_layer, shard_rows)
    vectors = [lines[:, i] for i in range(8)]
    after = 8 + 2 * TAPS
    grad_up_bias = lines[:, after:].reshape(layers, -1)
    return (
        layer_output, input_grad,
        *[jnp.stack([t[i] for t in totals]) if i != 4 else up_totals for i in range(6)],
        vectors[0], vectors[1], vectors[2], grad_up_bias, *vectors[3:],
        lines[:, 8 : 8 + TAPS], lines[:, 8 + TAPS : after],
    )


def solution(mesh):
    rows = P(None, "batch", "seq", None)
    matrix = P(None, ("seq", "batch"), None)
    vector = P(None, ("seq", "batch"))
    taps = P(None, None, ("seq", "batch"))
    params = (matrix,) * 6 + (vector,) * 9 + (taps,) * 2
    return jax.shard_map(
        on_device,
        mesh=mesh,
        in_specs=(rows, rows, P(None, "batch", "seq")) + params,
        out_specs=(rows, rows) + params,
        check_vma=False,
    )
```
